128 devices in a mesh: ctx: 64 (over y_hi, x, z, core), mp: 2 (over y_lo).
Axes of the slice: x: 4, y: 4 (y_hi: 2, y_lo: 2; y = y_hi * 2 + y_lo), z: 4, core: 2. Of those that a mesh axis runs over, the one named last changes fastest.
Arguments:
- tokens: bfloat16 [8192, 768], P('ctx'), may hold values from -6 to 6
- attn_gain: float32 [768], replicated, may hold values from 0.5 to 1.5
- w_query: bfloat16 [768, 768], P(None, 'mp'), may hold values from -0.0546875 to 0.0546875
- w_key: bfloat16 [768, 768], P(None, 'mp'), may hold values from -0.21875 to 0.21875
- w_value: bfloat16 [768, 768], P(None, 'mp'), may hold values from -0.21875 to 0.21875
- w_proj: bfloat16 [768, 768], P('mp'), may hold values from -2 to 2
- rel_table: float32 [32, 12], P(None, 'mp'), may hold values from -6 to 6
- rel_bucket: int32 [16383], replicated, may hold values from 0 to 31, as said below
- ffn_gain: float32 [768], replicated, may hold values from 0.5 to 1.5
- router: float32 [768, 64], replicated, may hold values from -0.15625 to 0.15625
- w_in: bfloat16 [64, 768, 3072], P('ctx', None, 'mp'), may hold values from -0.21875 to 0.21875
- w_out: bfloat16 [64, 3072, 768], P('ctx', 'mp'), may hold values from -10 to 10
- expert_route: int32 [8192], P('ctx'), may hold values from 0 to 63, as said below
- expert_slot: int32 [8192], P('ctx'), may hold values from 0 to 3, as said below
- cotangent: bfloat16 [8192, 768], P('ctx'), may hold values from -6 to 6
Outputs:
- mixed: bfloat16 [8192, 768], P('ctx')
- grad_input: float32 [8192, 768], P('ctx')
- grad_attn_gain: float32 [768], replicated
- grad_query: float32 [768, 768], P(None, 'mp')
- grad_key: float32 [768, 768], P(None, 'mp')
- grad_value: float32 [768, 768], P(None, 'mp')
- grad_proj: float32 [768, 768], P('mp')
- grad_table: float32 [32, 12], P(None, 'mp')
- grad_ffn_gain: float32 [768], replicated
- grad_router: float32 [768, 64], replicated
- grad_expert_in: float32 [64, 768, 3072], P('ctx', None, 'mp')
- grad_expert_out: float32 [64, 3072, 768], P('ctx', 'mp')
The draws below stay inside these ranges and needn't reach their ends.
Inputs may be any that keep to these rules, and one draw needn't show every extreme that they name: `rel_bucket`: entry 8191 + r is the bucket of the offset r = key position - query position: offsets of size under 8 have buckets 0 to 7, larger sizes share buckets 8 to 15 that never fall as the size grows, and positive offsets add 16. `expert_route`: of the 128 tokens of one device, at most 4 go to one expert, and one expert gets exactly 4 tokens from every device. `expert_slot`: tokens of one device with the same expert have distinct slots.
All inputs are finite; a program needn't handle non-finite values.
Results may differ from the reference program's by a relative error of at most 0.024.
Values may be sent and summed in bfloat16 or wider, within the bound.
A program may use at most 192 MiB of HBM per device.

```python
import jax
import jax.numpy as jnp
from jax import lax

D = 768
HEADS = 12
HEAD = 64
FF = 3072
BUCKETS = 32
TOK_DEV = 128
TOKENS = 8192
EXPERTS = 64
CAP = 4


def route_table(key):
    pop_key, star_key, score_key, order_key = jax.random.split(key, 4)
    total_slots = EXPERTS * CAP
    block_count = TOKENS // TOK_DEV
    star_expert = jax.random.randint(star_key, (), 0, EXPERTS)
    popularity = jax.random.randint(pop_key, (EXPERTS,), 0, 4)
    slot_ids = jnp.arange(total_slots, dtype=jnp.int32)
    owners = slot_ids // CAP
    raw_score = jax.random.randint(score_key, (block_count, total_slots), 0, 65536)
    priority = raw_score // (1 + 3 * popularity[owners])[None, :] + 1
    priority = jnp.where((owners == star_expert)[None, :], 0, priority)
    priority = priority * total_slots + slot_ids[None, :]
    chosen = jnp.argsort(priority, axis=1, stable=True)[:, :TOK_DEV].astype(jnp.int32)
    shuffle_keys = jax.random.split(order_key, block_count)

    def shuffle_one(one_key):
        return jax.random.permutation(one_key, TOK_DEV)
    shuffle = jax.vmap(shuffle_one)(shuffle_keys)
    picked = jnp.take_along_axis(chosen, shuffle, axis=1).reshape(TOKENS)
    return ((picked // CAP).astype(jnp.int32), (picked % CAP).astype(jnp.int32))


def draw_expert_route(key, part):
    return route_table(key)[0]


def draw_expert_slot(key, part):
    return route_table(key)[1]


def draw_rel_bucket(key, part):
    key = jax.random.fold_in(key, 7)
    lower_cut = jnp.array([9, 12, 17, 23, 33, 46, 65], jnp.int32)
    upper_cut = jnp.array([11, 16, 22, 32, 45, 64, 90], jnp.int32)
    thresholds = jax.random.randint(key, (7,), 0, 1 << 20) % (upper_cut - lower_cut + 1) + lower_cut
    offsets = jnp.arange(2 * TOKENS - 1, dtype=jnp.int32) - (TOKENS - 1)
    distance = jnp.abs(offsets)
    far_bucket = 8 + jnp.sum((distance[:, None] >= thresholds[None, :]).astype(jnp.int32), axis=1)
    near_bucket = jnp.where(distance < 8, distance, far_bucket)
    return (near_bucket + 16 * (offsets > 0).astype(jnp.int32)).astype(jnp.int32)


def block_levels(stream_key, shape, cuts, least, largest):
    factor_of, own = 1.0, jax.random.fold_in(stream_key, 6)
    for dim, parts in cuts:
        draws = jnp.exp(jax.random.uniform(jax.random.fold_in(own, dim), (parts,), jnp.float32, least / len(cuts), largest / len(cuts)))
        factor_of = factor_of * jnp.repeat(draws, shape[dim] // parts).reshape([-1 if axis == dim else 1 for axis in range(len(shape))])
    return factor_of


def normal_values(stream_key, shape, spread, most, shards=(), kind=jnp.bfloat16):
    loudness = block_levels(stream_key, shape, shards, -0.22, 0.18) if shards else 1.0
    values = jax.random.normal(stream_key, shape, jnp.float32) * spread * loudness
    return jnp.minimum(jnp.maximum(values, -most), most).astype(kind)


def setup_inputs(seed: int = 0) -> dict:
    streams_of = jax.random.split(jax.random.key(seed), 16)
    return {
        "tokens": normal_values(streams_of[0], (TOKENS, D), 1.0, 6.0, ((0, 64),)),
        "attn_gain": jnp.clip(1.0 + 0.1 * jax.random.normal(streams_of[1], (D,), jnp.float32), 0.5, 1.5),
        "w_query": normal_values(streams_of[2], (D, D), (D * HEAD // 4) ** -0.5, 0.0546875, ((1, 2),)),
        "w_key": normal_values(streams_of[3], (D, D), D ** -0.5, 0.21875, ((1, 2),)),
        "w_value": normal_values(streams_of[4], (D, D), D ** -0.5, 0.21875, ((1, 2),)),
        "w_proj": normal_values(streams_of[5], (D, D), ((TOKENS // 100) ** 0.5 * D ** -0.5), 2.0, ((0, 2),)),
        "rel_table": normal_values(streams_of[6], (BUCKETS, HEADS), 1.0, 6.0, ((1, 2),), jnp.float32),
        "rel_bucket": draw_rel_bucket(jax.random.fold_in(streams_of[15], 71), 0),
        "ffn_gain": jnp.clip(1.0 + 0.1 * jax.random.normal(streams_of[8], (D,), jnp.float32), 0.5, 1.5),
        "router": normal_values(streams_of[9], (D, EXPERTS), (2 * D) ** -0.5, 0.15625, (), jnp.float32),
        "w_in": normal_values(streams_of[10], (EXPERTS, D, FF), D ** -0.5, 0.21875, ((0, 64), (2, 2))),
        "w_out": normal_values(streams_of[11], (EXPERTS, FF, D), (1.5 * EXPERTS * FF ** -0.5), 10.0, ((0, 64), (1, 2))),
        "expert_route": draw_expert_route(jax.random.fold_in(streams_of[15], 71), 0),
        "expert_slot": draw_expert_slot(jax.random.fold_in(streams_of[15], 71), 0),
        "cotangent": normal_values(streams_of[14], (TOKENS, D), 1.0, 6.0, ((0, 64),)),
    }


EPSILON = 1e-06
PRECISE = lax.Precision.HIGHEST

@jax.custom_vjp
def low(v):
    return lax.optimization_barrier(v.astype(jnp.bfloat16)).astype(jnp.float32)

@jax.custom_vjp
def low_back(v):
    return v

def low_keep(v):
    return (low(v), None)

def low_pass(kept, grad):
    return (grad,)

def back_keep(v):
    return (v, None)

def back_low(kept, grad):
    return (low(grad),)
low.defvjp(low_keep, low_pass)
low_back.defvjp(back_keep, back_low)

def matmul_high(left, right):
    return jnp.dot(left, right, precision=PRECISE)

def rms_norm(values, gain):
    return values * lax.rsqrt(lax.optimization_barrier(jnp.mean(values * values, axis=-1, keepdims=True)) + EPSILON) * gain

def attend_rows(query_block, block_start, key_heads, value_heads, rel_table, rel_bucket):
    row_count = query_block.shape[0]
    query_pos = block_start + jnp.arange(row_count, dtype=jnp.int32)
    key_pos = jnp.arange(key_heads.shape[0], dtype=jnp.int32)
    bucket_ids = jnp.take(rel_bucket, key_pos[None, :] - query_pos[:, None] + (TOKENS - 1))
    bias_grid = jnp.transpose(jnp.take(rel_table, bucket_ids, axis=0), (2, 0, 1))
    raw_scores = jnp.einsum('qhd,khd->hqk', query_block, key_heads, precision=PRECISE)
    scores = low_back(raw_scores) + bias_grid
    attn_probs = low(jax.nn.softmax(scores, axis=-1))
    return jnp.einsum('hqk,khd->qhd', attn_probs, value_heads, precision=PRECISE)

def layer_forward(floats_in, attn_gain, w_query, w_key, w_value, w_proj, rel_table, ffn_gain, router, w_in, w_out, rel_bucket, expert_route, expert_slot):
    normed = low(rms_norm(floats_in, attn_gain))
    query_heads = low(low_back(matmul_high(normed, w_query))).reshape(TOKENS, HEADS, HEAD)
    key_heads = low(low_back(matmul_high(normed, w_key))).reshape(TOKENS, HEADS, HEAD)
    value_heads = low(low_back(matmul_high(normed, w_value))).reshape(TOKENS, HEADS, HEAD)
    row_block = min(TOKENS, 512)
    starts = jnp.arange(0, TOKENS, row_block, dtype=jnp.int32)

    def attend_pair(block_pair):
        return attend_rows(block_pair[0], block_pair[1], key_heads, value_heads, rel_table, rel_bucket)
    context = lax.map(jax.checkpoint(attend_pair), (query_heads.reshape(TOKENS // row_block, row_block, HEADS, HEAD), starts))
    context = low(low_back(context.reshape(TOKENS, D)))
    hidden1 = floats_in + low_back(matmul_high(context, w_proj))
    normed2 = rms_norm(hidden1, ffn_gain)
    logits = matmul_high(normed2, router)
    chosen = expert_route[:, None] == jnp.arange(EXPERTS, dtype=jnp.int32)[None, :]
    gate_prob = lax.optimization_barrier(jnp.sum(jnp.where(chosen, jax.nn.softmax(logits, axis=-1), 0.0), axis=1))
    sent_rows = low(low_back(normed2))
    per_expert = TOKENS // TOK_DEV * CAP
    slot_place = expert_route * per_expert + jnp.arange(TOKENS, dtype=jnp.int32) // TOK_DEV * CAP + expert_slot
    buffers = jnp.zeros((EXPERTS * per_expert, D), floats_in.dtype).at[slot_place].set(sent_rows)
    buffers = buffers.reshape(EXPERTS, per_expert, D)

    def expert(block_pair):
        buffer_rows, weights_in, weights_out = block_pair
        pre_act = low_back(matmul_high(buffer_rows, weights_in))
        return low(low_back(matmul_high(low(jax.nn.gelu(pre_act)), weights_out)))
    expert_rows = lax.map(jax.checkpoint(expert), (buffers, w_in, w_out)).reshape(EXPERTS * per_expert, D)
    return hidden1 + gate_prob[:, None] * expert_rows[slot_place]

def reference(tokens, attn_gain, w_query, w_key, w_value, w_proj, rel_table, rel_bucket, ffn_gain, router, w_in, w_out, expert_route, expert_slot, cotangent):
    floats = (tokens.astype(jnp.float32), attn_gain, w_query.astype(jnp.float32), w_key.astype(jnp.float32), w_value.astype(jnp.float32), w_proj.astype(jnp.float32), rel_table, ffn_gain, router, w_in.astype(jnp.float32), w_out.astype(jnp.float32))

    def forward(floats_in, gain_one, query_w, key_w, value_w, proj_w, table_w, gain_two, router_w, inner_w, outer_w):
        return layer_forward(floats_in, gain_one, query_w, key_w, value_w, proj_w, table_w, gain_two, router_w, inner_w, outer_w, rel_bucket, expert_route, expert_slot)
    mixed, pullback = jax.vjp(forward, *floats)
    grads = pullback(cotangent.astype(jnp.float32))
    return (mixed.astype(jnp.bfloat16), grads[0], grads[1], grads[2], grads[3], grads[4], grads[5], grads[6], grads[7], grads[8], grads[9], grads[10])
```

```python
import functools
import jax
import jax.numpy as jnp
from jax import lax
from jax.experimental import pallas as pl
from jax.experimental.pallas import tpu as pltpu
from jax.sharding import PartitionSpec as P

HEAD = 64
GROUP = 3
BLOCK = 128
PAIR = 2 * BLOCK
SPAN = 4
CHUNK = SPAN * PAIR
TILES = CHUNK // BLOCK
VMEM = pl.BlockSpec(memory_space=pltpu.VMEM)
SMEM = pl.BlockSpec(memory_space=pltpu.SMEM)
LARGE = pltpu.CompilerParams(vmem_limit_bytes=60 * 1024 * 1024)


def contract(left, right, left_dim, right_dim):
    return lax.dot_general(
        left,
        right,
        (((left_dim,), (right_dim,)), ((), ())),
        preferred_element_type=jnp.float32,
    )


def window_row(place, chunk, tile, half):
    return 63 - (SPAN * chunk + tile // 2) + place + BLOCK // 4 * (half - tile % 2)


def tile_consts(table_ref, head, place, chunk, tile):
    parts = []
    for half in range(2):
        row = window_row(place, chunk, tile, half)
        parts.append(jnp.broadcast_to(table_ref[head, pl.ds(row, 1), 0:1], (1, BLOCK)))
    return jnp.concatenate(parts, axis=1)


def chunk_mixed(uneven_ref, place, chunk):
    mixed = 0
    for tile in range(TILES):
        for half in range(2):
            mixed = mixed + uneven_ref[window_row(place, chunk, tile, half)]
    return mixed


def add_uneven(table_ref, uneven_ref, score_ref, place, chunk):
    for tile in range(TILES):
        for half in range(2):
            row = window_row(place, chunk, tile, half)

            @pl.when(uneven_ref[row] > 0)
            def _():
                for head in range(GROUP):
                    window = jnp.concatenate(
                        [table_ref[head, pl.ds(row, 1), :], table_ref[head, pl.ds(row + 1, 1), :]],
                        axis=1,
                    )
                    window = window - window[:, 0:1]
                    grid = pltpu.roll(
                        jnp.broadcast_to(window, (BLOCK, PAIR)),
                        BLOCK,
                        1,
                        stride=1,
                        stride_axis=0,
                    )[:, :BLOCK]
                    rows = slice(tile * BLOCK, (tile + 1) * BLOCK)
                    cols = slice(half * BLOCK, (half + 1) * BLOCK)
                    score_ref[head, rows, cols] += grid


def forward_kernel(
    place_ref, uneven_ref, table_ref, keys_ref, query_ref, out_ref, lse_ref,
    best_ref, sum_ref, total_ref, score_ref,
):
    place = place_ref[0]
    best_ref[...] = jnp.full_like(best_ref, -1e30)
    sum_ref[...] = jnp.zeros_like(sum_ref)
    total_ref[...] = jnp.zeros_like(total_ref)

    def rest(chunk, head, held, scores):
        consts = [tile_consts(table_ref, head, place, chunk, tile) for tile in range(TILES)]
        old = best_ref[head]
        new = old
        for tile in range(TILES):
            part = scores[tile * BLOCK : (tile + 1) * BLOCK]
            new = jnp.maximum(new, jnp.max(part, axis=0, keepdims=True) + consts[tile])
        decay = jnp.exp(old - new)
        weights = [
            jnp.exp(scores[tile * BLOCK : (tile + 1) * BLOCK] - (new - consts[tile]))
            for tile in range(TILES)
        ]
        weights = jnp.concatenate(weights, axis=0)
        sum_ref[head] = sum_ref[head] * decay + jnp.sum(weights, axis=0, keepdims=True)
        best_ref[head] = new
        total_ref[head] = total_ref[head] * decay + contract(
            held, weights.astype(jnp.bfloat16), 0, 0
        )

    @pl.loop(0, keys_ref.shape[0] // SPAN)
    def _(chunk):
        def held_of(head):
            return keys_ref[pl.ds(chunk * SPAN, SPAN), head].reshape(CHUNK, 2 * HEAD)

        mixed = chunk_mixed(uneven_ref, place, chunk)

        @pl.when(mixed == 0)
        def _():
            for head in range(GROUP):
                held = held_of(head)
                rest(chunk, head, held, contract(held, query_ref[head], 1, 0))

        @pl.when(mixed > 0)
        def _():
            for head in range(GROUP):
                score_ref[head] = contract(held_of(head), query_ref[head], 1, 0)
            add_uneven(table_ref, uneven_ref, score_ref, place, chunk)
            for head in range(GROUP):
                rest(chunk, head, held_of(head), score_ref[head])

    for head in range(GROUP):
        out_ref[head] = total_ref[head][HEAD:] / sum_ref[head]
        lse_ref[head] = best_ref[head] + jnp.log(sum_ref[head])


def backward_kernel(
    place_ref, uneven_ref, table_ref, keys_ref, query_t_ref, grad_t_ref, query_ref, grad_ref,
    lse_ref, delta_ref, grad_keys_ref, grad_query_ref, offsets_ref, score_ref,
):
    place = place_ref[0]
    grad_query_ref[...] = jnp.zeros_like(grad_query_ref)
    offsets_ref[...] = jnp.zeros_like(offsets_ref)

    def rest(chunk, head, held, scores):
        grads = contract(held, grad_t_ref[head], 1, 0)
        probs = jnp.concatenate(
            [
                jnp.exp(
                    scores[tile * BLOCK : (tile + 1) * BLOCK]
                    - (lse_ref[head] - tile_consts(table_ref, head, place, chunk, tile))
                )
                for tile in range(TILES)
            ],
            axis=0,
        )
        slopes = probs * (grads - delta_ref[head])
        rounded = slopes.astype(jnp.bfloat16)
        part = contract(rounded, query_ref[head], 1, 0) + contract(
            probs.astype(jnp.bfloat16), grad_ref[head], 1, 0
        )
        grad_keys_ref[pl.ds(chunk * SPAN, SPAN), head] = part.astype(grad_keys_ref.dtype).reshape(
            SPAN, PAIR, 2 * HEAD
        )
        grad_query_ref[head] += contract(held, rounded, 0, 0)
        return slopes

    def put_even(chunk, head, tile, half, slopes):
        row = window_row(place, chunk, tile, half)
        offsets_ref[head, pl.ds(row, 1), :] += jnp.sum(slopes, axis=0, keepdims=True)

    def put_uneven(chunk, head, tile, half, slopes):
        row = window_row(place, chunk, tile, half)
        wide = jnp.concatenate([slopes, jnp.zeros_like(slopes)], axis=1)
        folded = jnp.zeros((8, PAIR), jnp.float32)
        for group in range(BLOCK // 8):
            folded = folded + pltpu.roll(
                wide[group * 8 : (group + 1) * 8], (BLOCK - 8 * group) % PAIR, 1
            )
        line = jnp.zeros((1, PAIR), jnp.float32)
        for step in range(8):
            line = line + pltpu.roll(folded, (PAIR - step) % PAIR, 1)[step : step + 1]
        offsets_ref[head, pl.ds(row, 1), :] += line[:, :BLOCK]
        offsets_ref[head, pl.ds(row + 1, 1), :] += line[:, BLOCK:]

    @pl.loop(0, keys_ref.shape[0] // SPAN)
    def _(chunk):
        def held_of(head):
            return keys_ref[pl.ds(chunk * SPAN, SPAN), head].reshape(CHUNK, 2 * HEAD)

        mixed = chunk_mixed(uneven_ref, place, chunk)

        @pl.when(mixed == 0)
        def _():
            for head in range(GROUP):
                held = held_of(head)
                slopes = rest(chunk, head, held, contract(held, query_t_ref[head], 1, 0))
                for tile in range(TILES):
                    for half in range(2):
                        part = slopes[
                            tile * BLOCK : (tile + 1) * BLOCK, half * BLOCK : (half + 1) * BLOCK
                        ]
                        put_even(chunk, head, tile, half, part)

        @pl.when(mixed > 0)
        def _():
            for head in range(GROUP):
                score_ref[head] = contract(held_of(head), query_t_ref[head], 1, 0)
            add_uneven(table_ref, uneven_ref, score_ref, place, chunk)
            for head in range(GROUP):
                score_ref[head] = rest(chunk, head, held_of(head), score_ref[head])
            for tile in range(TILES):
                for half in range(2):
                    rows = slice(tile * BLOCK, (tile + 1) * BLOCK)
                    cols = slice(half * BLOCK, (half + 1) * BLOCK)
                    uneven = uneven_ref[window_row(place, chunk, tile, half)]

                    @pl.when(uneven == 0)
                    def _():
                        for head in range(GROUP):
                            put_even(chunk, head, tile, half, score_ref[head, rows, cols])

                    @pl.when(uneven > 0)
                    def _():
                        for head in range(GROUP):
                            put_uneven(chunk, head, tile, half, score_ref[head, rows, cols])


def attend(place, uneven, table, keys, query_t):
    shape = jax.ShapeDtypeStruct
    return pl.pallas_call(
        forward_kernel,
        out_shape=(
            shape((GROUP, HEAD, PAIR), jnp.float32),
            shape((GROUP, 1, PAIR), jnp.float32),
        ),
        in_specs=[SMEM, SMEM, VMEM, VMEM, VMEM],
        out_specs=(VMEM, VMEM),
        scratch_shapes=[
            pltpu.VMEM((GROUP, 1, PAIR), jnp.float32),
            pltpu.VMEM((GROUP, 1, PAIR), jnp.float32),
            pltpu.VMEM((GROUP, 2 * HEAD, PAIR), jnp.float32),
            pltpu.VMEM((GROUP, CHUNK, PAIR), jnp.float32),
        ],
        compiler_params=LARGE,
        name="attend",
    )(place, uneven, table, keys, query_t)


def attend_back(place, uneven, table, keys, query_t, grad_t, query, grad, lse, delta):
    shape = jax.ShapeDtypeStruct
    return pl.pallas_call(
        backward_kernel,
        out_shape=(
            shape(keys.shape, jnp.bfloat16),
            shape((GROUP, 2 * HEAD, PAIR), jnp.float32),
            shape((GROUP, BLOCK, BLOCK), jnp.float32),
        ),
        in_specs=[SMEM, SMEM] + [VMEM] * 8,
        out_specs=(VMEM, VMEM, VMEM),
        scratch_shapes=[pltpu.VMEM((GROUP, CHUNK, PAIR), jnp.float32)],
        compiler_params=LARGE,
        name="attend_back",
    )(place, uneven, table, keys, query_t, grad_t, query, grad, lse, delta)


def offset_tables(rel_bucket, rel_table):
    flipped = jnp.flip(jnp.pad(rel_bucket, (0, 1), mode="edge")).reshape(BLOCK, BLOCK)
    buckets = rel_table.shape[0]
    hit = flipped[None, None] == jnp.arange(buckets, dtype=jnp.int32)[None, :, None, None]
    table = jnp.sum(jnp.where(hit, rel_table.T[:, :, None, None], 0.0), axis=1)
    low = jnp.min(flipped, axis=1)
    high = jnp.max(flipped, axis=1)
    following = jnp.minimum(jnp.arange(BLOCK) + 1, BLOCK - 1)
    uneven = jnp.maximum(high, high[following]) != jnp.minimum(low, low[following])
    return flipped, table, uneven.astype(jnp.int32)


def table_grad(flipped, offsets, buckets):
    hit = flipped[None, None] == jnp.arange(buckets, dtype=jnp.int32)[:, None, None, None]
    return jnp.sum(jnp.where(hit, offsets[None], 0.0), axis=(2, 3))

ANYWHERE = pl.BlockSpec(memory_space=pl.ANY)
SIDE = 4


class Place:
    def __init__(self):
        self.me = lax.axis_index("ctx")
        self.core = lax.rem(self.me, 2)
        self.z = lax.rem(self.me // 2, SIDE)
        self.x = lax.rem(self.me // (2 * SIDE), SIDE)
        self.y = self.me // (2 * SIDE * SIDE)

    def at(self, dx=0, dz=0, dcore=0, dy=0):
        x = lax.rem(self.x + dx, SIDE)
        z = lax.rem(self.z + dz, SIDE)
        core = lax.rem(self.core + dcore, 2)
        y = lax.rem(self.y + dy, 2)
        return ((y * SIDE + x) * SIDE + z) * 2 + core

    def turned(self, axis, step):
        return self.at(dx=step) if axis == 0 else self.at(dz=step)

    def along(self, axis, step):
        return lax.rem((self.x if axis == 0 else self.z) + step, SIDE)


def meet(targets):
    barrier = pltpu.get_barrier_semaphore()
    for target in targets:
        pl.semaphore_signal(
            barrier, inc=1, device_id={"ctx": target}, device_id_type=pl.DeviceIdType.MESH
        )
    pl.semaphore_wait(barrier, len(targets))


def ring_targets(place):
    found = [place.at(dcore=1)]
    for step in range(1, SIDE):
        found += [place.at(dx=step), place.at(dz=step)]
    return found


def sender(target, src, dst, send_sem, recv_sem):
    return pltpu.make_async_remote_copy(
        src_ref=src,
        dst_ref=dst,
        send_sem=send_sem,
        recv_sem=recv_sem,
        device_id={"ctx": target},
        device_id_type=pl.DeviceIdType.MESH,
    )


def gather_kernel(block_ref, out_ref, local_sem, ring_send, ring_recv, twin_send, twin_recv):
    place = Place()
    meet(ring_targets(place))
    half_rows = block_ref.shape[1] // 2
    started = []

    def view(x, z, core, half):
        slot = (x * SIDE + z) * 2 + core
        return out_ref.at[slot, :, pl.ds(half * half_rows, half_rows)]

    def origin(half, first, second):
        x, z = (second, first) if half == 0 else (first, second)
        return place.along(0, x), place.along(1, z)

    def pass_on(half, first, second, axis, step, src):
        x, z = origin(half, first, second)
        copy = sender(
            place.turned(axis, step),
            src,
            view(x, z, place.core, half),
            ring_send.at[len(started)],
            ring_recv.at[half, x * SIDE + z],
        )
        copy.start()
        started.append(copy)

    def to_twin(half, first, second, src):
        x, z = origin(half, first, second)
        copy = sender(
            place.at(dcore=1),
            src,
            view(x, z, place.core, half),
            twin_send.at[half, first, second],
            twin_recv.at[half, x * SIDE + z],
        )
        copy.start()
        twins.append(copy)

    def arrived(half, first, second, core, sems):
        x, z = origin(half, first, second)
        spot = view(x, z, core, half)
        sender(place.me, spot, spot, sems.at[half, x * SIDE + z], sems.at[half, x * SIDE + z]).wait_recv()
        return spot

    twins = []
    own = pltpu.make_async_copy(
        block_ref, out_ref.at[(place.x * SIDE + place.z) * 2 + place.core], local_sem
    )
    own.start()
    pieces = [block_ref.at[:, pl.ds(half * half_rows, half_rows)] for half in range(2)]
    for step in range(1, SIDE):
        for half in range(2):
            pass_on(half, 0, 0, 1 - half, step, pieces[half])
    for step in range(1, SIDE):
        for half in range(2):
            pass_on(half, 0, 0, half, step, pieces[half])
    for half in range(2):
        to_twin(half, 0, 0, pieces[half])
    for back in range(1, SIDE):
        for half in range(2):
            spot = arrived(half, SIDE - back, 0, place.core, ring_recv)
            for step in range(1, SIDE):
                pass_on(half, SIDE - back, 0, half, step, spot)
            to_twin(half, SIDE - back, 0, spot)
    for first in (0, 3, 2, 1):
        for back in range(1, SIDE):
            for half in range(2):
                spot = arrived(half, first, SIDE - back, place.core, ring_recv)
                to_twin(half, first, SIDE - back, spot)
    for first in range(SIDE):
        for second in range(SIDE):
            for half in range(2):
                arrived(half, first, second, 1 - place.core, twin_recv)
    own.wait()
    for copy in started + twins:
        copy.wait_send()


def gather_plane(block):
    shape = (2 * SIDE * SIDE,) + block.shape
    return pl.pallas_call(
        gather_kernel,
        out_shape=jax.ShapeDtypeStruct(shape, block.dtype),
        in_specs=[ANYWHERE],
        out_specs=ANYWHERE,
        scratch_shapes=[
            pltpu.SemaphoreType.DMA,
            pltpu.SemaphoreType.DMA((30,)),
            pltpu.SemaphoreType.DMA((2, SIDE * SIDE)),
            pltpu.SemaphoreType.DMA((2, SIDE, SIDE)),
            pltpu.SemaphoreType.DMA((2, SIDE * SIDE)),
        ],
        compiler_params=pltpu.CompilerParams(
            collective_id=1, has_side_effects=True, vmem_limit_bytes=32 * 1024 * 1024
        ),
        name="gather_plane",
    )(block)


def wide(value):
    return value.astype(jnp.float32)


def scatter_kernel(
    parts_ref, out_ref, mine, twin, sums, ring_one, halves, ring_two,
    local_sem, twin_send, twin_recv, one_send, one_recv, two_send, two_recv,
):
    place = Place()
    half_rows = parts_ref.shape[4] // 2

    def source(half, group, core):
        rows = pl.ds(half * half_rows, half_rows)
        if half == 0:
            return parts_ref.at[group, :, core, :, rows]
        return parts_ref.at[:, group, core, :, rows]

    loads, twins, ones, twos = {}, {}, {}, {}
    for step in (1, 2, 3, 0):
        for half in range(2):
            group = place.along(half, step)
            loads[half, step] = pltpu.make_async_copy(
                source(half, group, place.core), mine.at[half, step], local_sem.at[half, step]
            )
            loads[half, step].start()
    meet(ring_targets(place))
    for step in (1, 2, 3, 0):
        for half in range(2):
            group = place.along(half, step)
            twins[half, step] = sender(
                place.at(dcore=1),
                source(half, group, 1 - place.core),
                twin.at[half, step],
                twin_send.at[half, step],
                twin_recv.at[half, step],
            )
            twins[half, step].start()
    for step in (1, 2, 3, 0):
        for half in range(2):
            loads[half, step].wait()
            twins[half, step].wait_recv()
            sums[half, step] = (wide(mine[half, step]) + wide(twin[half, step])).astype(sums.dtype)
            if step:
                ones[half, step] = sender(
                    place.turned(half, step),
                    sums.at[half, step],
                    ring_one.at[half, step - 1],
                    one_send.at[half, step - 1],
                    one_recv.at[half, step - 1],
                )
                ones[half, step].start()
    for half in range(2):
        for step in range(1, SIDE):
            ones[half, step].wait_recv()
        for shift in (1, 2, 3, 0):
            spot = place.along(1 - half, shift)
            total = wide(sums[half, 0, spot])
            for step in range(1, SIDE):
                total = total + wide(ring_one[half, step - 1, spot])
            halves[half, shift] = total.astype(halves.dtype)
            if shift:
                twos[half, shift] = sender(
                    place.turned(1 - half, shift),
                    halves.at[half, shift],
                    ring_two.at[half, shift - 1],
                    two_send.at[half, shift - 1],
                    two_recv.at[half, shift - 1],
                )
                twos[half, shift].start()
    for half in range(2):
        total = wide(halves[half, 0])
        for shift in range(1, SIDE):
            twos[half, shift].wait_recv()
            total = total + wide(ring_two[half, shift - 1])
        out_ref[:, half * half_rows : (half + 1) * half_rows] = total.astype(out_ref.dtype)
    for copy in list(twins.values()) + list(ones.values()) + list(twos.values()):
        copy.wait_send()


def scatter_plane(parts):
    heads, rows, lanes = parts.shape[1:]
    piece = (heads, rows // 2, lanes)
    kind = parts.dtype
    sem = pltpu.SemaphoreType.DMA
    return pl.pallas_call(
        scatter_kernel,
        out_shape=jax.ShapeDtypeStruct((heads, rows, lanes), kind),
        in_specs=[ANYWHERE],
        out_specs=pl.BlockSpec(memory_space=pltpu.VMEM),
        scratch_shapes=[
            pltpu.VMEM((2, SIDE, SIDE) + piece, kind),
            pltpu.VMEM((2, SIDE, SIDE) + piece, kind),
            pltpu.VMEM((2, SIDE, SIDE) + piece, kind),
            pltpu.VMEM((2, SIDE - 1, SIDE) + piece, kind),
            pltpu.VMEM((2, SIDE) + piece, kind),
            pltpu.VMEM((2, SIDE - 1) + piece, kind),
            sem((2, SIDE)), sem((2, SIDE)), sem((2, SIDE)),
            sem((2, SIDE - 1)), sem((2, SIDE - 1)), sem((2, SIDE - 1)), sem((2, SIDE - 1)),
        ],
        compiler_params=pltpu.CompilerParams(
            collective_id=2, has_side_effects=True, vmem_limit_bytes=32 * 1024 * 1024
        ),
        name="scatter_plane",
    )(parts.reshape((SIDE, SIDE, 2) + parts.shape[1:]))


def total_kernel(
    parts_ref, out_ref, twin, sums, ring_one, halves, ring_two, pairs, other,
    twin_send, twin_recv, one_send, one_recv, two_send, two_recv, far_send, far_recv,
    far_back_send, far_back_recv, two_back_send, two_back_recv, one_back_send, one_back_recv,
    twin_back_send, twin_back_recv,
):
    place = Place()
    meet(ring_targets(place) + [place.at(dy=1)])
    sent = []

    def go(target, src, dst, send_sem, recv_sem):
        copy = sender(target, src, dst, send_sem, recv_sem)
        copy.start()
        sent.append(copy)
        return copy

    twins, ones, twos, fars = {}, {}, {}, {}
    for step in (1, 2, 3, 0):
        for half in range(2):
            twins[half, step] = go(
                place.at(dcore=1),
                parts_ref.at[half, 1 - place.core, place.along(half, step)],
                twin.at[half, step],
                twin_send.at[half, step],
                twin_recv.at[half, step],
            )
    for step in (1, 2, 3, 0):
        for half in range(2):
            twins[half, step].wait_recv()
            own = parts_ref[half, place.core, place.along(half, step)]
            sums[half, step] = (wide(own) + wide(twin[half, step])).astype(sums.dtype)
            if step:
                ones[half, step] = go(
                    place.turned(half, step),
                    sums.at[half, step],
                    ring_one.at[half, step - 1],
                    one_send.at[half, step - 1],
                    one_recv.at[half, step - 1],
                )
    for half in range(2):
        for step in range(1, SIDE):
            ones[half, step].wait_recv()
        for shift in (1, 2, 3, 0):
            spot = place.along(1 - half, shift)
            total = wide(sums[half, 0, spot])
            for step in range(1, SIDE):
                total = total + wide(ring_one[half, step - 1, spot])
            halves[half, shift] = total.astype(halves.dtype)
            if shift:
                twos[half, shift] = go(
                    place.turned(1 - half, shift),
                    halves.at[half, shift],
                    ring_two.at[half, shift - 1],
                    two_send.at[half, shift - 1],
                    two_recv.at[half, shift - 1],
                )
    for half in range(2):
        for shift in range(1, SIDE):
            twos[half, shift].wait_recv()
        total = wide(halves[half, 0])
        for shift in range(1, SIDE):
            total = total + wide(ring_two[half, shift - 1])
        pairs[half] = total.astype(pairs.dtype)
        fars[half] = go(
            place.at(dy=1),
            pairs.at[half, 1 - place.y],
            other.at[half],
            far_send.at[half],
            far_recv.at[half],
        )

    def spot(half, core, first, second):
        return out_ref.at[half, core, place.along(half, first), place.along(1 - half, second)]

    def landed(view, sem):
        sender(place.me, view, view, sem, sem).wait_recv()

    for half in range(2):
        fars[half].wait_recv()
        total = wide(pairs[half, place.y]) + wide(other[half])
        out_ref[
            half, place.core, place.along(half, 0), place.along(1 - half, 0), place.y
        ] = total.astype(out_ref.dtype)
        view = spot(half, place.core, 0, 0).at[place.y]
        go(place.at(dy=1), view, view, far_back_send.at[half], far_back_recv.at[half])
    for half in range(2):
        landed(spot(half, place.core, 0, 0).at[1 - place.y], far_back_recv.at[half])
        view = spot(half, place.core, 0, 0)
        for step in range(1, SIDE):
            go(
                place.turned(1 - half, step),
                view,
                view,
                two_back_send.at[half, step - 1],
                two_back_recv.at[half, step - 1],
            )
    for half in range(2):
        for step in range(1, SIDE):
            landed(spot(half, place.core, 0, SIDE - step), two_back_recv.at[half, step - 1])
        view = out_ref.at[half, place.core, place.along(half, 0)]
        for step in range(1, SIDE):
            go(
                place.turned(half, step),
                view,
                view,
                one_back_send.at[half, step - 1],
                one_back_recv.at[half, step - 1],
            )
        go(
            place.at(dcore=1), view, view, twin_back_send.at[half, 0], twin_back_recv.at[half, 0]
        )
    for step in range(1, SIDE):
        for half in range(2):
            view = out_ref.at[half, place.core, place.along(half, SIDE - step)]
            landed(view, one_back_recv.at[half, step - 1])
            go(
                place.at(dcore=1),
                view,
                view,
                twin_back_send.at[half, step],
                twin_back_recv.at[half, step],
            )
    for step in range(SIDE):
        for half in range(2):
            view = out_ref.at[half, 1 - place.core, place.along(half, (SIDE - step) % SIDE)]
            landed(view, twin_back_recv.at[half, step])
    for copy in sent:
        copy.wait_send()


def total_all(rows):
    count, lanes = rows.shape
    piece = (2, count // 128, lanes)
    kind = rows.dtype
    sem = pltpu.SemaphoreType.DMA
    shape = (2, 2, SIDE, SIDE) + piece
    out = pl.pallas_call(
        total_kernel,
        out_shape=jax.ShapeDtypeStruct(shape, kind),
        in_specs=[pl.BlockSpec(memory_space=pltpu.VMEM)],
        out_specs=pl.BlockSpec(memory_space=pltpu.VMEM),
        scratch_shapes=[
            pltpu.VMEM((2, SIDE, SIDE) + piece, kind),
            pltpu.VMEM((2, SIDE, SIDE) + piece, kind),
            pltpu.VMEM((2, SIDE - 1, SIDE) + piece, kind),
            pltpu.VMEM((2, SIDE) + piece, kind),
            pltpu.VMEM((2, SIDE - 1) + piece, kind),
            pltpu.VMEM((2,) + piece, kind),
            pltpu.VMEM((2,) + piece[1:], kind),
            sem((2, SIDE)), sem((2, SIDE)),
            sem((2, SIDE - 1)), sem((2, SIDE - 1)), sem((2, SIDE - 1)), sem((2, SIDE - 1)),
            sem((2,)), sem((2,)), sem((2,)), sem((2,)),
            sem((2, SIDE - 1)), sem((2, SIDE - 1)), sem((2, SIDE - 1)), sem((2, SIDE - 1)),
            sem((2, SIDE)), sem((2, SIDE)),
        ],
        compiler_params=pltpu.CompilerParams(
            collective_id=3, has_side_effects=True, vmem_limit_bytes=32 * 1024 * 1024
        ),
        name="total_all",
    )(rows.reshape(shape))
    return out.reshape(count, lanes)


EPSILON = 1e-06
PRECISE = lax.Precision.HIGHEST


def rms_scale(values):
    return lax.rsqrt(jnp.mean(values * values, axis=1, keepdims=True) + EPSILON)


def product(left, right, left_dim=1, right_dim=0):
    return contract(left, right, left_dim, right_dim)


def swap(values, axis):
    count = lax.axis_size(axis)
    pairs = [(index, (index + count // 2) % count) for index in range(count)]
    return lax.ppermute(values, axis, pairs)


def add_halves(partial):
    rounded = partial.astype(jnp.bfloat16)
    other = swap(rounded, "mp")
    return rounded.astype(jnp.float32) + other.astype(jnp.float32)


def split_columns(values, first, width):
    kept = jnp.where(first, values[:, :width], values[:, width:])
    given = jnp.where(first, values[:, width:], values[:, :width])
    return kept, given


def stack_rows(kept, received, first):
    return jnp.concatenate(
        [jnp.where(first, kept, received), jnp.where(first, received, kept)], axis=0
    )


def per_head(values):
    return jnp.transpose(values.reshape(values.shape[0], GROUP, HEAD), (1, 0, 2))


def shards(
    tokens,
    attn_gain,
    w_query,
    w_key,
    w_value,
    w_proj,
    rel_table,
    rel_bucket,
    ffn_gain,
    router,
    w_in,
    w_out,
    expert_route,
    expert_slot,
    cotangent,
):
    tok_rows = tokens.shape[0]
    model_width = tokens.shape[1]
    width = GROUP * HEAD
    half_bf = jnp.bfloat16
    me = lax.axis_index("ctx")
    first = me < 32
    place = jnp.full((1,), me % 32, jnp.int32)

    floats_in = tokens.astype(jnp.float32)
    scale1 = rms_scale(floats_in)
    normed = (floats_in * scale1 * attn_gain).astype(half_bf)
    pieces = [
        split_columns(product(normed, weight).astype(half_bf), first, width)
        for weight in (w_query, w_key, w_value)
    ]
    kept = jnp.concatenate([piece[0] for piece in pieces], axis=1)
    received = swap(jnp.concatenate([piece[1] for piece in pieces], axis=1), "ctx")
    both = stack_rows(kept, received, first)
    query, key, value = (per_head(both[:, n * width : (n + 1) * width]) for n in range(3))
    held = gather_plane(jnp.concatenate([key, value], axis=2))
    query = jnp.pad(query, ((0, 0), (0, 0), (0, HEAD)))
    query_t = jnp.swapaxes(query, 1, 2)

    own_table = jnp.where(first, rel_table[:, :GROUP], rel_table[:, GROUP:])
    flipped, table, uneven = offset_tables(rel_bucket, own_table)
    context_t, lse = attend(place, uneven, table, held, query_t)

    both = jnp.transpose(context_t, (2, 0, 1)).astype(half_bf).reshape(2 * tok_rows, width)
    kept = jnp.where(first, both[:tok_rows], both[tok_rows:])
    received = swap(jnp.where(first, both[tok_rows:], both[:tok_rows]), "ctx")
    context = jnp.concatenate(
        [jnp.where(first, kept, received), jnp.where(first, received, kept)], axis=1
    )
    hidden1 = floats_in + add_halves(product(context, w_proj))
    scale2 = rms_scale(hidden1)
    normed2 = hidden1 * scale2 * ffn_gain
    logits = jnp.dot(normed2, router, precision=PRECISE)
    experts = router.shape[1]
    capacity = 2 * tok_rows // experts
    probs_route = jax.nn.softmax(logits, axis=1)
    chosen = (expert_route[:, None] == jnp.arange(experts, dtype=jnp.int32)[None, :]).astype(
        jnp.float32
    )
    gate_prob = jnp.sum(probs_route * chosen, axis=1)
    slot_place = expert_route * capacity + expert_slot
    dispatch = (
        jnp.arange(experts * capacity, dtype=jnp.int32)[:, None] == slot_place[None, :]
    ).astype(half_bf)
    grad_y = cotangent.astype(jnp.float32)
    grad_rows = (gate_prob[:, None] * grad_y).astype(half_bf)
    send = product(
        dispatch, jnp.concatenate([normed2.astype(half_bf), grad_rows], axis=1)
    ).astype(half_bf)
    send = send.reshape(experts, capacity, 2 * model_width)
    received = lax.all_to_all(send, "ctx", split_axis=0, concat_axis=0, tiled=True)
    received = received.reshape(experts * capacity, 2 * model_width)
    rows_in = received[:, :model_width]
    rows_grad = received[:, model_width:]
    weights_in = w_in[0]
    weights_out = w_out[0]
    pre_act = product(rows_in, weights_in)
    activ_f, gelu_back = jax.vjp(jax.nn.gelu, pre_act)
    activ = activ_f.astype(half_bf)
    partial_out = product(activ, weights_out)
    grad_expert_out = product(activ, rows_grad, 0, 0)
    grad_activ = product(rows_grad, weights_out, 1, 1)
    grad_pre = gelu_back(grad_activ)[0].astype(half_bf)
    grad_expert_in = product(rows_in, grad_pre, 0, 0)
    partial_in = product(grad_pre, weights_in, 1, 1)
    whole = add_halves(jnp.concatenate([partial_out, partial_in], axis=1)).astype(half_bf)
    whole = whole.reshape(experts, capacity, 2 * model_width)
    returned = lax.all_to_all(whole, "ctx", split_axis=0, concat_axis=0, tiled=True)
    combined = product(dispatch, returned.reshape(experts * capacity, 2 * model_width), 0, 0)
    expert_rows = combined[:, :model_width]
    grad_dispatch = combined[:, model_width:]

    mixed = (hidden1 + gate_prob[:, None] * expert_rows).astype(half_bf)
    grad_gate = jnp.sum(grad_y * expert_rows, axis=1)
    grad_logits = (grad_gate * gate_prob)[:, None] * (chosen - probs_route)
    grad_router = jnp.dot(normed2.T, grad_logits, precision=PRECISE)
    grad_normed2 = grad_dispatch + jnp.dot(grad_logits, router.T, precision=PRECISE)
    scaled2 = ffn_gain * grad_normed2
    grad_ffn_gain = jnp.sum(grad_normed2 * hidden1 * scale2, axis=0)
    grad_hidden1 = (
        grad_y
        + scale2 * scaled2
        - hidden1 * scale2**3 * jnp.mean(scaled2 * hidden1, axis=1, keepdims=True)
    )
    grad_attended = grad_hidden1.astype(half_bf)
    grad_proj = product(context, grad_attended, 0, 0)
    kept, given = split_columns(
        product(grad_attended, w_proj, 1, 1).astype(half_bf), first, width
    )
    grad_context = per_head(stack_rows(kept, swap(given, "ctx"), first))
    grad_context_t = jnp.swapaxes(grad_context, 1, 2)
    delta = jnp.sum(grad_context_t.astype(jnp.float32) * context_t, axis=1, keepdims=True)
    grad_parts, grad_query_t, offsets = attend_back(
        place,
        uneven,
        table,
        held,
        query_t,
        jnp.pad(grad_context_t, ((0, 0), (HEAD, 0), (0, 0))),
        query,
        jnp.pad(grad_context, ((0, 0), (0, 0), (HEAD, 0))),
        lse,
        delta,
    )
    grad_held = scatter_plane(grad_parts)
    grad_both = jnp.concatenate(
        [
            jnp.transpose(grad_query_t[:, :HEAD], (2, 0, 1)).astype(half_bf),
            jnp.transpose(grad_held, (1, 0, 2))[:, :, :HEAD],
            jnp.transpose(grad_held, (1, 0, 2))[:, :, HEAD:],
        ],
        axis=1,
    ).reshape(2 * tok_rows, 3 * width)
    kept = jnp.where(first, grad_both[:tok_rows], grad_both[tok_rows:])
    received = swap(jnp.where(first, grad_both[tok_rows:], grad_both[:tok_rows]), "ctx")
    low = jnp.where(first, kept, received)
    high = jnp.where(first, received, kept)
    grad_q, grad_k, grad_v = (
        jnp.concatenate(
            [low[:, n * width : (n + 1) * width], high[:, n * width : (n + 1) * width]], axis=1
        )
        for n in range(3)
    )
    grad_weights = [product(normed, grad, 0, 0) for grad in (grad_q, grad_k, grad_v)]
    grad_normed = add_halves(
        product(grad_q, w_query, 1, 1)
        + product(grad_k, w_key, 1, 1)
        + product(grad_v, w_value, 1, 1)
    )
    scaled1 = attn_gain * grad_normed
    grad_attn_gain = jnp.sum(grad_normed * floats_in * scale1, axis=0)
    grad_input = (
        grad_hidden1
        + scale1 * scaled1
        - floats_in * scale1**3 * jnp.mean(scaled1 * floats_in, axis=1, keepdims=True)
    )

    own_tab = table_grad(flipped, offsets, rel_table.shape[0])
    none = jnp.zeros_like(own_tab)
    grad_tab = jnp.concatenate(
        [jnp.where(first, own_tab, none), jnp.where(first, none, own_tab)], axis=1
    )
    buckets, heads = grad_tab.shape
    lanes = 128
    slabs = []
    for grad in grad_weights + [grad_proj]:
        slabs += [grad[:, n : n + lanes] for n in range(0, grad.shape[1], lanes)]
    split = model_width // 2
    slabs.append(jnp.concatenate([grad_router[:split], grad_router[split:]], axis=1))
    slabs.append(jnp.pad(grad_tab, ((0, 0), (0, lanes - heads))))
    slabs.append(grad_attn_gain.reshape(-1, lanes))
    slabs.append(grad_ffn_gain.reshape(-1, lanes))
    slabs = [slab.astype(half_bf) for slab in slabs]
    count = sum(slab.shape[0] for slab in slabs)
    slabs.append(jnp.zeros((-count % 2048, lanes), half_bf))
    reduced = total_all(jnp.concatenate(slabs, axis=0)).astype(jnp.float32)
    parts, start = [], 0
    for slab in slabs[:-1]:
        parts.append(reduced[start : start + slab.shape[0]])
        start += slab.shape[0]
    outs = []
    for grad in grad_weights + [grad_proj]:
        used = grad.shape[1] // lanes
        outs.append(jnp.concatenate(parts[:used], axis=1))
        parts = parts[used:]
    router_part, tab_part, attn_part, ffn_part = parts
    return (
        mixed,
        grad_input,
        attn_part.reshape(-1),
        outs[0],
        outs[1],
        outs[2],
        outs[3],
        tab_part[:, :heads],
        ffn_part.reshape(-1),
        jnp.concatenate([router_part[:, :experts], router_part[:, experts:]], axis=0),
        grad_expert_in[None],
        grad_expert_out[None],
    )


def solution(mesh):
    return jax.shard_map(
        shards,
        mesh=mesh,
        in_specs=(
            P("ctx", None),
            P(),
            P(None, "mp"),
            P(None, "mp"),
            P(None, "mp"),
            P("mp", None),
            P(None, "mp"),
            P(),
            P(),
            P(),
            P("ctx", None, "mp"),
            P("ctx", "mp", None),
            P("ctx"),
            P("ctx"),
            P("ctx", None),
        ),
        out_specs=(
            P("ctx", None),
            P("ctx", None),
            P(),
            P(None, "mp"),
            P(None, "mp"),
            P(None, "mp"),
            P("mp", None),
            P(None, "mp"),
            P(),
            P(),
            P("ctx", None, "mp"),
            P("ctx", "mp", None),
        ),
        check_vma=False,
    )
```

```python
import functools
import jax
import jax.numpy as jnp
from jax import lax
from jax.experimental import pallas as pl
from jax.experimental.pallas import tpu as pltpu
from jax.sharding import PartitionSpec as P

HEAD = 64
GROUP = 3
BLOCK = 128
PAIR = 2 * BLOCK
SPAN = 4
CHUNK = SPAN * PAIR
TILES = CHUNK // BLOCK
VMEM = pl.BlockSpec(memory_space=pltpu.VMEM)
SMEM = pl.BlockSpec(memory_space=pltpu.SMEM)
LARGE = pltpu.CompilerParams(vmem_limit_bytes=60 * 1024 * 1024)


def contract(left, right, left_dim, right_dim):
    return lax.dot_general(
        left,
        right,
        (((left_dim,), (right_dim,)), ((), ())),
        preferred_element_type=jnp.float32,
    )


def window_row(place, chunk, tile, half):
    return 63 - (SPAN * chunk + tile // 2) + place + BLOCK // 4 * (half - tile % 2)


def tile_consts(table_ref, head, place, chunk, tile):
    parts = []
    for half in range(2):
        row = window_row(place, chunk, tile, half)
        parts.append(jnp.broadcast_to(table_ref[head, pl.ds(row, 1), 0:1], (1, BLOCK)))
    return jnp.concatenate(parts, axis=1)


def chunk_mixed(uneven_ref, place, chunk):
    mixed = 0
    for tile in range(TILES):
        for half in range(2):
            mixed = mixed + uneven_ref[window_row(place, chunk, tile, half)]
    return mixed


def add_uneven(table_ref, uneven_ref, score_ref, place, chunk):
    for tile in range(TILES):
        for half in range(2):
            row = window_row(place, chunk, tile, half)

            @pl.when(uneven_ref[row] > 0)
            def _():
                for head in range(GROUP):
                    window = jnp.concatenate(
                        [table_ref[head, pl.ds(row, 1), :], table_ref[head, pl.ds(row + 1, 1), :]],
                        axis=1,
                    )
                    window = window - window[:, 0:1]
                    grid = pltpu.roll(
                        jnp.broadcast_to(window, (BLOCK, PAIR)),
                        BLOCK,
                        1,
                        stride=1,
                        stride_axis=0,
                    )[:, :BLOCK]
                    rows = slice(tile * BLOCK, (tile + 1) * BLOCK)
                    cols = slice(half * BLOCK, (half + 1) * BLOCK)
                    score_ref[head, rows, cols] += grid


def head_columns(ref, head):
    return ref[:, head * HEAD : (head + 1) * HEAD]


def turn(values):
    return values.astype(jnp.float32).T


def fill_turned(dst_ref, src_ref, first):
    for head in range(GROUP):
        part = turn(head_columns(src_ref, head))
        none = jnp.zeros_like(part)
        parts = [part, none] if first else [none, part]
        dst_ref[head] = jnp.concatenate(parts, axis=0).astype(dst_ref.dtype)


def fill_padded(dst_ref, src_ref, first):
    for head in range(GROUP):
        part = head_columns(src_ref, head)
        none = jnp.zeros_like(part)
        parts = [part, none] if first else [none, part]
        dst_ref[head] = jnp.concatenate(parts, axis=1)


def side_by_side(parts):
    return jnp.concatenate([turn(part) for part in parts], axis=1).astype(jnp.bfloat16)


def forward_kernel(
    place_ref, uneven_ref, table_ref, keys_ref, rows_ref, out_ref, turned_ref, lse_ref,
    query_ref, best_ref, sum_ref, total_ref, score_ref,
):
    place = place_ref[0]
    fill_turned(query_ref, rows_ref, True)
    best_ref[...] = jnp.full_like(best_ref, -1e30)
    sum_ref[...] = jnp.zeros_like(sum_ref)
    total_ref[...] = jnp.zeros_like(total_ref)

    def rest(chunk, head, held, scores):
        consts = [tile_consts(table_ref, head, place, chunk, tile) for tile in range(TILES)]
        old = best_ref[head]
        new = old
        for tile in range(TILES):
            part = scores[tile * BLOCK : (tile + 1) * BLOCK]
            new = jnp.maximum(new, jnp.max(part, axis=0, keepdims=True) + consts[tile])
        decay = jnp.exp(old - new)
        weights = [
            jnp.exp(scores[tile * BLOCK : (tile + 1) * BLOCK] - (new - consts[tile]))
            for tile in range(TILES)
        ]
        weights = jnp.concatenate(weights, axis=0)
        sum_ref[head] = sum_ref[head] * decay + jnp.sum(weights, axis=0, keepdims=True)
        best_ref[head] = new
        total_ref[head] = total_ref[head] * decay + contract(
            held, weights.astype(jnp.bfloat16), 0, 0
        )

    @pl.loop(0, keys_ref.shape[0] // SPAN)
    def _(chunk):
        def held_of(head):
            return keys_ref[pl.ds(chunk * SPAN, SPAN), head].reshape(CHUNK, 2 * HEAD)

        mixed = chunk_mixed(uneven_ref, place, chunk)

        @pl.when(mixed == 0)
        def _():
            for head in range(GROUP):
                held = held_of(head)
                rest(chunk, head, held, contract(held, query_ref[head], 1, 0))

        @pl.when(mixed > 0)
        def _():
            for head in range(GROUP):
                score_ref[head] = contract(held_of(head), query_ref[head], 1, 0)
            add_uneven(table_ref, uneven_ref, score_ref, place, chunk)
            for head in range(GROUP):
                rest(chunk, head, held_of(head), score_ref[head])

    for head in range(GROUP):
        turned_ref[head] = total_ref[head][HEAD:] / sum_ref[head]
    out_ref[...] = side_by_side([turned_ref[head] for head in range(GROUP)])
    for head in range(GROUP):
        lse_ref[head] = best_ref[head] + jnp.log(sum_ref[head])


def backward_kernel(
    place_ref, uneven_ref, table_ref, keys_ref, rows_ref, grads_ref, turned_ref, lse_ref,
    grad_keys_ref, grad_rows_ref, offsets_ref,
    query_t_ref, grad_t_ref, query_ref, grad_ref, delta_ref, grad_query_ref, score_ref,
):
    place = place_ref[0]
    fill_turned(query_t_ref, rows_ref, True)
    fill_turned(grad_t_ref, grads_ref, False)
    fill_padded(query_ref, rows_ref, True)
    fill_padded(grad_ref, grads_ref, False)
    for head in range(GROUP):
        delta_ref[head] = jnp.sum(
            grad_t_ref[head][HEAD:].astype(jnp.float32) * turned_ref[head], axis=0, keepdims=True
        )
    grad_query_ref[...] = jnp.zeros_like(grad_query_ref)
    offsets_ref[...] = jnp.zeros_like(offsets_ref)

    def rest(chunk, head, held, scores):
        grads = contract(held, grad_t_ref[head], 1, 0)
        probs = jnp.concatenate(
            [
                jnp.exp(
                    scores[tile * BLOCK : (tile + 1) * BLOCK]
                    - (lse_ref[head] - tile_consts(table_ref, head, place, chunk, tile))
                )
                for tile in range(TILES)
            ],
            axis=0,
        )
        slopes = probs * (grads - delta_ref[head])
        rounded = slopes.astype(jnp.bfloat16)
        part = contract(rounded, query_ref[head], 1, 0) + contract(
            probs.astype(jnp.bfloat16), grad_ref[head], 1, 0
        )
        grad_keys_ref[pl.ds(chunk * SPAN, SPAN), head] = part.astype(grad_keys_ref.dtype).reshape(
            SPAN, PAIR, 2 * HEAD
        )
        grad_query_ref[head] += contract(held, rounded, 0, 0)
        return slopes

    def put_even(chunk, head, tile, half, slopes):
        row = window_row(place, chunk, tile, half)
        offsets_ref[head, pl.ds(row, 1), :] += jnp.sum(slopes, axis=0, keepdims=True)

    def put_uneven(chunk, head, tile, half, slopes):
        row = window_row(place, chunk, tile, half)
        wide = jnp.concatenate([slopes, jnp.zeros_like(slopes)], axis=1)
        folded = jnp.zeros((8, PAIR), jnp.float32)
        for group in range(BLOCK // 8):
            folded = folded + pltpu.roll(
                wide[group * 8 : (group + 1) * 8], (BLOCK - 8 * group) % PAIR, 1
            )
        line = jnp.zeros((1, PAIR), jnp.float32)
        for step in range(8):
            line = line + pltpu.roll(folded, (PAIR - step) % PAIR, 1)[step : step + 1]
        offsets_ref[head, pl.ds(row, 1), :] += line[:, :BLOCK]
        offsets_ref[head, pl.ds(row + 1, 1), :] += line[:, BLOCK:]

    @pl.loop(0, keys_ref.shape[0] // SPAN)
    def _(chunk):
        def held_of(head):
            return keys_ref[pl.ds(chunk * SPAN, SPAN), head].reshape(CHUNK, 2 * HEAD)

        mixed = chunk_mixed(uneven_ref, place, chunk)

        @pl.when(mixed == 0)
        def _():
            for head in range(GROUP):
                held = held_of(head)
                slopes = rest(chunk, head, held, contract(held, query_t_ref[head], 1, 0))
                for tile in range(TILES):
                    for half in range(2):
                        part = slopes[
                            tile * BLOCK : (tile + 1) * BLOCK, half * BLOCK : (half + 1) * BLOCK
                        ]
                        put_even(chunk, head, tile, half, part)

        @pl.when(mixed > 0)
        def _():
            for head in range(GROUP):
                score_ref[head] = contract(held_of(head), query_t_ref[head], 1, 0)
            add_uneven(table_ref, uneven_ref, score_ref, place, chunk)
            for head in range(GROUP):
                score_ref[head] = rest(chunk, head, held_of(head), score_ref[head])
            for tile in range(TILES):
                for half in range(2):
                    rows = slice(tile * BLOCK, (tile + 1) * BLOCK)
                    cols = slice(half * BLOCK, (half + 1) * BLOCK)
                    uneven = uneven_ref[window_row(place, chunk, tile, half)]

                    @pl.when(uneven == 0)
                    def _():
                        for head in range(GROUP):
                            put_even(chunk, head, tile, half, score_ref[head, rows, cols])

                    @pl.when(uneven > 0)
                    def _():
                        for head in range(GROUP):
                            put_uneven(chunk, head, tile, half, score_ref[head, rows, cols])

    grad_rows_ref[...] = side_by_side([grad_query_ref[head][:HEAD] for head in range(GROUP)])


def attend(place, uneven, table, keys, rows):
    shape = jax.ShapeDtypeStruct
    return pl.pallas_call(
        forward_kernel,
        out_shape=(
            shape(rows.shape, jnp.bfloat16),
            shape((GROUP, HEAD, PAIR), jnp.float32),
            shape((GROUP, 1, PAIR), jnp.float32),
        ),
        in_specs=[SMEM, SMEM, VMEM, VMEM, VMEM],
        out_specs=(VMEM, VMEM, VMEM),
        scratch_shapes=[
            pltpu.VMEM((GROUP, 2 * HEAD, PAIR), jnp.bfloat16),
            pltpu.VMEM((GROUP, 1, PAIR), jnp.float32),
            pltpu.VMEM((GROUP, 1, PAIR), jnp.float32),
            pltpu.VMEM((GROUP, 2 * HEAD, PAIR), jnp.float32),
            pltpu.VMEM((GROUP, CHUNK, PAIR), jnp.float32),
        ],
        compiler_params=LARGE,
        name="attend",
    )(place, uneven, table, keys, rows)


def attend_back(place, uneven, table, keys, rows, grads, turned, lse):
    shape = jax.ShapeDtypeStruct
    return pl.pallas_call(
        backward_kernel,
        out_shape=(
            shape(keys.shape, jnp.bfloat16),
            shape(rows.shape, jnp.bfloat16),
            shape((GROUP, BLOCK, BLOCK), jnp.float32),
        ),
        in_specs=[SMEM, SMEM] + [VMEM] * 6,
        out_specs=(VMEM, VMEM, VMEM),
        scratch_shapes=[
            pltpu.VMEM((GROUP, 2 * HEAD, PAIR), jnp.bfloat16),
            pltpu.VMEM((GROUP, 2 * HEAD, PAIR), jnp.bfloat16),
            pltpu.VMEM((GROUP, PAIR, 2 * HEAD), jnp.bfloat16),
            pltpu.VMEM((GROUP, PAIR, 2 * HEAD), jnp.bfloat16),
            pltpu.VMEM((GROUP, 1, PAIR), jnp.float32),
            pltpu.VMEM((GROUP, 2 * HEAD, PAIR), jnp.float32),
            pltpu.VMEM((GROUP, CHUNK, PAIR), jnp.float32),
        ],
        compiler_params=LARGE,
        name="attend_back",
    )(place, uneven, table, keys, rows, grads, turned, lse)


def offset_tables(rel_bucket, rel_table):
    flipped = jnp.flip(jnp.pad(rel_bucket, (0, 1), mode="edge")).reshape(BLOCK, BLOCK)
    buckets = rel_table.shape[0]
    hit = flipped[None, None] == jnp.arange(buckets, dtype=jnp.int32)[None, :, None, None]
    table = jnp.sum(jnp.where(hit, rel_table.T[:, :, None, None], 0.0), axis=1)
    low = jnp.min(flipped, axis=1)
    high = jnp.max(flipped, axis=1)
    following = jnp.minimum(jnp.arange(BLOCK) + 1, BLOCK - 1)
    uneven = jnp.maximum(high, high[following]) != jnp.minimum(low, low[following])
    return flipped, table, uneven.astype(jnp.int32)


def table_grad(flipped, offsets, buckets):
    hit = flipped[None, None] == jnp.arange(buckets, dtype=jnp.int32)[:, None, None, None]
    return jnp.sum(jnp.where(hit, offsets[None], 0.0), axis=(2, 3))


EPSILON = 1e-06
PRECISE = lax.Precision.HIGHEST
ANYWHERE = pl.BlockSpec(memory_space=pl.ANY)
SIDE = 4


class Place:
    def __init__(self):
        self.me = lax.axis_index("ctx")
        self.core = lax.rem(self.me, 2)
        self.z = lax.rem(self.me // 2, SIDE)
        self.x = lax.rem(self.me // (2 * SIDE), SIDE)
        self.y = self.me // (2 * SIDE * SIDE)

    def at(self, dx=0, dz=0, dcore=0, dy=0):
        x = lax.rem(self.x + dx, SIDE)
        z = lax.rem(self.z + dz, SIDE)
        core = lax.rem(self.core + dcore, 2)
        y = lax.rem(self.y + dy, 2)
        return ((y * SIDE + x) * SIDE + z) * 2 + core

    def turned(self, axis, step):
        return self.at(dx=step) if axis == 0 else self.at(dz=step)

    def along(self, axis, step):
        return lax.rem((self.x if axis == 0 else self.z) + step, SIDE)


def meet(targets, across=False):
    barrier = pltpu.get_barrier_semaphore()
    if across:
        pl.semaphore_signal(
            barrier,
            inc=1,
            device_id={"mp": 1 - lax.axis_index("mp")},
            device_id_type=pl.DeviceIdType.MESH,
        )
    for target in targets:
        pl.semaphore_signal(
            barrier, inc=1, device_id={"ctx": target}, device_id_type=pl.DeviceIdType.MESH
        )
    pl.semaphore_wait(barrier, len(targets) + int(across))


def ring_targets(place):
    found = [place.at(dcore=1)]
    for step in (1, SIDE - 1):
        found += [place.at(dx=step), place.at(dz=step)]
    return found


def sender(target, src, dst, send_sem, recv_sem):
    return pltpu.make_async_remote_copy(
        src_ref=src,
        dst_ref=dst,
        send_sem=send_sem,
        recv_sem=recv_sem,
        device_id={"ctx": target},
        device_id_type=pl.DeviceIdType.MESH,
    )


def wide(value):
    return value.astype(jnp.float32)


class Sends:
    def __init__(self, place, sems):
        self.place, self.sems, self.started = place, sems, []

    def go(self, target, src, dst, recv_sem):
        copy = sender(target, src, dst, self.sems.at[len(self.started)], recv_sem)
        copy.start()
        self.started.append(copy)
        return copy

    def across(self, src, dst, recv_sem):
        copy = pltpu.make_async_remote_copy(
            src_ref=src,
            dst_ref=dst,
            send_sem=self.sems.at[len(self.started)],
            recv_sem=recv_sem,
            device_id={"mp": 1 - lax.axis_index("mp")},
            device_id_type=pl.DeviceIdType.MESH,
        )
        copy.start()
        self.started.append(copy)

    def landed(self, view, sem):
        sender(self.place.me, view, view, sem, sem).wait_recv()

    def finish(self):
        for copy in self.started:
            copy.wait_send()


def gather_kernel(block_ref, out_ref, local_sem, send_sem, ring_recv, twin_recv):
    place = Place()
    meet(ring_targets(place))
    sends = Sends(place, send_sem)
    half_rows = block_ref.shape[1] // 2
    sub_rows = half_rows // 2

    def rows_of(half, piece):
        if piece is None:
            return pl.ds(half * half_rows, half_rows)
        return pl.ds(half * half_rows + piece * sub_rows, sub_rows)

    def view(half, first, second, core, piece=None):
        x, z = (second, first) if half == 0 else (first, second)
        slot = (place.along(0, x) * SIDE + place.along(1, z)) * 2 + core
        return out_ref.at[slot, :, rows_of(half, piece)]

    def held(half, first, second, piece=None):
        if first == 0 and second == 0:
            return block_ref.at[:, rows_of(half, piece)]
        return view(half, first, second, place.core, piece)

    def shift(half, first, second, stage, step, piece=None):
        axis = 1 - half if stage == 0 else half
        if stage == 0:
            slot = ((first - step) % SIDE, second)
        else:
            slot = (first, (second - step) % SIDE)
        sends.go(
            place.turned(axis, step % SIDE),
            held(half, first, second, piece),
            view(half, first, second, place.core, piece),
            ring_recv.at[half, slot[0], slot[1], piece or 0],
        )

    def to_twin(half, first, second):
        sends.go(
            place.at(dcore=1),
            held(half, first, second),
            view(half, first, second, place.core),
            twin_recv.at[half, first, second],
        )

    def wait(half, first, second):
        if 2 in (first, second) and not (first == 2 and second in (1, 3)):
            for piece in range(2):
                sends.landed(
                    view(half, first, second, place.core, piece),
                    ring_recv.at[half, first, second, piece],
                )
        else:
            sends.landed(
                view(half, first, second, place.core), ring_recv.at[half, first, second, 0]
            )

    def relay(half, first, second, stage):
        moved = first if stage == 0 else second
        if moved == SIDE - 1:
            shift(half, first, second, stage, 1, 0)
        elif moved == 1:
            shift(half, first, second, stage, -1, 1)

    own = pltpu.make_async_copy(
        block_ref, out_ref.at[(place.x * SIDE + place.z) * 2 + place.core], local_sem
    )
    own.start()
    for stage in range(2):
        for step in (1, -1):
            for half in range(2):
                shift(half, 0, 0, stage, step)
    for half in range(2):
        to_twin(half, 0, 0)
    order = [(3, 0), (1, 0), (0, 3), (0, 1), (2, 0), (3, 3), (3, 1), (1, 3), (1, 1), (0, 2)]
    order += [(3, 2), (1, 2), (2, 3), (2, 1), (2, 2)]
    for first, second in order:
        for half in range(2):
            wait(half, first, second)
            if second == 0:
                relay(half, first, second, 0)
                for step in (1, -1):
                    shift(half, first, second, 1, step)
            else:
                relay(half, first, second, 1)
            to_twin(half, first, second)
    for first, second in [(0, 0)] + order:
        for half in range(2):
            sends.landed(
                view(half, first, second, 1 - place.core), twin_recv.at[half, first, second]
            )
    own.wait()
    sends.finish()


def gather_plane(block):
    shape = (2 * SIDE * SIDE,) + block.shape
    sem = pltpu.SemaphoreType.DMA
    return pl.pallas_call(
        gather_kernel,
        out_shape=jax.ShapeDtypeStruct(shape, block.dtype),
        in_specs=[ANYWHERE],
        out_specs=ANYWHERE,
        scratch_shapes=[sem, sem((72,)), sem((2, SIDE, SIDE, 2)), sem((2, SIDE, SIDE))],
        compiler_params=pltpu.CompilerParams(
            collective_id=1, has_side_effects=True, vmem_limit_bytes=32 * 1024 * 1024
        ),
        name="gather_plane",
    )(block)


def ring_sum(sends, axis_of, sums, via, landing, via_recv, land_recv, ready):
    place = sends.place
    rows = sums.shape[-2] // 2
    middle = (slice(None),) * (len(sums.shape) - 4)

    def cut(ref, index, piece):
        return ref.at[index + middle + (pl.ds(piece * rows, rows),)]

    for half in range(2):
        ready(half, 2)
        for piece, step in ((0, 1), (1, SIDE - 1)):
            sends.go(
                place.turned(axis_of(half), step),
                cut(sums, (half, 2), piece),
                via.at[half, piece],
                via_recv.at[half, piece],
            )
    for half in range(2):
        for piece, step in ((0, 1), (1, SIDE - 1)):
            ready(half, step)
            sends.go(
                place.turned(axis_of(half), step),
                cut(sums, (half, step), 1 - piece),
                cut(landing, (half, piece), 1 - piece),
                land_recv.at[half, piece, 1 - piece],
            )
    for half in range(2):
        ready(half, 0)
    for half in range(2):
        for piece, step in ((0, 1), (1, SIDE - 1)):
            sends.landed(via.at[half, piece], via_recv.at[half, piece])
            spot = (half, step) + middle + (slice(piece * rows, (piece + 1) * rows),)
            sums[spot] = (wide(sums[spot]) + wide(via[half, piece])).astype(sums.dtype)
            sends.go(
                place.turned(axis_of(half), step),
                cut(sums, (half, step), piece),
                cut(landing, (half, piece), piece),
                land_recv.at[half, piece, piece],
            )

    def finish(half):
        for piece in range(2):
            for part in (1 - piece, piece):
                sends.landed(cut(landing, (half, piece), part), land_recv.at[half, piece, part])

    return finish


def scatter_kernel(
    parts_ref, rows_ref, out_ref, mine, twin, sums, via_one, land_one, halves, via_two, land_two,
    both, other,
    local_sem, send_sem, twin_recv, via_one_recv, land_one_recv, via_two_recv, land_two_recv,
    far_recv,
):
    place = Place()
    half_rows = parts_ref.shape[4] // 2

    def source(half, group, core):
        rows = pl.ds(half * half_rows, half_rows)
        if half == 0:
            return parts_ref.at[group, :, core, :, rows]
        return parts_ref.at[:, group, core, :, rows]

    loads = {}
    order = (2, 1, 3, 0)
    for step in order:
        for half in range(2):
            loads[half, step] = pltpu.make_async_copy(
                source(half, place.along(half, step), place.core),
                mine.at[half, step],
                local_sem.at[half, step],
            )
            loads[half, step].start()
    meet(ring_targets(place) + [place.at(dy=1)])
    sends = Sends(place, send_sem)
    for step in order:
        for half in range(2):
            sends.go(
                place.at(dcore=1),
                source(half, place.along(half, step), 1 - place.core),
                twin.at[half, step],
                twin_recv.at[half, step],
            )

    def ready_one(half, step):
        loads[half, step].wait()
        sends.landed(twin.at[half, step], twin_recv.at[half, step])
        sums[half, step] = (wide(mine[half, step]) + wide(twin[half, step])).astype(sums.dtype)

    done_one = ring_sum(
        sends, lambda half: half, sums, via_one, land_one, via_one_recv, land_one_recv, ready_one
    )
    arrived = set()

    def ready_two(half, step):
        if half not in arrived:
            arrived.add(half)
            done_one(half)
        spot = place.along(1 - half, step)
        total = wide(sums[half, 0, spot])
        for side in range(2):
            total = total + wide(land_one[half, side, spot])
        halves[half, step] = total.astype(halves.dtype)

    done_two = ring_sum(
        sends, lambda half: 1 - half, halves, via_two, land_two, via_two_recv, land_two_recv,
        ready_two,
    )
    for half in range(2):
        done_two(half)
        total = wide(halves[half, 0])
        for side in range(2):
            total = total + wide(land_two[half, side])
        total = total.astype(both.dtype)
        parts = [rows_ref[half * half_rows : (half + 1) * half_rows]]
        parts += [total[head, :, :HEAD] for head in range(GROUP)]
        parts += [total[head, :, HEAD:] for head in range(GROUP)]
        both[half] = jnp.concatenate(parts, axis=1)
    sends.go(place.at(dy=1), both.at[1 - place.y], other, far_recv)
    width = GROUP * HEAD
    kept = both[place.y]
    sends.landed(other, far_recv)
    received = other[...]
    low = jnp.where(place.y == 0, kept, received)
    high = jnp.where(place.y == 0, received, kept)
    parts = []
    for n in range(3):
        parts += [low[:, n * width : (n + 1) * width], high[:, n * width : (n + 1) * width]]
    out_ref[...] = jnp.concatenate(parts, axis=1)
    sends.finish()


def scatter_plane(parts, rows_grad):
    heads, rows, lanes = parts.shape[1:]
    piece = (heads, rows // 2, lanes)
    small = (heads, rows // 4, lanes)
    kind = parts.dtype
    sem = pltpu.SemaphoreType.DMA
    return pl.pallas_call(
        scatter_kernel,
        out_shape=jax.ShapeDtypeStruct((rows // 2, 6 * rows_grad.shape[1]), kind),
        in_specs=[ANYWHERE, VMEM],
        out_specs=pl.BlockSpec(memory_space=pltpu.VMEM),
        scratch_shapes=[
            pltpu.VMEM((2, SIDE, SIDE) + piece, kind),
            pltpu.VMEM((2, SIDE, SIDE) + piece, kind),
            pltpu.VMEM((2, SIDE, SIDE) + piece, kind),
            pltpu.VMEM((2, 2, SIDE) + small, kind),
            pltpu.VMEM((2, 2, SIDE) + piece, kind),
            pltpu.VMEM((2, SIDE) + piece, kind),
            pltpu.VMEM((2, 2) + small, kind),
            pltpu.VMEM((2, 2) + piece, kind),
            pltpu.VMEM((2, rows // 2, 3 * rows_grad.shape[1]), kind),
            pltpu.VMEM((rows // 2, 3 * rows_grad.shape[1]), kind),
            sem((2, SIDE)), sem((33,)), sem((2, SIDE)),
            sem((2, 2)), sem((2, 2, 2)), sem((2, 2)), sem((2, 2, 2)), sem,
        ],
        compiler_params=pltpu.CompilerParams(
            collective_id=2, has_side_effects=True, vmem_limit_bytes=32 * 1024 * 1024
        ),
        name="scatter_plane",
    )(parts.reshape((SIDE, SIDE, 2) + parts.shape[1:]), rows_grad)


LANES = 128
UNIT = 16
UNITS = 9
BLOCK_ROWS = UNIT * (UNITS + 1)


def runs(slab_rows):
    found, unit = [], 0
    for slab, rows in enumerate(slab_rows):
        row = 0
        while row < rows:
            block, inside = divmod(unit, UNITS)
            take = min(UNITS - inside, (rows - row) // UNIT)
            found.append((slab, row, block, inside * UNIT, take * UNIT))
            row += take * UNIT
            unit += take
    return found


def block_at(block):
    return block // 32, block // 16 % 2, block // 4 % 4, block % 4


def weights_kernel(
    normed_ref, grads_ref, context_ref, attended_ref, small_ref, w_query_ref, w_key_ref,
    w_value_ref, tokens_ref, hidden_ref, gain_ref,
    query_ref, key_ref, value_ref, proj_ref, small_out_ref, input_ref,
    share, share_other, parts, full, twin, sums, via_one, land_one, halves, via_two, land_two, other,
    send_sem, twin_recv, via_one_recv, land_one_recv, via_two_recv, land_two_recv,
    far_recv, far_back_recv, two_back_recv, one_back_recv, twin_back_recv, share_recv,
):
    place = Place()
    width = query_ref.shape[1]
    meet(ring_targets(place) + [place.at(dy=1)], True)
    sends = Sends(place, send_sem)
    partial = jnp.zeros(share.shape, jnp.float32)
    for n, ref in enumerate((w_query_ref, w_key_ref, w_value_ref)):
        partial = partial + contract(grads_ref[:, n * width : (n + 1) * width], ref[...], 1, 1)
    share[...] = partial.astype(share.dtype)
    sends.across(share, share_other, share_recv)
    slabs = []
    for n, ref in enumerate((query_ref, key_ref, value_ref)):
        for lane in range(0, width, LANES):
            slabs.append((ref, lane, normed_ref, grads_ref, n * width + lane))
    for lane in range(0, proj_ref.shape[1], LANES):
        slabs.append((proj_ref, lane, context_ref, attended_ref, lane))
    table = runs([slab[0].shape[0] for slab in slabs])
    for index, (_, _, left, right, lane) in enumerate(slabs):
        grad = contract(left[...], right[:, lane : lane + LANES], 0, 0).astype(parts.dtype)
        for slab, row, block, inside, rows in table:
            if slab == index:
                parts[block_at(block) + (slice(inside, inside + rows),)] = grad[row : row + rows]
    sends.landed(share_other, share_recv)
    grad_normed = wide(share[...]) + wide(share_other[...])
    floats_in = wide(tokens_ref[...])
    scale = lax.rsqrt(jnp.mean(floats_in * floats_in, axis=1, keepdims=True) + EPSILON)
    scaled = gain_ref[...] * grad_normed
    input_ref[...] = (
        hidden_ref[...]
        + scale * scaled
        - floats_in * scale**3 * jnp.mean(scaled * floats_in, axis=1, keepdims=True)
    )
    gain_sum = jnp.sum(grad_normed * floats_in * scale, axis=0, keepdims=True)
    for block in range(64):
        parts[block_at(block) + (slice(UNIT * UNITS, BLOCK_ROWS),)] = small_ref[
            block * UNIT : (block + 1) * UNIT
        ]
    lines = [gain_sum[:, n : n + LANES] for n in range(0, gain_sum.shape[1], LANES)]
    lines.append(jnp.zeros((UNIT - len(lines), LANES), jnp.float32))
    parts[block_at(63) + (slice(UNIT * UNITS, BLOCK_ROWS),)] = jnp.concatenate(
        lines, axis=0
    ).astype(parts.dtype)

    order = (2, 1, 3, 0)
    for step in order:
        for half in range(2):
            sends.go(
                place.at(dcore=1),
                parts.at[half, 1 - place.core, place.along(half, step)],
                twin.at[half, step],
                twin_recv.at[half, step],
            )

    def ready_one(half, step):
        sends.landed(twin.at[half, step], twin_recv.at[half, step])
        own = parts[half, place.core, place.along(half, step)]
        sums[half, step] = (wide(own) + wide(twin[half, step])).astype(sums.dtype)

    done_one = ring_sum(
        sends, lambda half: half, sums, via_one, land_one, via_one_recv, land_one_recv, ready_one
    )
    arrived = set()

    def ready_two(half, step):
        if half not in arrived:
            arrived.add(half)
            done_one(half)
        spot = place.along(1 - half, step)
        total = wide(sums[half, 0, spot])
        for side in range(2):
            total = total + wide(land_one[half, side, spot])
        halves[half, step] = total.astype(halves.dtype)

    done_two = ring_sum(
        sends, lambda half: 1 - half, halves, via_two, land_two, via_two_recv, land_two_recv,
        ready_two,
    )
    low = BLOCK_ROWS // 2
    for half in range(2):
        done_two(half)
        total = wide(halves[half, 0])
        for side in range(2):
            total = total + wide(land_two[half, side])
        halves[half, 0] = total.astype(halves.dtype)
        sends.go(
            place.at(dy=1),
            halves.at[half, 0, pl.ds(pl.multiple_of((1 - place.y) * low, UNIT), low)],
            other.at[half],
            far_recv.at[half],
        )

    def spot(half, core, first, second, rows=None):
        place_of = (half, core, place.along(half, first), place.along(1 - half, second))
        return full.at[place_of] if rows is None else full.at[place_of + (rows,)]

    def y_rows(y):
        return pl.ds(pl.multiple_of(y * low, UNIT), low)

    for half in range(2):
        sends.landed(other.at[half], far_recv.at[half])
        total = wide(halves[half, 0, y_rows(place.y)]) + wide(other[half])
        full[
            half, place.core, place.along(half, 0), place.along(1 - half, 0), y_rows(place.y)
        ] = total.astype(full.dtype)
        view = spot(half, place.core, 0, 0, y_rows(place.y))
        sends.go(place.at(dy=1), view, view, far_back_recv.at[half])

    subs = [pl.ds(piece * low, low) for piece in range(2)]
    for half in range(2):
        sends.landed(
            spot(half, place.core, 0, 0, y_rows(1 - place.y)), far_back_recv.at[half]
        )
        view = spot(half, place.core, 0, 0)
        for index, step in enumerate((1, SIDE - 1)):
            sends.go(
                place.turned(1 - half, step), view, view, two_back_recv.at[half, SIDE - step, 0]
            )
    for half in range(2):
        for piece, step in ((0, 1), (1, SIDE - 1)):
            sends.landed(
                spot(half, place.core, 0, SIDE - step), two_back_recv.at[half, SIDE - step, 0]
            )
            view = spot(half, place.core, 0, SIDE - step, subs[piece])
            sends.go(
                place.turned(1 - half, step), view, view, two_back_recv.at[half, 2, piece]
            )

    def group(half, core, first, rows=None):
        if rows is None:
            return full.at[half, core, place.along(half, first)]
        return full.at[half, core, place.along(half, first), :, rows]

    for half in range(2):
        for piece in range(2):
            sends.landed(
                spot(half, place.core, 0, 2, subs[piece]), two_back_recv.at[half, 2, piece]
            )
        view = group(half, place.core, 0)
        for step in (1, SIDE - 1):
            sends.go(place.turned(half, step), view, view, one_back_recv.at[half, SIDE - step, 0])
        sends.go(place.at(dcore=1), view, view, twin_back_recv.at[half, 0])
    for half in range(2):
        for piece, step in ((0, 1), (1, SIDE - 1)):
            view = group(half, place.core, SIDE - step)
            sends.landed(view, one_back_recv.at[half, SIDE - step, 0])
            part = group(half, place.core, SIDE - step, subs[piece])
            sends.go(place.turned(half, step), part, part, one_back_recv.at[half, 2, piece])
            sends.go(place.at(dcore=1), view, view, twin_back_recv.at[half, SIDE - step])
    for half in range(2):
        for piece in range(2):
            sends.landed(group(half, place.core, 2, subs[piece]), one_back_recv.at[half, 2, piece])
        view = group(half, place.core, 2)
        sends.go(place.at(dcore=1), view, view, twin_back_recv.at[half, 2])
    for first in (0, 3, 1, 2):
        for half in range(2):
            sends.landed(group(half, 1 - place.core, first), twin_back_recv.at[half, first])

    for slab, row, block, inside, rows in table:
        ref, lane = slabs[slab][:2]
        ref[row : row + rows, lane : lane + LANES] = wide(
            full[block_at(block) + (slice(inside, inside + rows),)]
        )
    for block in range(64):
        small_out_ref[block * UNIT : (block + 1) * UNIT] = wide(
            full[block_at(block) + (slice(UNIT * UNITS, BLOCK_ROWS),)]
        )
    sends.finish()


def weight_totals(normed, grads, context, attended, small, weights, tokens, grad_hidden, gain):
    kind = jnp.bfloat16
    tall = normed.shape[1]
    local = context.shape[1]
    piece = (BLOCK_ROWS, LANES)
    part = (BLOCK_ROWS // 2, LANES)
    sem = pltpu.SemaphoreType.DMA
    floats = functools.partial(jax.ShapeDtypeStruct, dtype=jnp.float32)
    return pl.pallas_call(
        weights_kernel,
        out_shape=(
            floats((tall, local)),
            floats((tall, local)),
            floats((tall, local)),
            floats((local, tall)),
            floats(small.shape),
            floats(tokens.shape),
        ),
        in_specs=[VMEM] * 11,
        out_specs=(VMEM,) * 6,
        scratch_shapes=[
            pltpu.VMEM(tokens.shape, kind),
            pltpu.VMEM(tokens.shape, kind),
            pltpu.VMEM((2, 2, SIDE, SIDE) + piece, kind),
            pltpu.VMEM((2, 2, SIDE, SIDE) + piece, kind),
            pltpu.VMEM((2, SIDE, SIDE) + piece, kind),
            pltpu.VMEM((2, SIDE, SIDE) + piece, kind),
            pltpu.VMEM((2, 2, SIDE) + part, kind),
            pltpu.VMEM((2, 2, SIDE) + piece, kind),
            pltpu.VMEM((2, SIDE) + piece, kind),
            pltpu.VMEM((2, 2) + part, kind),
            pltpu.VMEM((2, 2) + piece, kind),
            pltpu.VMEM((2,) + part, kind),
            sem((64,)), sem((2, SIDE)),
            sem((2, 2)), sem((2, 2, 2)), sem((2, 2)), sem((2, 2, 2)),
            sem((2,)), sem((2,)), sem((2, SIDE, 2)), sem((2, SIDE, 2)), sem((2, SIDE)), sem,
        ],
        compiler_params=pltpu.CompilerParams(
            collective_id=3, has_side_effects=True, vmem_limit_bytes=48 * 1024 * 1024
        ),
        name="weight_totals",
    )(normed, grads, context, attended, small, *weights, tokens, grad_hidden, gain)


QUARTERS = 4


def gelu_pair(values):
    root = 0.7978845608028654
    cubic = 0.044715
    square = values * values
    bend = jnp.tanh(root * values * (1.0 + cubic * square))
    active = 0.5 * values * (1.0 + bend)
    slope = 0.5 * (1.0 + bend) + 0.5 * values * (1.0 - bend * bend) * root * (
        1.0 + 3.0 * cubic * square
    )
    return active, slope


def middle_kernel(
    both_ref, tokens_ref, cotangent_ref, proj_ref, gain_ref, router_ref, route_ref, spot_row_ref,
    spot_col_ref, w_in_hbm, w_out_hbm,
    mixed_ref, hidden_ref, attended_ref, context_ref, grad_both_ref, grad_router_ref,
    grad_gain_ref, rows_in_ref, rows_grad_ref, activ_ref, grad_pre_ref,
    w_in, w_out, swapped, share, share_other, order, order_t, gather_t, send_one, recv_one,
    send_two, recv_two, sums, sums_other, given,
    load_sem, send_sem, one_send, one_recv, two_send, two_recv, swap_recv, share_recv,
    sums_recv, back_recv,
):
    place = Place()
    me = place.me
    count = 2 * 2 * SIDE * SIDE
    loads = [
        pltpu.make_async_copy(w_in_hbm, w_in, load_sem.at[0]),
        pltpu.make_async_copy(w_out_hbm, w_out, load_sem.at[1]),
    ]
    for load in loads:
        load.start()
    barrier = pltpu.get_barrier_semaphore()

    @pl.loop(1, count)
    def _(step):
        pl.semaphore_signal(
            barrier,
            inc=1,
            device_id={"ctx": lax.rem(me + step, count)},
            device_id_type=pl.DeviceIdType.MESH,
        )

    pl.semaphore_signal(
        barrier,
        inc=1,
        device_id={"mp": 1 - lax.axis_index("mp")},
        device_id_type=pl.DeviceIdType.MESH,
    )
    pl.semaphore_wait(barrier, count)
    sends = Sends(place, send_sem)
    tok_rows = tokens_ref.shape[0]
    first = place.y == 0

    mine = pl.ds(pl.multiple_of(place.y * tok_rows, tok_rows), tok_rows)
    theirs = pl.ds(pl.multiple_of((1 - place.y) * tok_rows, tok_rows), tok_rows)
    sends.go(place.at(dy=1), both_ref.at[theirs], swapped, swap_recv)
    kept = both_ref[mine]
    sends.landed(swapped, swap_recv)
    received = swapped[...]
    context = jnp.concatenate(
        [jnp.where(first, kept, received), jnp.where(first, received, kept)], axis=1
    )
    context_ref[...] = context
    share[...] = contract(context, proj_ref[...], 1, 0).astype(share.dtype)
    sends.across(share, share_other, share_recv)
    spots = tok_rows * QUARTERS
    cells = 16 * count
    gather = jnp.where(
        lax.broadcasted_iota(jnp.int32, (cells, spots), 0) == spot_row_ref[...], 1.0, 0.0
    ).astype(jnp.bfloat16)
    sends.landed(share_other, share_recv)
    hidden = wide(tokens_ref[...]) + (wide(share[...]) + wide(share_other[...]))
    scale = lax.rsqrt(jnp.mean(hidden * hidden, axis=1, keepdims=True) + EPSILON)
    normed = hidden * scale * gain_ref[...]
    logits = lax.dot_general(
        normed, router_ref[...], (((1,), (0,)), ((), ())), precision=PRECISE,
        preferred_element_type=jnp.float32,
    )
    shifted = jnp.exp(logits - jnp.max(logits, axis=1, keepdims=True))
    probs = shifted / jnp.sum(shifted, axis=1, keepdims=True)
    chosen = jnp.where(
        route_ref[...] == lax.broadcasted_iota(jnp.int32, probs.shape, 1), 1.0, 0.0
    )
    gate = jnp.sum(probs * chosen, axis=1, keepdims=True)
    grad_y = wide(cotangent_ref[...])
    width = 2 * tokens_ref.shape[1] // QUARTERS
    payload = [normed[:, :width], normed[:, width:]]
    payload += [gate * grad_y[:, :width], gate * grad_y[:, width:]]
    payload = jnp.concatenate(payload, axis=0).astype(jnp.bfloat16)
    send_one[...] = (
        contract(gather, payload, 1, 0).astype(send_one.dtype).reshape(send_one.shape)
    )

    def exchange(src, dst, send, recv):
        @pl.loop(1, count)
        def _(step):
            target = lax.rem(me + step, count)
            sender(target, src.at[target], dst.at[me], send.at[step], recv.at[step]).start()

        dst[me] = src[me]

    def arrive(dst, recv):
        @pl.loop(1, count)
        def _(step):
            source = lax.rem(me + count - step, count)
            sends.landed(dst.at[source], recv.at[step])

    exchange(send_one, recv_one, one_send, one_recv)
    rows = cells // QUARTERS

    def cell_of(index):
        row = index & (rows - 1)
        return (row >> 2) * 16 + (index >> 8) * 4 + (row & 3)

    down = lax.broadcasted_iota(jnp.int32, (cells, cells), 0)
    right = lax.broadcasted_iota(jnp.int32, (cells, cells), 1)
    order[...] = jnp.where(cell_of(down) == right, 1.0, 0.0).astype(order.dtype)
    order_t[...] = jnp.where(down == cell_of(right), 1.0, 0.0).astype(order_t.dtype)
    gather_t[...] = jnp.where(
        spot_col_ref[...] == lax.broadcasted_iota(jnp.int32, (spots, cells), 1), 1.0, 0.0
    ).astype(gather_t.dtype)
    for load in loads:
        load.wait()
    arrive(recv_one, one_recv)

    got = contract(order[...], recv_one[...].reshape(cells, width), 1, 0).astype(jnp.bfloat16)
    rows_in_ref[...] = jnp.concatenate([got[:rows], got[rows : 2 * rows]], axis=1)
    rows_grad_ref[...] = jnp.concatenate([got[2 * rows : 3 * rows], got[3 * rows :]], axis=1)
    hidden_units = w_in.shape[1]
    chunk = hidden_units // 3
    out = jnp.zeros(rows_in_ref.shape, jnp.float32)
    back = jnp.zeros(rows_in_ref.shape, jnp.float32)
    for start in range(0, hidden_units, chunk):
        units = slice(start, start + chunk)
        active, slope = gelu_pair(contract(rows_in_ref[...], w_in[:, units], 1, 0))
        active = active.astype(jnp.bfloat16)
        activ_ref[:, units] = active
        out = out + contract(active, w_out[units], 1, 0)
        grad_pre = (contract(rows_grad_ref[...], w_out[units], 1, 1) * slope).astype(jnp.bfloat16)
        grad_pre_ref[:, units] = grad_pre
        back = back + contract(grad_pre, w_in[:, units], 1, 1)
    whole = [out[:, :width], out[:, width:], back[:, :width], back[:, width:]]
    whole = jnp.concatenate(whole, axis=0).astype(jnp.bfloat16)
    send_two[...] = (
        contract(order_t[...], whole, 1, 0).astype(send_two.dtype).reshape(send_two.shape)
    )
    exchange(send_two, recv_two, two_send, two_recv)
    arrive(recv_two, two_recv)
    sums[...] = contract(gather_t[...], recv_two[...].reshape(cells, width), 1, 0).astype(
        sums.dtype
    )
    sends.across(sums, sums_other, sums_recv)
    sends.landed(sums_other, sums_recv)
    total = wide(sums[...]) + wide(sums_other[...])
    parts = [total[n * tok_rows : (n + 1) * tok_rows] for n in range(QUARTERS)]
    expert_rows = jnp.concatenate(parts[:2], axis=1).astype(jnp.bfloat16).astype(jnp.float32)
    grad_sent = jnp.concatenate(parts[2:], axis=1).astype(jnp.bfloat16).astype(jnp.float32)

    mixed_ref[...] = (hidden + gate * expert_rows).astype(mixed_ref.dtype)
    grad_gate = jnp.sum(grad_y * expert_rows, axis=1, keepdims=True)
    grad_logits = grad_gate * gate * (chosen - probs)
    grad_router_ref[...] = lax.dot_general(
        normed, grad_logits, (((0,), (0,)), ((), ())), precision=PRECISE,
        preferred_element_type=jnp.float32,
    )
    grad_normed = grad_sent + lax.dot_general(
        grad_logits, router_ref[...], (((1,), (1,)), ((), ())), precision=PRECISE,
        preferred_element_type=jnp.float32,
    )
    scaled = gain_ref[...] * grad_normed
    grad_gain_ref[...] = jnp.sum(grad_normed * hidden * scale, axis=0, keepdims=True)
    grad_hidden = (
        grad_y
        + scale * scaled
        - hidden * scale**3 * jnp.mean(scaled * hidden, axis=1, keepdims=True)
    )
    hidden_ref[...] = grad_hidden
    attended = grad_hidden.astype(jnp.bfloat16)
    attended_ref[...] = attended
    grad_context = contract(attended, proj_ref[...], 1, 1).astype(jnp.bfloat16)
    half = grad_context.shape[1] // 2
    left, right_part = grad_context[:, :half], grad_context[:, half:]
    given[...] = jnp.where(first, right_part, left)
    grad_both_ref[mine] = jnp.where(first, left, right_part)
    sends.go(place.at(dy=1), given, grad_both_ref.at[mine], back_recv)
    sends.landed(grad_both_ref.at[theirs], back_recv)
    sends.finish()

    @pl.loop(1, count)
    def _(step):
        for src, send in ((send_one, one_send), (send_two, two_send)):
            sender(me, src.at[0], src.at[0], send.at[step], send.at[step]).wait_send()


def middle(
    both, tokens, cotangent, w_proj, gain, router, w_in, w_out, route, slot
):
    kind = jnp.bfloat16
    tok_rows, wide_row = tokens.shape
    count = router.shape[1]
    rows = 4 * count
    hidden = w_in.shape[1]
    width = 2 * wide_row // QUARTERS
    spots = QUARTERS * tok_rows
    spot = jnp.concatenate([route * 16 + 4 * n + slot for n in range(QUARTERS)])
    shape = jax.ShapeDtypeStruct
    sem = pltpu.SemaphoreType.DMA
    buffer = pltpu.VMEM((count, 16, width), kind)
    return pl.pallas_call(
        middle_kernel,
        out_shape=(
            shape(tokens.shape, kind),
            shape(tokens.shape, jnp.float32),
            shape(tokens.shape, kind),
            shape((tok_rows, 2 * both.shape[1]), kind),
            shape(both.shape, kind),
            shape(router.shape, jnp.float32),
            shape((1, wide_row), jnp.float32),
            shape((rows, wide_row), kind),
            shape((rows, wide_row), kind),
            shape((rows, hidden), kind),
            shape((rows, hidden), kind),
        ),
        in_specs=[VMEM] * 9 + [ANYWHERE] * 2,
        out_specs=(VMEM,) * 11,
        scratch_shapes=[
            pltpu.VMEM(w_in.shape, kind),
            pltpu.VMEM(w_out.shape, kind),
            pltpu.VMEM((tok_rows, both.shape[1]), kind),
            pltpu.VMEM(tokens.shape, kind),
            pltpu.VMEM(tokens.shape, kind),
            pltpu.VMEM((16 * count, 16 * count), kind),
            pltpu.VMEM((16 * count, 16 * count), kind),
            pltpu.VMEM((spots, 16 * count), kind),
            buffer, buffer, buffer, buffer,
            pltpu.VMEM((spots, width), kind),
            pltpu.VMEM((spots, width), kind),
            pltpu.VMEM((tok_rows, both.shape[1]), kind),
            sem((2,)), sem((4,)), sem((count,)), sem((count,)), sem((count,)), sem((count,)),
            sem, sem, sem, sem,
        ],
        compiler_params=pltpu.CompilerParams(
            collective_id=4, has_side_effects=True, vmem_limit_bytes=60 * 1024 * 1024
        ),
        name="middle",
    )(
        both, tokens, cotangent, w_proj, gain[None], router, route[:, None], spot[None],
        spot[:, None], w_in, w_out,
    )


def rms_scale(values):
    return lax.rsqrt(jnp.mean(values * values, axis=1, keepdims=True) + EPSILON)


def product(left, right, left_dim=1, right_dim=0):
    return contract(left, right, left_dim, right_dim)


def swap(values, axis):
    count = lax.axis_size(axis)
    pairs = [(index, (index + count // 2) % count) for index in range(count)]
    return lax.ppermute(values, axis, pairs)


def split_columns(values, first, width):
    kept = jnp.where(first, values[:, :width], values[:, width:])
    given = jnp.where(first, values[:, width:], values[:, :width])
    return kept, given


def stack_rows(kept, received, first):
    return jnp.concatenate(
        [jnp.where(first, kept, received), jnp.where(first, received, kept)], axis=0
    )


def per_head(values):
    return jnp.transpose(values.reshape(values.shape[0], GROUP, HEAD), (1, 0, 2))


def shards(
    tokens,
    attn_gain,
    w_query,
    w_key,
    w_value,
    w_proj,
    rel_table,
    rel_bucket,
    ffn_gain,
    router,
    w_in,
    w_out,
    expert_route,
    expert_slot,
    cotangent,
):
    tok_rows = tokens.shape[0]
    model_width = tokens.shape[1]
    width = GROUP * HEAD
    half_bf = jnp.bfloat16
    me = lax.axis_index("ctx")
    first = me < 32
    place = jnp.full((1,), me % 32, jnp.int32)

    floats_in = tokens.astype(jnp.float32)
    scale1 = rms_scale(floats_in)
    normed = (floats_in * scale1 * attn_gain).astype(half_bf)
    pieces = [
        split_columns(product(normed, weight).astype(half_bf), first, width)
        for weight in (w_query, w_key, w_value)
    ]
    kept = jnp.concatenate([piece[0] for piece in pieces], axis=1)
    received = swap(jnp.concatenate([piece[1] for piece in pieces], axis=1), "ctx")
    both = stack_rows(kept, received, first)
    rows = both[:, :width]
    key, value = (per_head(both[:, n * width : (n + 1) * width]) for n in (1, 2))
    held = gather_plane(jnp.concatenate([key, value], axis=2))

    own_table = jnp.where(first, rel_table[:, :GROUP], rel_table[:, GROUP:])
    flipped, table, uneven = offset_tables(rel_bucket, own_table)
    both, turned, lse = attend(place, uneven, table, held, rows)
    (
        mixed, grad_hidden1, grad_attended, context, grad_both, grad_router, grad_ffn_gain,
        rows_in, rows_grad, activ, grad_pre,
    ) = middle(
        both, tokens, cotangent, w_proj, ffn_gain, router, w_in[0], w_out[0], expert_route,
        expert_slot,
    )
    grad_expert_in = product(rows_in, grad_pre, 0, 0)
    grad_expert_out = product(activ, rows_grad, 0, 0)
    grad_parts, grad_rows, offsets = attend_back(
        place, uneven, table, held, rows, grad_both, turned, lse
    )
    grads = scatter_plane(grad_parts, grad_rows)

    own_tab = table_grad(flipped, offsets, rel_table.shape[0])
    none = jnp.zeros_like(own_tab)
    grad_tab = jnp.concatenate(
        [jnp.where(first, own_tab, none), jnp.where(first, none, own_tab)], axis=1
    )
    heads = grad_tab.shape[1]
    split = model_width // 2
    slabs = [
        jnp.concatenate([grad_router[:split], grad_router[split:]], axis=1),
        jnp.pad(grad_tab, ((0, 0), (0, LANES - heads))),
        grad_ffn_gain.reshape(-1, LANES),
    ]
    counts = [slab.shape[0] for slab in slabs]
    slabs.append(jnp.zeros((64 * UNIT - sum(counts), LANES), jnp.float32))
    small = jnp.concatenate([slab.astype(half_bf) for slab in slabs], axis=0)
    grad_query, grad_key, grad_value, grad_proj, small, grad_input = weight_totals(
        normed, grads, context, grad_attended, small, (w_query, w_key, w_value), tokens,
        grad_hidden1, attn_gain[None],
    )
    parts, start = [], 0
    for count in counts:
        parts.append(small[start : start + count])
        start += count
    router_part, tab_part, ffn_part = parts
    attn_part = small[63 * UNIT : 63 * UNIT + model_width // LANES]
    experts = router.shape[1]
    return (
        mixed,
        grad_input,
        attn_part.reshape(-1),
        grad_query,
        grad_key,
        grad_value,
        grad_proj,
        tab_part[:, :heads],
        ffn_part.reshape(-1),
        jnp.concatenate([router_part[:, :experts], router_part[:, experts:]], axis=0),
        grad_expert_in[None],
        grad_expert_out[None],
    )


def solution(mesh):
    return jax.shard_map(
        shards,
        mesh=mesh,
        in_specs=(
            P("ctx", None),
            P(),
            P(None, "mp"),
            P(None, "mp"),
            P(None, "mp"),
            P("mp", None),
            P(None, "mp"),
            P(),
            P(),
            P(),
            P("ctx", None, "mp"),
            P("ctx", "mp", None),
            P("ctx"),
            P("ctx"),
            P("ctx", None),
        ),
        out_specs=(
            P("ctx", None),
            P("ctx", None),
            P(),
            P(None, "mp"),
            P(None, "mp"),
            P(None, "mp"),
            P("mp", None),
            P(None, "mp"),
            P(),
            P(),
            P("ctx", None, "mp"),
            P("ctx", "mp", None),
        ),
        check_vma=False,
    )
```

```python
import functools
import jax
import jax.numpy as jnp
from jax import lax
from jax.experimental import pallas as pl
from jax.experimental.pallas import tpu as pltpu
from jax.sharding import PartitionSpec as P

HEAD = 64
GROUP = 3
BLOCK = 128
PAIR = 2 * BLOCK
FORWARD_SPAN = 8
BACKWARD_SPAN = 4
VMEM = pl.BlockSpec(memory_space=pltpu.VMEM)
SMEM = pl.BlockSpec(memory_space=pltpu.SMEM)
LARGE = pltpu.CompilerParams(vmem_limit_bytes=60 * 1024 * 1024)


def contract(left, right, left_dim, right_dim):
    return lax.dot_general(
        left,
        right,
        (((left_dim,), (right_dim,)), ((), ())),
        preferred_element_type=jnp.float32,
    )


def window_row(place, chunk, tile, half, span):
    return 63 - (span * chunk + tile // 2) + place + BLOCK // 4 * (half - tile % 2)


def tile_consts(table_ref, head, place, chunk, tile, span):
    parts = []
    for half in range(2):
        row = window_row(place, chunk, tile, half, span)
        parts.append(jnp.broadcast_to(table_ref[head, pl.ds(row, 1), 0:1], (1, BLOCK)))
    return jnp.concatenate(parts, axis=1)


def chunk_mixed(uneven_ref, place, chunk, span):
    mixed = 0
    for tile in range(2 * span):
        for half in range(2):
            mixed = mixed + uneven_ref[0, window_row(place, chunk, tile, half, span)]
    return mixed


def add_uneven(table_ref, uneven_ref, score_ref, place, chunk, span):
    for tile in range(2 * span):
        for half in range(2):
            row = window_row(place, chunk, tile, half, span)

            @pl.when(uneven_ref[0, row] > 0)
            def _():
                for head in range(GROUP):
                    window = jnp.concatenate(
                        [table_ref[head, pl.ds(row, 1), :], table_ref[head, pl.ds(row + 1, 1), :]],
                        axis=1,
                    )
                    window = window - window[:, 0:1]
                    grid = pltpu.roll(
                        jnp.broadcast_to(window, (BLOCK, PAIR)),
                        BLOCK,
                        1,
                        stride=1,
                        stride_axis=0,
                    )[:, :BLOCK]
                    rows = slice(tile * BLOCK, (tile + 1) * BLOCK)
                    cols = slice(half * BLOCK, (half + 1) * BLOCK)
                    score_ref[head, rows, cols] += grid


def stream(keys_hbm, held_ref, sems, span):
    def copy(chunk):
        slot = lax.rem(chunk, 2)
        return pltpu.make_async_copy(
            keys_hbm.at[pl.ds(chunk * span, span)], held_ref.at[slot], sems.at[slot]
        )

    return copy


def head_columns(ref, head):
    return ref[:, head * HEAD : (head + 1) * HEAD]


def turn(values):
    return values.astype(jnp.float32).T


def fill_turned(dst_ref, src_ref, first):
    for head in range(GROUP):
        part = turn(head_columns(src_ref, head))
        none = jnp.zeros_like(part)
        parts = [part, none] if first else [none, part]
        dst_ref[head] = jnp.concatenate(parts, axis=0).astype(dst_ref.dtype)


def fill_padded(dst_ref, src_ref, first):
    for head in range(GROUP):
        part = head_columns(src_ref, head)
        none = jnp.zeros_like(part)
        parts = [part, none] if first else [none, part]
        dst_ref[head] = jnp.concatenate(parts, axis=1)


def side_by_side(parts):
    return jnp.concatenate([turn(part) for part in parts], axis=1).astype(jnp.bfloat16)


def flip_both(values):
    down = lax.broadcasted_iota(jnp.int32, (BLOCK, BLOCK), 0)
    right = lax.broadcasted_iota(jnp.int32, (BLOCK, BLOCK), 1)
    anti = jnp.where(down + right == BLOCK - 1, 1.0, 0.0).astype(jnp.bfloat16)
    once = contract(anti, values.astype(jnp.float32).astype(jnp.bfloat16), 1, 0)
    return contract(once.astype(jnp.bfloat16), anti, 1, 0).astype(jnp.int32)


def line_of(column):
    down = lax.broadcasted_iota(jnp.int32, (BLOCK, BLOCK), 0)
    right = lax.broadcasted_iota(jnp.int32, (BLOCK, BLOCK), 1)
    return jnp.sum(jnp.where(down == right, column, 0.0), axis=0, keepdims=True)


def shifted_up(column):
    return jnp.concatenate([column[1:], column[-1:]], axis=0)


def forward_kernel(
    place_ref, rel_ref, buckets_ref, keys_hbm, rows_ref,
    out_ref, turned_ref, lse_ref, flipped_ref, table_ref, uneven_out_ref,
    held_ref, held_sem, uneven_ref, uneven_sem,
    query_ref, best_ref, sum_ref, total_ref, score_ref,
):
    place = place_ref[0]
    span = FORWARD_SPAN
    tiles, length = 2 * span, PAIR * span
    fetch = stream(keys_hbm, held_ref, held_sem, span)
    chunks = keys_hbm.shape[0] // span
    fetch(0).start()
    flipped = flip_both(buckets_ref[...])
    flipped_ref[...] = flipped
    floats = flipped.astype(jnp.float32)
    high = jnp.max(floats, axis=1, keepdims=True)
    low = jnp.min(floats, axis=1, keepdims=True)
    high = jnp.maximum(high, shifted_up(high))
    low = jnp.minimum(low, shifted_up(low))
    uneven_out_ref[...] = line_of(jnp.where(high > low, 1.0, 0.0)).astype(jnp.int32)
    flags = pltpu.make_async_copy(uneven_out_ref, uneven_ref, uneven_sem)
    flags.start()
    for head in range(GROUP):
        values = jnp.zeros((BLOCK, BLOCK), jnp.float32)
        for bucket in range(rel_ref.shape[0]):
            value = rel_ref[bucket, place_ref[1] * GROUP + head]
            values = jnp.where(flipped == bucket, value, values)
        table_ref[head] = values
    fill_turned(query_ref, rows_ref, True)
    flags.wait()
    best_ref[...] = jnp.full_like(best_ref, -1e30)
    sum_ref[...] = jnp.zeros_like(sum_ref)
    total_ref[...] = jnp.zeros_like(total_ref)

    def rest(chunk, head, held, scores):
        consts = [tile_consts(table_ref, head, place, chunk, tile, span) for tile in range(tiles)]
        old = best_ref[head]
        new = old
        for tile in range(tiles):
            part = scores[tile * BLOCK : (tile + 1) * BLOCK]
            new = jnp.maximum(new, jnp.max(part, axis=0, keepdims=True) + consts[tile])
        decay = jnp.exp(old - new)
        weights = [
            jnp.exp(scores[tile * BLOCK : (tile + 1) * BLOCK] - (new - consts[tile]))
            for tile in range(tiles)
        ]
        weights = jnp.concatenate(weights, axis=0)
        sum_ref[head] = sum_ref[head] * decay + jnp.sum(weights, axis=0, keepdims=True)
        best_ref[head] = new
        total_ref[head] = total_ref[head] * decay + contract(
            held, weights.astype(jnp.bfloat16), 0, 0
        )

    @pl.loop(0, chunks)
    def _(chunk):
        slot = lax.rem(chunk, 2)
        fetch(chunk).wait()

        @pl.when(chunk + 1 < chunks)
        def _():
            fetch(chunk + 1).start()

        def held_of(head):
            return held_ref[slot, :, head].reshape(length, 2 * HEAD)

        mixed = chunk_mixed(uneven_ref, place, chunk, span)

        @pl.when(mixed == 0)
        def _():
            helds = [held_of(head) for head in range(GROUP)]
            scores = [contract(helds[head], query_ref[head], 1, 0) for head in range(GROUP)]
            for head in range(GROUP):
                rest(chunk, head, helds[head], scores[head])

        @pl.when(mixed > 0)
        def _():
            for head in range(GROUP):
                score_ref[head] = contract(held_of(head), query_ref[head], 1, 0)
            add_uneven(table_ref, uneven_ref, score_ref, place, chunk, span)
            for head in range(GROUP):
                rest(chunk, head, held_of(head), score_ref[head])

    for head in range(GROUP):
        turned_ref[head] = total_ref[head][HEAD:] / sum_ref[head]
    out_ref[...] = side_by_side([turned_ref[head] for head in range(GROUP)])
    for head in range(GROUP):
        lse_ref[head] = best_ref[head] + jnp.log(sum_ref[head])


def backward_kernel(
    place_ref, uneven_ref, table_ref, keys_hbm, rows_ref, grads_ref, turned_ref, lse_ref,
    flipped_ref, rows_in_ref, rows_grad_ref, activ_ref, grad_pre_ref,
    grad_keys_hbm, grad_rows_ref, slab_ref, expert_in_hbm, expert_out_hbm,
    held_ref, held_sem, grad_keys_ref, grad_keys_sem, expert_in, expert_out, expert_sem, offsets_ref, query_t_ref, grad_t_ref, query_ref, grad_ref, delta_ref, grad_query_ref, score_ref,
):
    place = place_ref[0]
    span = BACKWARD_SPAN
    tiles, length = 2 * span, PAIR * span
    fetch = stream(keys_hbm, held_ref, held_sem, span)
    chunks = keys_hbm.shape[0] // span
    fetch(0).start()

    def give(chunk):
        slot = lax.rem(chunk, 2)
        return pltpu.make_async_copy(
            grad_keys_ref.at[slot],
            grad_keys_hbm.at[pl.ds(chunk * span, span)],
            grad_keys_sem.at[slot],
        )

    expert_in[...] = contract(rows_in_ref[...], grad_pre_ref[...], 0, 0)
    expert_out[...] = contract(activ_ref[...], rows_grad_ref[...], 0, 0)
    stores = [
        pltpu.make_async_copy(expert_in, expert_in_hbm, expert_sem.at[0]),
        pltpu.make_async_copy(expert_out, expert_out_hbm, expert_sem.at[1]),
    ]
    for store in stores:
        store.start()
    fill_turned(query_t_ref, rows_ref, True)
    fill_turned(grad_t_ref, grads_ref, False)
    fill_padded(query_ref, rows_ref, True)
    fill_padded(grad_ref, grads_ref, False)
    for head in range(GROUP):
        delta_ref[head] = jnp.sum(
            grad_t_ref[head][HEAD:].astype(jnp.float32) * turned_ref[head], axis=0, keepdims=True
        )
    grad_query_ref[...] = jnp.zeros_like(grad_query_ref)
    offsets_ref[...] = jnp.zeros_like(offsets_ref)

    def rest(chunk, head, held, scores, grads):
        probs = jnp.concatenate(
            [
                jnp.exp(
                    scores[tile * BLOCK : (tile + 1) * BLOCK]
                    - (lse_ref[head] - tile_consts(table_ref, head, place, chunk, tile, span))
                )
                for tile in range(tiles)
            ],
            axis=0,
        )
        slopes = probs * (grads - delta_ref[head])
        rounded = slopes.astype(jnp.bfloat16)
        part = contract(rounded, query_ref[head], 1, 0) + contract(
            probs.astype(jnp.bfloat16), grad_ref[head], 1, 0
        )
        grad_keys_ref[lax.rem(chunk, 2), :, head] = part.astype(grad_keys_ref.dtype).reshape(
            span, PAIR, 2 * HEAD
        )
        grad_query_ref[head] += contract(held, rounded, 0, 0)
        return slopes

    def put_even(chunk, head, tile, half, slopes):
        row = window_row(place, chunk, tile, half, span)
        offsets_ref[head, pl.ds(row, 1), :] += jnp.sum(slopes, axis=0, keepdims=True)

    def put_uneven(chunk, head, tile, half, slopes):
        row = window_row(place, chunk, tile, half, span)
        wide = jnp.concatenate([slopes, jnp.zeros_like(slopes)], axis=1)
        folded = jnp.zeros((8, PAIR), jnp.float32)
        for group in range(BLOCK // 8):
            folded = folded + pltpu.roll(
                wide[group * 8 : (group + 1) * 8], (BLOCK - 8 * group) % PAIR, 1
            )
        line = jnp.zeros((1, PAIR), jnp.float32)
        for step in range(8):
            line = line + pltpu.roll(folded, (PAIR - step) % PAIR, 1)[step : step + 1]
        offsets_ref[head, pl.ds(row, 1), :] += line[:, :BLOCK]
        offsets_ref[head, pl.ds(row + 1, 1), :] += line[:, BLOCK:]

    @pl.loop(0, chunks)
    def _(chunk):
        slot = lax.rem(chunk, 2)
        fetch(chunk).wait()

        @pl.when(chunk + 1 < chunks)
        def _():
            fetch(chunk + 1).start()

        def held_of(head):
            return held_ref[slot, :, head].reshape(length, 2 * HEAD)

        @pl.when(chunk >= 2)
        def _():
            give(chunk - 2).wait()

        mixed = chunk_mixed(uneven_ref, place, chunk, span)

        @pl.when(mixed == 0)
        def _():
            helds = [held_of(head) for head in range(GROUP)]
            scores = [contract(helds[head], query_t_ref[head], 1, 0) for head in range(GROUP)]
            grads = [contract(helds[head], grad_t_ref[head], 1, 0) for head in range(GROUP)]
            for head in range(GROUP):
                slopes = rest(chunk, head, helds[head], scores[head], grads[head])
                for tile in range(tiles):
                    for half in range(2):
                        part = slopes[
                            tile * BLOCK : (tile + 1) * BLOCK, half * BLOCK : (half + 1) * BLOCK
                        ]
                        put_even(chunk, head, tile, half, part)

        @pl.when(mixed > 0)
        def _():
            for head in range(GROUP):
                score_ref[head] = contract(held_of(head), query_t_ref[head], 1, 0)
            add_uneven(table_ref, uneven_ref, score_ref, place, chunk, span)
            for head in range(GROUP):
                held = held_of(head)
                grads = contract(held, grad_t_ref[head], 1, 0)
                score_ref[head] = rest(chunk, head, held, score_ref[head], grads)
            for tile in range(tiles):
                for half in range(2):
                    rows = slice(tile * BLOCK, (tile + 1) * BLOCK)
                    cols = slice(half * BLOCK, (half + 1) * BLOCK)
                    uneven = uneven_ref[0, window_row(place, chunk, tile, half, span)]

                    @pl.when(uneven == 0)
                    def _():
                        for head in range(GROUP):
                            put_even(chunk, head, tile, half, score_ref[head, rows, cols])

                    @pl.when(uneven > 0)
                    def _():
                        for head in range(GROUP):
                            put_uneven(chunk, head, tile, half, score_ref[head, rows, cols])

        give(chunk).start()

    for chunk in (chunks - 2, chunks - 1):
        give(chunk).wait()
    grad_rows_ref[...] = side_by_side([grad_query_ref[head][:HEAD] for head in range(GROUP)])
    lanes = lax.broadcasted_iota(jnp.int32, (1, BLOCK), 1)
    for bucket in range(slab_ref.shape[0]):
        hit = flipped_ref[...] == bucket
        line = jnp.zeros((1, BLOCK), jnp.float32)
        for head in range(GROUP):
            part = jnp.sum(jnp.where(hit, offsets_ref[head], 0.0), axis=0, keepdims=True)
            part = jnp.sum(part, axis=1, keepdims=True)
            line = jnp.where(lanes == place_ref[1] * GROUP + head, part, line)
        slab_ref[pl.ds(bucket, 1)] = line
    for store in stores:
        store.wait()


def attend(place, rel_table, buckets, keys, rows):
    shape = jax.ShapeDtypeStruct
    anywhere = pl.BlockSpec(memory_space=pl.ANY)
    return pl.pallas_call(
        forward_kernel,
        out_shape=(
            shape(rows.shape, jnp.bfloat16),
            shape((GROUP, HEAD, PAIR), jnp.float32),
            shape((GROUP, 1, PAIR), jnp.float32),
            shape((BLOCK, BLOCK), jnp.int32),
            shape((GROUP, BLOCK, BLOCK), jnp.float32),
            shape((1, BLOCK), jnp.int32),
        ),
        in_specs=[SMEM, SMEM, VMEM, anywhere, VMEM],
        out_specs=(VMEM,) * 6,
        scratch_shapes=[
            pltpu.VMEM((2, FORWARD_SPAN) + keys.shape[1:], keys.dtype),
            pltpu.SemaphoreType.DMA((2,)),
            pltpu.SMEM((1, BLOCK), jnp.int32),
            pltpu.SemaphoreType.DMA,
            pltpu.VMEM((GROUP, 2 * HEAD, PAIR), jnp.bfloat16),
            pltpu.VMEM((GROUP, 1, PAIR), jnp.float32),
            pltpu.VMEM((GROUP, 1, PAIR), jnp.float32),
            pltpu.VMEM((GROUP, 2 * HEAD, PAIR), jnp.float32),
            pltpu.VMEM((GROUP, FORWARD_SPAN * PAIR, PAIR), jnp.float32),
        ],
        compiler_params=LARGE,
        name="attend",
    )(place, rel_table, buckets, keys, rows)


def attend_back(
    place, uneven, table, keys, rows, grads, turned, lse, flipped, rows_in, rows_grad, activ,
    grad_pre, buckets,
):
    shape = jax.ShapeDtypeStruct
    wide_row, hidden = rows_in.shape[1], activ.shape[1]
    anywhere = pl.BlockSpec(memory_space=pl.ANY)
    return pl.pallas_call(
        backward_kernel,
        out_shape=(
            shape(keys.shape, jnp.bfloat16),
            shape(rows.shape, jnp.bfloat16),
            shape((buckets, BLOCK), jnp.float32),
            shape((wide_row, hidden), jnp.float32),
            shape((hidden, wide_row), jnp.float32),
        ),
        in_specs=[SMEM, SMEM, VMEM, anywhere] + [VMEM] * 9,
        out_specs=(anywhere, VMEM, VMEM, anywhere, anywhere),
        scratch_shapes=[
            pltpu.VMEM((2, BACKWARD_SPAN) + keys.shape[1:], keys.dtype),
            pltpu.SemaphoreType.DMA((2,)),
            pltpu.VMEM((2, BACKWARD_SPAN) + keys.shape[1:], keys.dtype),
            pltpu.SemaphoreType.DMA((2,)),
            pltpu.VMEM((wide_row, hidden), jnp.float32),
            pltpu.VMEM((hidden, wide_row), jnp.float32),
            pltpu.SemaphoreType.DMA((2,)),
            pltpu.VMEM((GROUP, BLOCK, BLOCK), jnp.float32),
            pltpu.VMEM((GROUP, 2 * HEAD, PAIR), jnp.bfloat16),
            pltpu.VMEM((GROUP, 2 * HEAD, PAIR), jnp.bfloat16),
            pltpu.VMEM((GROUP, PAIR, 2 * HEAD), jnp.bfloat16),
            pltpu.VMEM((GROUP, PAIR, 2 * HEAD), jnp.bfloat16),
            pltpu.VMEM((GROUP, 1, PAIR), jnp.float32),
            pltpu.VMEM((GROUP, 2 * HEAD, PAIR), jnp.float32),
            pltpu.VMEM((GROUP, BACKWARD_SPAN * PAIR, PAIR), jnp.float32),
        ],
        compiler_params=LARGE,
        name="attend_back",
    )(
        place, uneven, table, keys, rows, grads, turned, lse, flipped, rows_in, rows_grad, activ,
        grad_pre,
    )


EPSILON = 1e-06
PRECISE = lax.Precision.HIGHEST
ANYWHERE = pl.BlockSpec(memory_space=pl.ANY)
SIDE = 4


class Place:
    def __init__(self):
        self.me = lax.axis_index("ctx")
        self.core = lax.rem(self.me, 2)
        self.z = lax.rem(self.me // 2, SIDE)
        self.x = lax.rem(self.me // (2 * SIDE), SIDE)
        self.y = self.me // (2 * SIDE * SIDE)

    def at(self, dx=0, dz=0, dcore=0, dy=0):
        x = lax.rem(self.x + dx, SIDE)
        z = lax.rem(self.z + dz, SIDE)
        core = lax.rem(self.core + dcore, 2)
        y = lax.rem(self.y + dy, 2)
        return ((y * SIDE + x) * SIDE + z) * 2 + core

    def turned(self, axis, step):
        return self.at(dx=step) if axis == 0 else self.at(dz=step)

    def along(self, axis, step):
        return lax.rem((self.x if axis == 0 else self.z) + step, SIDE)


def greet(targets, across=False):
    barrier = pltpu.get_barrier_semaphore()
    if across:
        pl.semaphore_signal(
            barrier,
            inc=1,
            device_id={"mp": 1 - lax.axis_index("mp")},
            device_id_type=pl.DeviceIdType.MESH,
        )
    for target in targets:
        pl.semaphore_signal(
            barrier, inc=1, device_id={"ctx": target}, device_id_type=pl.DeviceIdType.MESH
        )
    return barrier, len(targets) + int(across)


def meet(targets, across=False):
    pl.semaphore_wait(*greet(targets, across))


def ring_targets(place):
    found = [place.at(dcore=1)]
    for step in range(1, SIDE):
        found += [place.at(dx=step), place.at(dz=step)]
    return found


def sender(target, src, dst, send_sem, recv_sem):
    return pltpu.make_async_remote_copy(
        src_ref=src,
        dst_ref=dst,
        send_sem=send_sem,
        recv_sem=recv_sem,
        device_id={"ctx": target},
        device_id_type=pl.DeviceIdType.MESH,
    )


def wide(value):
    return value.astype(jnp.float32)


class Sends:
    def __init__(self, place, sems):
        self.place, self.sems, self.started = place, sems, []

    def go(self, target, src, dst, recv_sem):
        copy = sender(target, src, dst, self.sems.at[len(self.started)], recv_sem)
        copy.start()
        self.started.append(copy)
        return copy

    def across(self, src, dst, recv_sem):
        copy = pltpu.make_async_remote_copy(
            src_ref=src,
            dst_ref=dst,
            send_sem=self.sems.at[len(self.started)],
            recv_sem=recv_sem,
            device_id={"mp": 1 - lax.axis_index("mp")},
            device_id_type=pl.DeviceIdType.MESH,
        )
        copy.start()
        self.started.append(copy)

    def landed(self, view, sem):
        sender(self.place.me, view, view, sem, sem).wait_recv()

    def finish(self):
        for copy in self.started:
            copy.wait_send()


def gather_kernel(
    tokens_ref, gain_ref, w_query_ref, w_key_ref, w_value_ref,
    normed_ref, rows_ref, out_ref,
    block_ref, given, other, local_sem, send_sem, ring_recv, twin_recv, swap_recv,
):
    place = Place()
    barrier = greet(ring_targets(place) + [place.at(dy=1)])
    sends = Sends(place, send_sem)
    half_rows = block_ref.shape[1] // 2
    sub_rows = half_rows // 2
    first = place.y == 0
    width = GROUP * HEAD
    floats_in = wide(tokens_ref[...])
    scale = lax.rsqrt(jnp.mean(floats_in * floats_in, axis=1, keepdims=True) + EPSILON)
    normed = (floats_in * scale * gain_ref[...][None]).astype(normed_ref.dtype)
    normed_ref[...] = normed
    kept = []
    for n, ref in enumerate((w_query_ref, w_key_ref, w_value_ref)):
        made = contract(normed, ref[...], 1, 0).astype(given.dtype)
        kept.append(jnp.where(first, made[:, :width], made[:, width:]))
        given[n] = jnp.where(first, made[:, width:], made[:, :width])

    def rows_at(half, start=0, count=half_rows):
        side = place.y if half == 0 else 1 - place.y
        return pl.ds(pl.multiple_of(side * half_rows + start, sub_rows), count)

    def put(half, query, key, value):
        rows_ref[rows_at(half)] = query
        for head in range(GROUP):
            lanes = slice(head * HEAD, (head + 1) * HEAD)
            block_ref[head, rows_at(half)] = jnp.concatenate(
                [key[:, lanes], value[:, lanes]], axis=1
            )

    put(0, *kept)
    pl.semaphore_wait(*barrier)
    sends.go(place.at(dy=1), given, other, swap_recv)

    def rows_of(half, piece):
        if piece is None:
            return rows_at(half)
        return rows_at(half, piece * sub_rows, sub_rows)

    def view(half, first, second, core, piece=None):
        x, z = (second, first) if half == 0 else (first, second)
        slot = (place.along(0, x) * SIDE + place.along(1, z)) * 2 + core
        return out_ref.at[slot, :, rows_of(half, piece)]

    def held(half, first, second, piece=None):
        if first == 0 and second == 0:
            return block_ref.at[:, rows_of(half, piece)]
        return view(half, first, second, place.core, piece)

    def shift(half, first, second, stage, step, piece=None):
        axis = 1 - half if stage == 0 else half
        if stage == 0:
            slot = ((first - step) % SIDE, second)
        else:
            slot = (first, (second - step) % SIDE)
        sends.go(
            place.turned(axis, step % SIDE),
            held(half, first, second, piece),
            view(half, first, second, place.core, piece),
            ring_recv.at[half, slot[0], slot[1], piece or 0],
        )

    def to_twin(half, first, second):
        sends.go(
            place.at(dcore=1),
            held(half, first, second),
            view(half, first, second, place.core),
            twin_recv.at[half, first, second],
        )

    def wait(half, first, second):
        if second == 2:
            for piece in range(2):
                sends.landed(
                    view(half, first, second, place.core, piece),
                    ring_recv.at[half, first, second, piece],
                )
        else:
            sends.landed(
                view(half, first, second, place.core), ring_recv.at[half, first, second, 0]
            )

    def relay(half, first, second):
        if second == SIDE - 1:
            shift(half, first, second, 1, 1, 0)
        elif second == 1:
            shift(half, first, second, 1, -1, 1)

    for half in range(2):
        if half == 1:
            sends.landed(other, swap_recv)
            put(1, other[0], other[1], other[2])
        for stage in range(2):
            for step in (1, -1, 2)[: 3 - stage]:
                shift(half, 0, 0, stage, step)
        to_twin(half, 0, 0)
    own = pltpu.make_async_copy(
        block_ref, out_ref.at[(place.x * SIDE + place.z) * 2 + place.core], local_sem
    )
    own.start()
    order = [(3, 0), (1, 0), (0, 3), (0, 1), (2, 0), (3, 3), (3, 1), (1, 3), (1, 1), (0, 2)]
    order += [(3, 2), (1, 2), (2, 3), (2, 1), (2, 2)]
    for first, second in order:
        for half in range(2):
            wait(half, first, second)
            if second == 0:
                for step in (1, -1):
                    shift(half, first, second, 1, step)
            else:
                relay(half, first, second)
            to_twin(half, first, second)
    for first, second in [(0, 0)] + order:
        for half in range(2):
            sends.landed(
                view(half, first, second, 1 - place.core), twin_recv.at[half, first, second]
            )
    own.wait()
    sends.finish()


def gather_plane(tokens, gain, w_query, w_key, w_value):
    kind = tokens.dtype
    tok_rows = tokens.shape[0]
    width = GROUP * HEAD
    block = (GROUP, 2 * tok_rows, 2 * HEAD)
    shape = jax.ShapeDtypeStruct
    sem = pltpu.SemaphoreType.DMA
    return pl.pallas_call(
        gather_kernel,
        out_shape=(
            shape(tokens.shape, kind),
            shape((2 * tok_rows, width), kind),
            shape((2 * SIDE * SIDE,) + block, kind),
        ),
        in_specs=[VMEM] * 5,
        out_specs=(VMEM, VMEM, ANYWHERE),
        scratch_shapes=[
            pltpu.VMEM(block, kind),
            pltpu.VMEM((3, tok_rows, width), kind),
            pltpu.VMEM((3, tok_rows, width), kind),
            sem, sem((73,)), sem((2, SIDE, SIDE, 2)), sem((2, SIDE, SIDE)), sem,
        ],
        compiler_params=pltpu.CompilerParams(
            collective_id=1, has_side_effects=True, vmem_limit_bytes=60 * 1024 * 1024
        ),
        name="gather_plane",
    )(tokens, gain, w_query, w_key, w_value)


def ring_sum(sends, axis_of, sums, via, landing, via_recv, land_recv, ready):
    place = sends.place
    rows = sums.shape[-2] // 2
    middle = (slice(None),) * (len(sums.shape) - 4)

    def cut(ref, index, piece):
        return ref.at[index + middle + (pl.ds(piece * rows, rows),)]

    for half in range(2):
        ready(half, 2)
        for piece, step in ((0, 1), (1, SIDE - 1)):
            sends.go(
                place.turned(axis_of(half), step),
                cut(sums, (half, 2), piece),
                via.at[half, piece],
                via_recv.at[half, piece],
            )
    for half in range(2):
        for piece, step in ((0, 1), (1, SIDE - 1)):
            ready(half, step)
            sends.go(
                place.turned(axis_of(half), step),
                cut(sums, (half, step), 1 - piece),
                cut(landing, (half, piece), 1 - piece),
                land_recv.at[half, piece, 1 - piece],
            )
    for half in range(2):
        ready(half, 0)
    for half in range(2):
        for piece, step in ((0, 1), (1, SIDE - 1)):
            sends.landed(via.at[half, piece], via_recv.at[half, piece])
            spot = (half, step) + middle + (slice(piece * rows, (piece + 1) * rows),)
            sums[spot] = (wide(sums[spot]) + wide(via[half, piece])).astype(sums.dtype)
            sends.go(
                place.turned(axis_of(half), step),
                cut(sums, (half, step), piece),
                cut(landing, (half, piece), piece),
                land_recv.at[half, piece, piece],
            )

    def finish(half):
        for piece in range(2):
            for part in (1 - piece, piece):
                sends.landed(cut(landing, (half, piece), part), land_recv.at[half, piece, part])

    return finish


def ring_sum_direct(sends, axis_of, sums, landing, land_recv, ready):
    for step in (2, 1, 3):
        for half in range(2):
            ready(half, step)
            sends.go(
                sends.place.turned(axis_of(half), step),
                sums.at[half, step],
                landing.at[half, step - 1],
                land_recv.at[half, step - 1],
            )
    for half in range(2):
        ready(half, 0)

    def finish(half):
        for step in range(1, SIDE):
            sends.landed(landing.at[half, step - 1], land_recv.at[half, step - 1])

    return finish


def scatter_kernel(
    parts_ref, rows_ref, out_ref, mine, twin, sums, via_one, land_one, halves, land_two,
    both, other,
    local_sem, send_sem, twin_recv, via_one_recv, land_one_recv, land_two_recv,
    far_recv,
):
    place = Place()
    half_rows = parts_ref.shape[4] // 2

    def source(half, group, core):
        rows = pl.ds(half * half_rows, half_rows)
        if half == 0:
            return parts_ref.at[group, :, core, :, rows]
        return parts_ref.at[:, group, core, :, rows]

    barrier = greet(ring_targets(place) + [place.at(dy=1)])
    loads = {}
    order = (2, 1, 3, 0)
    for step in order:
        for half in range(2):
            loads[half, step] = pltpu.make_async_copy(
                source(half, place.along(half, step), place.core),
                mine.at[half, step],
                local_sem.at[half, step],
            )
            loads[half, step].start()
    pl.semaphore_wait(*barrier)
    sends = Sends(place, send_sem)
    for step in order:
        for half in range(2):
            sends.go(
                place.at(dcore=1),
                source(half, place.along(half, step), 1 - place.core),
                twin.at[half, step],
                twin_recv.at[half, step],
            )

    def ready_one(half, step):
        loads[half, step].wait()
        sends.landed(twin.at[half, step], twin_recv.at[half, step])
        sums[half, step] = (wide(mine[half, step]) + wide(twin[half, step])).astype(sums.dtype)

    done_one = ring_sum(
        sends, lambda half: half, sums, via_one, land_one, via_one_recv, land_one_recv, ready_one
    )
    arrived = set()

    def ready_two(half, step):
        if half not in arrived:
            arrived.add(half)
            done_one(half)
        spot = place.along(1 - half, step)
        total = wide(sums[half, 0, spot])
        for side in range(2):
            total = total + wide(land_one[half, side, spot])
        halves[half, step] = total.astype(halves.dtype)

    done_two = ring_sum_direct(
        sends, lambda half: 1 - half, halves, land_two, land_two_recv, ready_two
    )
    for half in range(2):
        done_two(half)
        total = wide(halves[half, 0])
        for side in range(SIDE - 1):
            total = total + wide(land_two[half, side])
        total = total.astype(both.dtype)
        parts = [rows_ref[half * half_rows : (half + 1) * half_rows]]
        parts += [total[head, :, :HEAD] for head in range(GROUP)]
        parts += [total[head, :, HEAD:] for head in range(GROUP)]
        both[half] = jnp.concatenate(parts, axis=1)
    sends.go(place.at(dy=1), both.at[1 - place.y], other, far_recv)
    width = GROUP * HEAD
    kept = both[place.y]
    sends.landed(other, far_recv)
    received = other[...]
    low = jnp.where(place.y == 0, kept, received)
    high = jnp.where(place.y == 0, received, kept)
    parts = []
    for n in range(3):
        parts += [low[:, n * width : (n + 1) * width], high[:, n * width : (n + 1) * width]]
    out_ref[...] = jnp.concatenate(parts, axis=1)
    sends.finish()


def scatter_plane(parts, rows_grad):
    heads, rows, lanes = parts.shape[1:]
    piece = (heads, rows // 2, lanes)
    small = (heads, rows // 4, lanes)
    kind = parts.dtype
    sem = pltpu.SemaphoreType.DMA
    return pl.pallas_call(
        scatter_kernel,
        out_shape=jax.ShapeDtypeStruct((rows // 2, 6 * rows_grad.shape[1]), kind),
        in_specs=[ANYWHERE, VMEM],
        out_specs=pl.BlockSpec(memory_space=pltpu.VMEM),
        scratch_shapes=[
            pltpu.VMEM((2, SIDE, SIDE) + piece, kind),
            pltpu.VMEM((2, SIDE, SIDE) + piece, kind),
            pltpu.VMEM((2, SIDE, SIDE) + piece, kind),
            pltpu.VMEM((2, 2, SIDE) + small, kind),
            pltpu.VMEM((2, 2, SIDE) + piece, kind),
            pltpu.VMEM((2, SIDE) + piece, kind),
            pltpu.VMEM((2, SIDE - 1) + piece, kind),
            pltpu.VMEM((2, rows // 2, 3 * rows_grad.shape[1]), kind),
            pltpu.VMEM((rows // 2, 3 * rows_grad.shape[1]), kind),
            sem((2, SIDE)), sem((33,)), sem((2, SIDE)),
            sem((2, 2)), sem((2, 2, 2)), sem((2, SIDE - 1)), sem,
        ],
        compiler_params=pltpu.CompilerParams(
            collective_id=2, has_side_effects=True, vmem_limit_bytes=60 * 1024 * 1024
        ),
        name="scatter_plane",
    )(parts.reshape((SIDE, SIDE, 2) + parts.shape[1:]), rows_grad)


LANES = 128
UNIT = 16
UNITS = 9
BLOCK_ROWS = UNIT * (UNITS + 1)


def runs(slab_rows):
    found, unit = [], 0
    for slab, rows in enumerate(slab_rows):
        row = 0
        while row < rows:
            block, inside = divmod(unit, UNITS)
            take = min(UNITS - inside, (rows - row) // UNIT)
            found.append((slab, row, block, inside * UNIT, take * UNIT))
            row += take * UNIT
            unit += take
    return found


def block_at(block):
    return block // 32, block // 16 % 2, block // 4 % 4, block % 4


def weights_kernel(
    normed_ref, grads_ref, context_ref, attended_ref, router_ref, slab_ref, ffn_ref, w_query_ref,
    w_key_ref, w_value_ref, tokens_ref, hidden_ref, gain_ref,
    full, input_ref,
    share, share_other, parts, twin, sums, via_one, land_one, halves, land_two, other,
    send_sem, twin_recv, via_one_recv, land_one_recv, land_two_recv,
    far_recv, far_back_recv, two_back_recv, one_back_recv, twin_back_recv, share_recv,
):
    place = Place()
    width = context_ref.shape[1]
    barrier = greet(ring_targets(place) + [place.at(dy=1)], True)
    sends = Sends(place, send_sem)
    partial = jnp.zeros(share.shape, jnp.float32)
    for n, ref in enumerate((w_query_ref, w_key_ref, w_value_ref)):
        partial = partial + contract(grads_ref[:, n * width : (n + 1) * width], ref[...], 1, 1)
    share[...] = partial.astype(share.dtype)
    pl.semaphore_wait(*barrier)
    sends.across(share, share_other, share_recv)
    slabs, table = slab_table(normed_ref.shape[1], width)
    operands = ((normed_ref, grads_ref), (context_ref, attended_ref))
    for index, (output, lane) in enumerate(slabs):
        left, right = operands[output // 3]
        lane = lane if output == 3 else output * width + lane
        grad = contract(left[...], right[:, lane : lane + LANES], 0, 0).astype(parts.dtype)
        for slab, row, block, inside, rows in table:
            if slab == index:
                parts[block_at(block) + (slice(inside, inside + rows),)] = grad[row : row + rows]
    sends.landed(share_other, share_recv)
    grad_normed = wide(share[...]) + wide(share_other[...])
    floats_in = wide(tokens_ref[...])
    scale = lax.rsqrt(jnp.mean(floats_in * floats_in, axis=1, keepdims=True) + EPSILON)
    scaled = gain_ref[...][None] * grad_normed
    input_ref[...] = (
        hidden_ref[...]
        + scale * scaled
        - floats_in * scale**3 * jnp.mean(scaled * floats_in, axis=1, keepdims=True)
    )
    gain_sum = jnp.sum(grad_normed * floats_in * scale, axis=0, keepdims=True)
    tall = router_ref.shape[0] // 2
    router = jnp.concatenate([router_ref[:tall], router_ref[tall:]], axis=1)
    lines = [
        line[:, n : n + LANES]
        for line in (gain_sum, ffn_ref[...])
        for n in range(0, gain_sum.shape[1], LANES)
    ]
    lines.append(jnp.zeros((UNIT - len(lines), LANES), jnp.float32))
    small = [router[n : n + UNIT] for n in range(0, tall, UNIT)]
    small += [slab_ref[n : n + UNIT] for n in range(0, slab_ref.shape[0], UNIT)]
    small.append(jnp.concatenate(lines, axis=0))
    for block in range(64):
        part = small[block] if block < len(small) else jnp.zeros((UNIT, LANES), jnp.float32)
        parts[block_at(block) + (slice(UNIT * UNITS, BLOCK_ROWS),)] = part.astype(parts.dtype)

    order = (2, 1, 3, 0)
    for step in order:
        for half in range(2):
            sends.go(
                place.at(dcore=1),
                parts.at[half, 1 - place.core, place.along(half, step)],
                twin.at[half, step],
                twin_recv.at[half, step],
            )

    def ready_one(half, step):
        sends.landed(twin.at[half, step], twin_recv.at[half, step])
        own = parts[half, place.core, place.along(half, step)]
        sums[half, step] = (wide(own) + wide(twin[half, step])).astype(sums.dtype)

    done_one = ring_sum(
        sends, lambda half: half, sums, via_one, land_one, via_one_recv, land_one_recv, ready_one
    )
    arrived = set()

    def ready_two(half, step):
        if half not in arrived:
            arrived.add(half)
            done_one(half)
        spot = place.along(1 - half, step)
        total = wide(sums[half, 0, spot])
        for side in range(2):
            total = total + wide(land_one[half, side, spot])
        halves[half, step] = total.astype(halves.dtype)

    done_two = ring_sum_direct(
        sends, lambda half: 1 - half, halves, land_two, land_two_recv, ready_two
    )
    low = BLOCK_ROWS // 2
    for half in range(2):
        done_two(half)
        total = wide(halves[half, 0])
        for side in range(SIDE - 1):
            total = total + wide(land_two[half, side])
        halves[half, 0] = total.astype(halves.dtype)
        sends.go(
            place.at(dy=1),
            halves.at[half, 0, pl.ds(pl.multiple_of((1 - place.y) * low, UNIT), low)],
            other.at[half],
            far_recv.at[half],
        )

    def spot(half, core, first, second, rows=None):
        place_of = (half, core, place.along(half, first), place.along(1 - half, second))
        return full.at[place_of] if rows is None else full.at[place_of + (rows,)]

    def y_rows(y):
        return pl.ds(pl.multiple_of(y * low, UNIT), low)

    for half in range(2):
        sends.landed(other.at[half], far_recv.at[half])
        total = wide(halves[half, 0, y_rows(place.y)]) + wide(other[half])
        full[
            half, place.core, place.along(half, 0), place.along(1 - half, 0), y_rows(place.y)
        ] = total.astype(full.dtype)
        view = spot(half, place.core, 0, 0, y_rows(place.y))
        sends.go(place.at(dy=1), view, view, far_back_recv.at[half])

    subs = [pl.ds(piece * low, low) for piece in range(2)]
    for half in range(2):
        sends.landed(
            spot(half, place.core, 0, 0, y_rows(1 - place.y)), far_back_recv.at[half]
        )
        view = spot(half, place.core, 0, 0)
        for step in range(1, SIDE):
            sends.go(
                place.turned(1 - half, step), view, view, two_back_recv.at[half, SIDE - step]
            )

    def group(half, core, first, rows=None):
        if rows is None:
            return full.at[half, core, place.along(half, first)]
        return full.at[half, core, place.along(half, first), :, rows]

    for half in range(2):
        for step in range(1, SIDE):
            sends.landed(spot(half, place.core, 0, step), two_back_recv.at[half, step])
        view = group(half, place.core, 0)
        for step in (1, SIDE - 1):
            sends.go(place.turned(half, step), view, view, one_back_recv.at[half, SIDE - step, 0])
        sends.go(place.at(dcore=1), view, view, twin_back_recv.at[half, 0])
    for half in range(2):
        for piece, step in ((0, 1), (1, SIDE - 1)):
            view = group(half, place.core, SIDE - step)
            sends.landed(view, one_back_recv.at[half, SIDE - step, 0])
            part = group(half, place.core, SIDE - step, subs[piece])
            sends.go(place.turned(half, step), part, part, one_back_recv.at[half, 2, piece])
            sends.go(place.at(dcore=1), view, view, twin_back_recv.at[half, SIDE - step])
    for half in range(2):
        for piece in range(2):
            sends.landed(group(half, place.core, 2, subs[piece]), one_back_recv.at[half, 2, piece])
        view = group(half, place.core, 2)
        sends.go(place.at(dcore=1), view, view, twin_back_recv.at[half, 2])
    for first in (0, 3, 1, 2):
        for half in range(2):
            sends.landed(group(half, 1 - place.core, first), twin_back_recv.at[half, first])

    sends.finish()


def slab_table(tall, width):
    slabs = [(output, lane) for output in range(3) for lane in range(0, width, LANES)]
    slabs += [(3, lane) for lane in range(0, tall, LANES)]
    return slabs, runs([tall if output < 3 else width for output, _ in slabs])


def unpack_kernel(
    full, input_ref, mixed_ref,
    query_ref, key_ref, value_ref, proj_ref, router_ref, slab_ref, gains_ref, grad_input_ref,
    mixed_out_ref,
):
    grad_input_ref[...] = input_ref[...]
    mixed_out_ref[...] = mixed_ref[...]
    slabs, table = slab_table(query_ref.shape[0], query_ref.shape[1])
    for slab, row, block, inside, rows in table:
        output, lane = slabs[slab]
        ref = (query_ref, key_ref, value_ref, proj_ref)[output]
        ref[row : row + rows, lane : lane + LANES] = wide(
            full[block_at(block) + (slice(inside, inside + rows),)]
        )
    tall = router_ref.shape[0] // 2
    experts = router_ref.shape[1]

    def small(block):
        return wide(full[block_at(block) + (slice(UNIT * UNITS, BLOCK_ROWS),)])

    for block in range(tall // UNIT):
        part = small(block)
        for side in range(2):
            start = side * tall + block * UNIT
            router_ref[start : start + UNIT] = part[:, side * experts : (side + 1) * experts]
    base = tall // UNIT
    for block in range(slab_ref.shape[0] // UNIT):
        slab_ref[block * UNIT : (block + 1) * UNIT] = small(base + block)[:, : slab_ref.shape[1]]
    gains_ref[...] = small(base + slab_ref.shape[0] // UNIT)


def weight_totals(
    normed, grads, context, attended, grad_router, slab, grad_ffn, weights, tokens, grad_hidden,
    gain, mixed,
):
    kind = jnp.bfloat16
    tall = normed.shape[1]
    local = context.shape[1]
    piece = (BLOCK_ROWS, LANES)
    part = (BLOCK_ROWS // 2, LANES)
    sem = pltpu.SemaphoreType.DMA
    floats = functools.partial(jax.ShapeDtypeStruct, dtype=jnp.float32)
    full, grad_input = pl.pallas_call(
        weights_kernel,
        out_shape=(
            jax.ShapeDtypeStruct((2, 2, SIDE, SIDE) + piece, kind),
            floats(tokens.shape),
        ),
        in_specs=[VMEM] * 13,
        out_specs=(VMEM,) * 2,
        scratch_shapes=[
            pltpu.VMEM(tokens.shape, kind),
            pltpu.VMEM(tokens.shape, kind),
            pltpu.VMEM((2, 2, SIDE, SIDE) + piece, kind),
            pltpu.VMEM((2, SIDE, SIDE) + piece, kind),
            pltpu.VMEM((2, SIDE, SIDE) + piece, kind),
            pltpu.VMEM((2, 2, SIDE) + part, kind),
            pltpu.VMEM((2, 2, SIDE) + piece, kind),
            pltpu.VMEM((2, SIDE) + piece, kind),
            pltpu.VMEM((2, SIDE - 1) + piece, kind),
            pltpu.VMEM((2,) + part, kind),
            sem((64,)), sem((2, SIDE)),
            sem((2, 2)), sem((2, 2, 2)), sem((2, SIDE - 1)),
            sem((2,)), sem((2,)), sem((2, SIDE)), sem((2, SIDE, 2)), sem((2, SIDE)), sem,
        ],
        compiler_params=pltpu.CompilerParams(
            collective_id=3, has_side_effects=True, vmem_limit_bytes=60 * 1024 * 1024
        ),
        name="weight_totals",
    )(
        normed, grads, context, attended, grad_router, slab, grad_ffn, *weights, tokens,
        grad_hidden, gain,
    )
    return pl.pallas_call(
        unpack_kernel,
        out_shape=(
            floats((tall, local)),
            floats((tall, local)),
            floats((tall, local)),
            floats((local, tall)),
            floats(grad_router.shape),
            floats((slab.shape[0], local // HEAD)),
            floats((UNIT, LANES)),
            floats(tokens.shape),
            jax.ShapeDtypeStruct(tokens.shape, kind),
        ),
        in_specs=[VMEM] * 3,
        out_specs=(VMEM,) * 9,
        compiler_params=pltpu.CompilerParams(vmem_limit_bytes=60 * 1024 * 1024),
        name="unpack",
    )(full, grad_input, mixed)


QUARTERS = 4


def gelu_pair(values):
    root = 0.7978845608028654
    cubic = 0.044715
    square = values * values
    bend = jnp.tanh(root * values * (1.0 + cubic * square))
    active = 0.5 * values * (1.0 + bend)
    slope = 0.5 * (1.0 + bend) + 0.5 * values * (1.0 - bend * bend) * root * (
        1.0 + 3.0 * cubic * square
    )
    return active, slope


def middle_kernel(
    both_ref, tokens_ref, cotangent_ref, proj_ref, gain_ref, router_ref, route_ref, slot_ref,
    w_in_hbm, w_out_hbm,
    mixed_ref, hidden_ref, attended_ref, context_ref, grad_both_ref, grad_router_ref,
    grad_gain_ref, rows_in_ref, rows_grad_ref, activ_ref, grad_pre_ref,
    w_in, w_out, swapped, share, share_other, order, order_t, gather_t, send_one, recv_one,
    send_two, recv_two, sums, sums_other, given,
    load_sem, send_sem, one_send, one_recv, two_send, two_recv, swap_recv, share_recv,
    sums_recv, back_recv,
):
    place = Place()
    me = place.me
    count = 2 * 2 * SIDE * SIDE
    loads = [
        pltpu.make_async_copy(w_in_hbm, w_in, load_sem.at[0]),
        pltpu.make_async_copy(w_out_hbm, w_out, load_sem.at[1]),
    ]
    for load in loads:
        load.start()
    barrier = pltpu.get_barrier_semaphore()

    @pl.loop(1, count)
    def _(step):
        pl.semaphore_signal(
            barrier,
            inc=1,
            device_id={"ctx": lax.rem(me + step, count)},
            device_id_type=pl.DeviceIdType.MESH,
        )

    pl.semaphore_signal(
        barrier,
        inc=1,
        device_id={"mp": 1 - lax.axis_index("mp")},
        device_id_type=pl.DeviceIdType.MESH,
    )
    pl.semaphore_wait(barrier, count)
    sends = Sends(place, send_sem)
    tok_rows = tokens_ref.shape[0]
    first = place.y == 0

    mine = pl.ds(pl.multiple_of(place.y * tok_rows, tok_rows), tok_rows)
    theirs = pl.ds(pl.multiple_of((1 - place.y) * tok_rows, tok_rows), tok_rows)
    sends.go(place.at(dy=1), both_ref.at[theirs], swapped, swap_recv)
    kept = both_ref[mine]
    sends.landed(swapped, swap_recv)
    received = swapped[...]
    context = jnp.concatenate(
        [jnp.where(first, kept, received), jnp.where(first, received, kept)], axis=1
    )
    context_ref[...] = context
    share[...] = contract(context, proj_ref[...], 1, 0).astype(share.dtype)
    sends.across(share, share_other, share_recv)
    spots = tok_rows * QUARTERS
    cells = 16 * count
    route = route_ref[...].astype(jnp.float32)
    spot = route * 16.0 + slot_ref[...].astype(jnp.float32)
    square = (tok_rows, tok_rows)
    diagonal = lax.broadcasted_iota(jnp.int32, square, 0) == lax.broadcasted_iota(
        jnp.int32, square, 1
    )

    def column(line):
        return jnp.sum(jnp.where(diagonal, line, 0.0), axis=1, keepdims=True).astype(jnp.int32)

    spot_row = jnp.concatenate(
        [spot.astype(jnp.int32) + 4 * n for n in range(QUARTERS)], axis=1
    )
    spot_col = column(spot)
    gather = jnp.where(
        lax.broadcasted_iota(jnp.int32, (cells, spots), 0) == spot_row, 1.0, 0.0
    ).astype(jnp.bfloat16)
    sends.landed(share_other, share_recv)
    hidden = wide(tokens_ref[...]) + (wide(share[...]) + wide(share_other[...]))
    scale = lax.rsqrt(jnp.mean(hidden * hidden, axis=1, keepdims=True) + EPSILON)
    normed = hidden * scale * gain_ref[...][None]
    logits = lax.dot_general(
        normed, router_ref[...], (((1,), (0,)), ((), ())), precision=PRECISE,
        preferred_element_type=jnp.float32,
    )
    shifted = jnp.exp(logits - jnp.max(logits, axis=1, keepdims=True))
    probs = shifted / jnp.sum(shifted, axis=1, keepdims=True)
    chosen = jnp.where(
        column(route) == lax.broadcasted_iota(jnp.int32, probs.shape, 1), 1.0, 0.0
    )
    gate = jnp.sum(probs * chosen, axis=1, keepdims=True)
    grad_y = wide(cotangent_ref[...])
    width = 2 * tokens_ref.shape[1] // QUARTERS
    payload = [normed[:, :width], normed[:, width:]]
    payload += [gate * grad_y[:, :width], gate * grad_y[:, width:]]
    payload = jnp.concatenate(payload, axis=0).astype(jnp.bfloat16)
    send_one[...] = (
        contract(gather, payload, 1, 0).astype(send_one.dtype).reshape(send_one.shape)
    )

    def exchange(src, dst, send, recv):
        @pl.loop(1, count)
        def _(step):
            target = lax.rem(me + step, count)
            sender(target, src.at[target], dst.at[me], send.at[step], recv.at[step]).start()

        dst[me] = src[me]

    def arrive(dst, recv):
        @pl.loop(1, count)
        def _(step):
            source = lax.rem(me + count - step, count)
            sends.landed(dst.at[source], recv.at[step])

    exchange(send_one, recv_one, one_send, one_recv)
    rows = cells // QUARTERS

    def cell_of(index):
        row = index & (rows - 1)
        return (row >> 2) * 16 + (index >> 8) * 4 + (row & 3)

    down = lax.broadcasted_iota(jnp.int32, (cells, cells), 0)
    right = lax.broadcasted_iota(jnp.int32, (cells, cells), 1)
    order[...] = jnp.where(cell_of(down) == right, 1.0, 0.0).astype(order.dtype)
    order_t[...] = jnp.where(down == cell_of(right), 1.0, 0.0).astype(order_t.dtype)
    cell = lax.broadcasted_iota(jnp.int32, (tok_rows, cells), 1)
    for n in range(QUARTERS):
        gather_t[n * tok_rows : (n + 1) * tok_rows] = jnp.where(
            spot_col + 4 * n == cell, 1.0, 0.0
        ).astype(gather_t.dtype)
    for load in loads:
        load.wait()
    arrive(recv_one, one_recv)

    got = contract(order[...], recv_one[...].reshape(cells, width), 1, 0).astype(jnp.bfloat16)
    rows_in_ref[...] = jnp.concatenate([got[:rows], got[rows : 2 * rows]], axis=1)
    rows_grad_ref[...] = jnp.concatenate([got[2 * rows : 3 * rows], got[3 * rows :]], axis=1)
    hidden_units = w_in.shape[1]
    chunk = hidden_units // 3
    out = jnp.zeros(rows_in_ref.shape, jnp.float32)
    back = jnp.zeros(rows_in_ref.shape, jnp.float32)
    for start in range(0, hidden_units, chunk):
        units = slice(start, start + chunk)
        active, slope = gelu_pair(contract(rows_in_ref[...], w_in[:, units], 1, 0))
        active = active.astype(jnp.bfloat16)
        activ_ref[:, units] = active
        out = out + contract(active, w_out[units], 1, 0)
        grad_pre = (contract(rows_grad_ref[...], w_out[units], 1, 1) * slope).astype(jnp.bfloat16)
        grad_pre_ref[:, units] = grad_pre
        back = back + contract(grad_pre, w_in[:, units], 1, 1)
    whole = [out[:, :width], out[:, width:], back[:, :width], back[:, width:]]
    whole = jnp.concatenate(whole, axis=0).astype(jnp.bfloat16)
    send_two[...] = (
        contract(order_t[...], whole, 1, 0).astype(send_two.dtype).reshape(send_two.shape)
    )
    exchange(send_two, recv_two, two_send, two_recv)
    arrive(recv_two, two_recv)
    sums[...] = contract(gather_t[...], recv_two[...].reshape(cells, width), 1, 0).astype(
        sums.dtype
    )
    sends.across(sums, sums_other, sums_recv)
    sends.landed(sums_other, sums_recv)
    total = wide(sums[...]) + wide(sums_other[...])
    parts = [total[n * tok_rows : (n + 1) * tok_rows] for n in range(QUARTERS)]
    expert_rows = jnp.concatenate(parts[:2], axis=1).astype(jnp.bfloat16).astype(jnp.float32)
    grad_sent = jnp.concatenate(parts[2:], axis=1).astype(jnp.bfloat16).astype(jnp.float32)

    mixed_ref[...] = (hidden + gate * expert_rows).astype(mixed_ref.dtype)
    grad_gate = jnp.sum(grad_y * expert_rows, axis=1, keepdims=True)
    grad_logits = grad_gate * gate * (chosen - probs)
    grad_router_ref[...] = lax.dot_general(
        normed, grad_logits, (((0,), (0,)), ((), ())), precision=PRECISE,
        preferred_element_type=jnp.float32,
    )
    grad_normed = grad_sent + lax.dot_general(
        grad_logits, router_ref[...], (((1,), (1,)), ((), ())), precision=PRECISE,
        preferred_element_type=jnp.float32,
    )
    scaled = gain_ref[...][None] * grad_normed
    grad_gain_ref[...] = jnp.sum(grad_normed * hidden * scale, axis=0, keepdims=True)
    grad_hidden = (
        grad_y
        + scale * scaled
        - hidden * scale**3 * jnp.mean(scaled * hidden, axis=1, keepdims=True)
    )
    hidden_ref[...] = grad_hidden
    attended = grad_hidden.astype(jnp.bfloat16)
    attended_ref[...] = attended
    grad_context = contract(attended, proj_ref[...], 1, 1).astype(jnp.bfloat16)
    half = grad_context.shape[1] // 2
    left, right_part = grad_context[:, :half], grad_context[:, half:]
    given[...] = jnp.where(first, right_part, left)
    grad_both_ref[mine] = jnp.where(first, left, right_part)
    sends.go(place.at(dy=1), given, grad_both_ref.at[mine], back_recv)
    sends.landed(grad_both_ref.at[theirs], back_recv)
    sends.finish()

    @pl.loop(1, count)
    def _(step):
        for src, send in ((send_one, one_send), (send_two, two_send)):
            sender(me, src.at[0], src.at[0], send.at[step], send.at[step]).wait_send()


def middle(
    both, tokens, cotangent, w_proj, gain, router, w_in, w_out, route, slot
):
    kind = jnp.bfloat16
    tok_rows, wide_row = tokens.shape
    count = router.shape[1]
    rows = 4 * count
    hidden = w_in.shape[1]
    width = 2 * wide_row // QUARTERS
    spots = QUARTERS * tok_rows
    shape = jax.ShapeDtypeStruct
    sem = pltpu.SemaphoreType.DMA
    buffer = pltpu.VMEM((count, 16, width), kind)
    return pl.pallas_call(
        middle_kernel,
        out_shape=(
            shape(tokens.shape, kind),
            shape(tokens.shape, jnp.float32),
            shape(tokens.shape, kind),
            shape((tok_rows, 2 * both.shape[1]), kind),
            shape(both.shape, kind),
            shape(router.shape, jnp.float32),
            shape((1, wide_row), jnp.float32),
            shape((rows, wide_row), kind),
            shape((rows, wide_row), kind),
            shape((rows, hidden), kind),
            shape((rows, hidden), kind),
        ),
        in_specs=[VMEM] * 8 + [ANYWHERE] * 2,
        out_specs=(VMEM,) * 11,
        scratch_shapes=[
            pltpu.VMEM(w_in.shape, kind),
            pltpu.VMEM(w_out.shape, kind),
            pltpu.VMEM((tok_rows, both.shape[1]), kind),
            pltpu.VMEM(tokens.shape, kind),
            pltpu.VMEM(tokens.shape, kind),
            pltpu.VMEM((16 * count, 16 * count), kind),
            pltpu.VMEM((16 * count, 16 * count), kind),
            pltpu.VMEM((spots, 16 * count), kind),
            buffer, buffer, buffer, buffer,
            pltpu.VMEM((spots, width), kind),
            pltpu.VMEM((spots, width), kind),
            pltpu.VMEM((tok_rows, both.shape[1]), kind),
            sem((2,)), sem((4,)), sem((count,)), sem((count,)), sem((count,)), sem((count,)),
            sem, sem, sem, sem,
        ],
        compiler_params=pltpu.CompilerParams(
            collective_id=4, has_side_effects=True, vmem_limit_bytes=60 * 1024 * 1024
        ),
        name="middle",
    )(
        both, tokens, cotangent, w_proj, gain, router, route[None], slot[None], w_in, w_out,
    )


def shards(
    tokens,
    attn_gain,
    w_query,
    w_key,
    w_value,
    w_proj,
    rel_table,
    rel_bucket,
    ffn_gain,
    router,
    w_in,
    w_out,
    expert_route,
    expert_slot,
    cotangent,
):
    me = lax.axis_index("ctx")
    side = 2 * SIDE * SIDE
    place = jnp.stack([me % side, me // side]).astype(jnp.int32)
    normed, rows, held = gather_plane(tokens, attn_gain, w_query, w_key, w_value)

    buckets = jnp.pad(rel_bucket, (0, 1), mode="edge").reshape(BLOCK, BLOCK)
    both, turned, lse, flipped, table, uneven = attend(place, rel_table, buckets, held, rows)
    (
        mixed, grad_hidden1, grad_attended, context, grad_both, grad_router, grad_ffn_gain,
        rows_in, rows_grad, activ, grad_pre,
    ) = middle(
        both, tokens, cotangent, w_proj, ffn_gain, router, w_in[0], w_out[0], expert_route,
        expert_slot,
    )
    grad_parts, grad_rows, slab, grad_expert_in, grad_expert_out = attend_back(
        place, uneven, table, held, rows, grad_both, turned, lse, flipped, rows_in, rows_grad,
        activ, grad_pre, rel_table.shape[0],
    )
    grads = scatter_plane(grad_parts, grad_rows)
    (
        grad_query, grad_key, grad_value, grad_proj, grad_router, grad_table, gains, grad_input,
        mixed,
    ) = weight_totals(
        normed, grads, context, grad_attended, grad_router, slab, grad_ffn_gain,
        (w_query, w_key, w_value), tokens, grad_hidden1, attn_gain, mixed,
    )
    lines = tokens.shape[1] // LANES
    return (
        mixed,
        grad_input,
        gains[:lines].reshape(-1),
        grad_query,
        grad_key,
        grad_value,
        grad_proj,
        grad_table,
        gains[lines : 2 * lines].reshape(-1),
        grad_router,
        grad_expert_in[None],
        grad_expert_out[None],
    )


def solution(mesh):
    return jax.shard_map(
        shards,
        mesh=mesh,
        in_specs=(
            P("ctx", None),
            P(),
            P(None, "mp"),
            P(None, "mp"),
            P(None, "mp"),
            P("mp", None),
            P(None, "mp"),
            P(),
            P(),
            P(),
            P("ctx", None, "mp"),
            P("ctx", "mp", None),
            P("ctx"),
            P("ctx"),
            P("ctx", None),
        ),
        out_specs=(
            P("ctx", None),
            P("ctx", None),
            P(),
            P(None, "mp"),
            P(None, "mp"),
            P(None, "mp"),
            P("mp", None),
            P(None, "mp"),
            P(),
            P(),
            P("ctx", None, "mp"),
            P("ctx", "mp", None),
        ),
        check_vma=False,
    )
```

```python
import functools
import jax
import jax.numpy as jnp
from jax import lax
from jax.experimental import pallas as pl
from jax.experimental.pallas import tpu as pltpu
from jax.sharding import PartitionSpec as P

HEAD = 64
GROUP = 3
BLOCK = 128
PAIR = 2 * BLOCK
FORWARD_SPAN = 8
BACKWARD_SPAN = 4
VMEM = pl.BlockSpec(memory_space=pltpu.VMEM)
SMEM = pl.BlockSpec(memory_space=pltpu.SMEM)
LARGE = pltpu.CompilerParams(vmem_limit_bytes=60 * 1024 * 1024)


def contract(left, right, left_dim, right_dim):
    return lax.dot_general(
        left,
        right,
        (((left_dim,), (right_dim,)), ((), ())),
        preferred_element_type=jnp.float32,
    )


def window_row(place, chunk, tile, half, span):
    return 63 - (span * chunk + tile // 2) + place + BLOCK // 4 * (half - tile % 2)


def tile_consts(table_ref, head, place, chunk, tile, span):
    parts = []
    for half in range(2):
        row = window_row(place, chunk, tile, half, span)
        parts.append(jnp.broadcast_to(table_ref[head, pl.ds(row, 1), 0:1], (1, BLOCK)))
    return jnp.concatenate(parts, axis=1)


def chunk_mixed(uneven_ref, place, chunk, span):
    mixed = 0
    for tile in range(2 * span):
        for half in range(2):
            mixed = mixed + uneven_ref[0, window_row(place, chunk, tile, half, span)]
    return mixed


def add_uneven(table_ref, uneven_ref, score_ref, place, chunk, span):
    for tile in range(2 * span):
        for half in range(2):
            row = window_row(place, chunk, tile, half, span)

            @pl.when(uneven_ref[0, row] > 0)
            def _():
                for head in range(GROUP):
                    window = jnp.concatenate(
                        [table_ref[head, pl.ds(row, 1), :], table_ref[head, pl.ds(row + 1, 1), :]],
                        axis=1,
                    )
                    window = window - window[:, 0:1]
                    grid = pltpu.roll(
                        jnp.broadcast_to(window, (BLOCK, PAIR)),
                        BLOCK,
                        1,
                        stride=1,
                        stride_axis=0,
                    )[:, :BLOCK]
                    rows = slice(tile * BLOCK, (tile + 1) * BLOCK)
                    cols = slice(half * BLOCK, (half + 1) * BLOCK)
                    score_ref[head, rows, cols] += grid


def stream(keys_hbm, held_ref, sems, span):
    def copy(chunk):
        slot = lax.rem(chunk, 2)
        return pltpu.make_async_copy(
            keys_hbm.at[pl.ds(chunk * span, span)], held_ref.at[slot], sems.at[slot]
        )

    return copy


def head_columns(ref, head):
    return ref[:, head * HEAD : (head + 1) * HEAD]


def turn(values):
    return values.astype(jnp.float32).T


def fill_turned(dst_ref, src_ref, first):
    for head in range(GROUP):
        part = turn(head_columns(src_ref, head))
        none = jnp.zeros_like(part)
        parts = [part, none] if first else [none, part]
        dst_ref[head] = jnp.concatenate(parts, axis=0).astype(dst_ref.dtype)


def fill_padded(dst_ref, src_ref, first):
    for head in range(GROUP):
        part = head_columns(src_ref, head)
        none = jnp.zeros_like(part)
        parts = [part, none] if first else [none, part]
        dst_ref[head] = jnp.concatenate(parts, axis=1)


def side_by_side(parts):
    return jnp.concatenate([turn(part) for part in parts], axis=1).astype(jnp.bfloat16)


def flip_both(values):
    down = lax.broadcasted_iota(jnp.int32, (BLOCK, BLOCK), 0)
    right = lax.broadcasted_iota(jnp.int32, (BLOCK, BLOCK), 1)
    anti = jnp.where(down + right == BLOCK - 1, 1.0, 0.0).astype(jnp.bfloat16)
    once = contract(anti, values.astype(jnp.float32).astype(jnp.bfloat16), 1, 0)
    return contract(once.astype(jnp.bfloat16), anti, 1, 0).astype(jnp.int32)


def line_of(column):
    down = lax.broadcasted_iota(jnp.int32, (BLOCK, BLOCK), 0)
    right = lax.broadcasted_iota(jnp.int32, (BLOCK, BLOCK), 1)
    return jnp.sum(jnp.where(down == right, column, 0.0), axis=0, keepdims=True)


def shifted_up(column):
    return jnp.concatenate([column[1:], column[-1:]], axis=0)


def forward_kernel(
    place_ref, rel_ref, buckets_ref, keys_hbm, rows_ref,
    out_ref, turned_ref, lse_ref, flipped_ref, table_ref, uneven_out_ref,
    held_ref, held_sem, uneven_ref, uneven_sem,
    query_ref, best_ref, sum_ref, total_ref, score_ref,
):
    place = place_ref[0]
    span = FORWARD_SPAN
    tiles, length = 2 * span, PAIR * span
    fetch = stream(keys_hbm, held_ref, held_sem, span)
    chunks = keys_hbm.shape[0] // span
    fetch(0).start()
    flipped = flip_both(buckets_ref[...])
    flipped_ref[...] = flipped
    floats = flipped.astype(jnp.float32)
    high = jnp.max(floats, axis=1, keepdims=True)
    low = jnp.min(floats, axis=1, keepdims=True)
    high = jnp.maximum(high, shifted_up(high))
    low = jnp.minimum(low, shifted_up(low))
    uneven_out_ref[...] = line_of(jnp.where(high > low, 1.0, 0.0)).astype(jnp.int32)
    flags = pltpu.make_async_copy(uneven_out_ref, uneven_ref, uneven_sem)
    flags.start()
    for head in range(GROUP):
        values = jnp.zeros((BLOCK, BLOCK), jnp.float32)
        for bucket in range(rel_ref.shape[1]):
            value = rel_ref[place_ref[1] * GROUP + head, bucket]
            values = jnp.where(flipped == bucket, value, values)
        table_ref[head] = values
    fill_turned(query_ref, rows_ref, True)
    flags.wait()
    best_ref[...] = jnp.full_like(best_ref, -1e30)
    sum_ref[...] = jnp.zeros_like(sum_ref)
    total_ref[...] = jnp.zeros_like(total_ref)

    def rest(chunk, head, held, scores):
        consts = [tile_consts(table_ref, head, place, chunk, tile, span) for tile in range(tiles)]
        old = best_ref[head]
        new = old
        for tile in range(tiles):
            part = scores[tile * BLOCK : (tile + 1) * BLOCK]
            new = jnp.maximum(new, jnp.max(part, axis=0, keepdims=True) + consts[tile])
        decay = jnp.exp(old - new)
        weights = [
            jnp.exp(scores[tile * BLOCK : (tile + 1) * BLOCK] - (new - consts[tile]))
            for tile in range(tiles)
        ]
        weights = jnp.concatenate(weights, axis=0)
        sum_ref[head] = sum_ref[head] * decay + jnp.sum(weights, axis=0, keepdims=True)
        best_ref[head] = new
        total_ref[head] = total_ref[head] * decay + contract(
            held, weights.astype(jnp.bfloat16), 0, 0
        )

    @pl.loop(0, chunks)
    def _(chunk):
        slot = lax.rem(chunk, 2)
        fetch(chunk).wait()

        @pl.when(chunk + 1 < chunks)
        def _():
            fetch(chunk + 1).start()

        def held_of(head):
            return held_ref[slot, :, head].reshape(length, 2 * HEAD)

        mixed = chunk_mixed(uneven_ref, place, chunk, span)

        @pl.when(mixed == 0)
        def _():
            helds = [held_of(head) for head in range(GROUP)]
            scores = [contract(helds[head], query_ref[head], 1, 0) for head in range(GROUP)]
            for head in range(GROUP):
                rest(chunk, head, helds[head], scores[head])

        @pl.when(mixed > 0)
        def _():
            for head in range(GROUP):
                score_ref[head] = contract(held_of(head), query_ref[head], 1, 0)
            add_uneven(table_ref, uneven_ref, score_ref, place, chunk, span)
            for head in range(GROUP):
                rest(chunk, head, held_of(head), score_ref[head])

    for head in range(GROUP):
        turned_ref[head] = total_ref[head][HEAD:] / sum_ref[head]
    out_ref[...] = side_by_side([turned_ref[head] for head in range(GROUP)])
    for head in range(GROUP):
        lse_ref[head] = best_ref[head] + jnp.log(sum_ref[head])


def backward_kernel(
    place_ref, uneven_ref, table_ref, keys_hbm, rows_ref, grads_ref, turned_ref, lse_ref,
    flipped_ref, rows_in_ref, rows_grad_ref, activ_ref, grad_pre_ref,
    grad_keys_hbm, grad_rows_ref, slab_ref, expert_in_hbm, expert_out_hbm,
    held_ref, held_sem, grad_keys_ref, grad_keys_sem, expert_in, expert_out, expert_sem, offsets_ref, query_t_ref, grad_t_ref, query_ref, grad_ref, delta_ref, grad_query_ref, score_ref,
):
    place = place_ref[0]
    span = BACKWARD_SPAN
    tiles, length = 2 * span, PAIR * span
    fetch = stream(keys_hbm, held_ref, held_sem, span)
    chunks = keys_hbm.shape[0] // span
    fetch(0).start()

    def give(chunk):
        slot = lax.rem(chunk, 2)
        return pltpu.make_async_copy(
            grad_keys_ref.at[slot],
            grad_keys_hbm.at[pl.ds(chunk * span, span)],
            grad_keys_sem.at[slot],
        )

    expert_in[...] = contract(rows_in_ref[...], grad_pre_ref[...], 0, 0)
    expert_out[...] = contract(activ_ref[...], rows_grad_ref[...], 0, 0)
    stores = [
        pltpu.make_async_copy(expert_in, expert_in_hbm, expert_sem.at[0]),
        pltpu.make_async_copy(expert_out, expert_out_hbm, expert_sem.at[1]),
    ]
    for store in stores:
        store.start()
    fill_turned(query_t_ref, rows_ref, True)
    fill_turned(grad_t_ref, grads_ref, False)
    fill_padded(query_ref, rows_ref, True)
    fill_padded(grad_ref, grads_ref, False)
    for head in range(GROUP):
        delta_ref[head] = jnp.sum(
            grad_t_ref[head][HEAD:].astype(jnp.float32) * turned_ref[head], axis=0, keepdims=True
        )
    grad_query_ref[...] = jnp.zeros_like(grad_query_ref)
    offsets_ref[...] = jnp.zeros_like(offsets_ref)

    def rest(chunk, head, held, scores, grads):
        probs = jnp.concatenate(
            [
                jnp.exp(
                    scores[tile * BLOCK : (tile + 1) * BLOCK]
                    - (lse_ref[head] - tile_consts(table_ref, head, place, chunk, tile, span))
                )
                for tile in range(tiles)
            ],
            axis=0,
        )
        slopes = probs * (grads - delta_ref[head])
        rounded = slopes.astype(jnp.bfloat16)
        part = contract(rounded, query_ref[head], 1, 0) + contract(
            probs.astype(jnp.bfloat16), grad_ref[head], 1, 0
        )
        grad_keys_ref[lax.rem(chunk, 2), :, head] = part.astype(grad_keys_ref.dtype).reshape(
            span, PAIR, 2 * HEAD
        )
        grad_query_ref[head] += contract(held, rounded, 0, 0)
        return slopes

    def put_even(chunk, head, tile, half, slopes):
        row = window_row(place, chunk, tile, half, span)
        offsets_ref[head, pl.ds(row, 1), :] += jnp.sum(slopes, axis=0, keepdims=True)

    def put_uneven(chunk, head, tile, half, slopes):
        row = window_row(place, chunk, tile, half, span)
        wide = jnp.concatenate([slopes, jnp.zeros_like(slopes)], axis=1)
        folded = jnp.zeros((8, PAIR), jnp.float32)
        for group in range(BLOCK // 8):
            folded = folded + pltpu.roll(
                wide[group * 8 : (group + 1) * 8], (BLOCK - 8 * group) % PAIR, 1
            )
        line = jnp.zeros((1, PAIR), jnp.float32)
        for step in range(8):
            line = line + pltpu.roll(folded, (PAIR - step) % PAIR, 1)[step : step + 1]
        offsets_ref[head, pl.ds(row, 1), :] += line[:, :BLOCK]
        offsets_ref[head, pl.ds(row + 1, 1), :] += line[:, BLOCK:]

    @pl.loop(0, chunks)
    def _(chunk):
        slot = lax.rem(chunk, 2)
        fetch(chunk).wait()

        @pl.when(chunk + 1 < chunks)
        def _():
            fetch(chunk + 1).start()

        def held_of(head):
            return held_ref[slot, :, head].reshape(length, 2 * HEAD)

        @pl.when(chunk >= 2)
        def _():
            give(chunk - 2).wait()

        mixed = chunk_mixed(uneven_ref, place, chunk, span)

        @pl.when(mixed == 0)
        def _():
            helds = [held_of(head) for head in range(GROUP)]
            scores = [contract(helds[head], query_t_ref[head], 1, 0) for head in range(GROUP)]
            grads = [contract(helds[head], grad_t_ref[head], 1, 0) for head in range(GROUP)]
            for head in range(GROUP):
                slopes = rest(chunk, head, helds[head], scores[head], grads[head])
                for tile in range(tiles):
                    for half in range(2):
                        part = slopes[
                            tile * BLOCK : (tile + 1) * BLOCK, half * BLOCK : (half + 1) * BLOCK
                        ]
                        put_even(chunk, head, tile, half, part)

        @pl.when(mixed > 0)
        def _():
            for head in range(GROUP):
                score_ref[head] = contract(held_of(head), query_t_ref[head], 1, 0)
            add_uneven(table_ref, uneven_ref, score_ref, place, chunk, span)
            for head in range(GROUP):
                held = held_of(head)
                grads = contract(held, grad_t_ref[head], 1, 0)
                score_ref[head] = rest(chunk, head, held, score_ref[head], grads)
            for tile in range(tiles):
                for half in range(2):
                    rows = slice(tile * BLOCK, (tile + 1) * BLOCK)
                    cols = slice(half * BLOCK, (half + 1) * BLOCK)
                    uneven = uneven_ref[0, window_row(place, chunk, tile, half, span)]

                    @pl.when(uneven == 0)
                    def _():
                        for head in range(GROUP):
                            put_even(chunk, head, tile, half, score_ref[head, rows, cols])

                    @pl.when(uneven > 0)
                    def _():
                        for head in range(GROUP):
                            put_uneven(chunk, head, tile, half, score_ref[head, rows, cols])

        give(chunk).start()

    for chunk in (chunks - 2, chunks - 1):
        give(chunk).wait()
    grad_rows_ref[...] = side_by_side([grad_query_ref[head][:HEAD] for head in range(GROUP)])
    lanes = lax.broadcasted_iota(jnp.int32, (1, BLOCK), 1)
    for bucket in range(slab_ref.shape[0]):
        hit = flipped_ref[...] == bucket
        line = jnp.zeros((1, BLOCK), jnp.float32)
        for head in range(GROUP):
            part = jnp.sum(jnp.where(hit, offsets_ref[head], 0.0), axis=0, keepdims=True)
            part = jnp.sum(part, axis=1, keepdims=True)
            line = jnp.where(lanes == place_ref[1] * GROUP + head, part, line)
        slab_ref[pl.ds(bucket, 1)] = line
    for store in stores:
        store.wait()


def attend(place, rel_table, buckets, keys, rows):
    shape = jax.ShapeDtypeStruct
    anywhere = pl.BlockSpec(memory_space=pl.ANY)
    return pl.pallas_call(
        forward_kernel,
        out_shape=(
            shape(rows.shape, jnp.bfloat16),
            shape((GROUP, HEAD, PAIR), jnp.float32),
            shape((GROUP, 1, PAIR), jnp.float32),
            shape((BLOCK, BLOCK), jnp.int32),
            shape((GROUP, BLOCK, BLOCK), jnp.float32),
            shape((1, BLOCK), jnp.int32),
        ),
        in_specs=[SMEM, SMEM, VMEM, anywhere, VMEM],
        out_specs=(VMEM,) * 6,
        scratch_shapes=[
            pltpu.VMEM((2, FORWARD_SPAN) + keys.shape[1:], keys.dtype),
            pltpu.SemaphoreType.DMA((2,)),
            pltpu.SMEM((1, BLOCK), jnp.int32),
            pltpu.SemaphoreType.DMA,
            pltpu.VMEM((GROUP, 2 * HEAD, PAIR), jnp.bfloat16),
            pltpu.VMEM((GROUP, 1, PAIR), jnp.float32),
            pltpu.VMEM((GROUP, 1, PAIR), jnp.float32),
            pltpu.VMEM((GROUP, 2 * HEAD, PAIR), jnp.float32),
            pltpu.VMEM((GROUP, FORWARD_SPAN * PAIR, PAIR), jnp.float32),
        ],
        compiler_params=LARGE,
        name="attend",
    )(place, rel_table, buckets, keys, rows)


def attend_back(
    place, uneven, table, keys, rows, grads, turned, lse, flipped, rows_in, rows_grad, activ,
    grad_pre, buckets,
):
    shape = jax.ShapeDtypeStruct
    wide_row, hidden = rows_in.shape[1], activ.shape[1]
    anywhere = pl.BlockSpec(memory_space=pl.ANY)
    return pl.pallas_call(
        backward_kernel,
        out_shape=(
            shape(keys.shape, jnp.bfloat16),
            shape(rows.shape, jnp.bfloat16),
            shape((buckets, BLOCK), jnp.float32),
            shape((wide_row, hidden), jnp.float32),
            shape((hidden, wide_row), jnp.float32),
        ),
        in_specs=[SMEM, SMEM, VMEM, anywhere] + [VMEM] * 9,
        out_specs=(anywhere, VMEM, VMEM, anywhere, anywhere),
        scratch_shapes=[
            pltpu.VMEM((2, BACKWARD_SPAN) + keys.shape[1:], keys.dtype),
            pltpu.SemaphoreType.DMA((2,)),
            pltpu.VMEM((2, BACKWARD_SPAN) + keys.shape[1:], keys.dtype),
            pltpu.SemaphoreType.DMA((2,)),
            pltpu.VMEM((wide_row, hidden), jnp.float32),
            pltpu.VMEM((hidden, wide_row), jnp.float32),
            pltpu.SemaphoreType.DMA((2,)),
            pltpu.VMEM((GROUP, BLOCK, BLOCK), jnp.float32),
            pltpu.VMEM((GROUP, 2 * HEAD, PAIR), jnp.bfloat16),
            pltpu.VMEM((GROUP, 2 * HEAD, PAIR), jnp.bfloat16),
            pltpu.VMEM((GROUP, PAIR, 2 * HEAD), jnp.bfloat16),
            pltpu.VMEM((GROUP, PAIR, 2 * HEAD), jnp.bfloat16),
            pltpu.VMEM((GROUP, 1, PAIR), jnp.float32),
            pltpu.VMEM((GROUP, 2 * HEAD, PAIR), jnp.float32),
            pltpu.VMEM((GROUP, BACKWARD_SPAN * PAIR, PAIR), jnp.float32),
        ],
        compiler_params=LARGE,
        name="attend_back",
    )(
        place, uneven, table, keys, rows, grads, turned, lse, flipped, rows_in, rows_grad, activ,
        grad_pre,
    )


EPSILON = 1e-06
PRECISE = lax.Precision.HIGHEST
ANYWHERE = pl.BlockSpec(memory_space=pl.ANY)
SIDE = 4


class Place:
    def __init__(self):
        self.me = lax.axis_index("ctx")
        self.core = lax.rem(self.me, 2)
        self.z = lax.rem(self.me // 2, SIDE)
        self.x = lax.rem(self.me // (2 * SIDE), SIDE)
        self.y = self.me // (2 * SIDE * SIDE)

    def at(self, dx=0, dz=0, dcore=0, dy=0):
        x = lax.rem(self.x + dx, SIDE)
        z = lax.rem(self.z + dz, SIDE)
        core = lax.rem(self.core + dcore, 2)
        y = lax.rem(self.y + dy, 2)
        return ((y * SIDE + x) * SIDE + z) * 2 + core

    def turned(self, axis, step):
        return self.at(dx=step) if axis == 0 else self.at(dz=step)

    def along(self, axis, step):
        return lax.rem((self.x if axis == 0 else self.z) + step, SIDE)


def greet(targets, across=False):
    barrier = pltpu.get_barrier_semaphore()
    if across:
        pl.semaphore_signal(
            barrier,
            inc=1,
            device_id={"mp": 1 - lax.axis_index("mp")},
            device_id_type=pl.DeviceIdType.MESH,
        )
    for target in targets:
        pl.semaphore_signal(
            barrier, inc=1, device_id={"ctx": target}, device_id_type=pl.DeviceIdType.MESH
        )
    return barrier, len(targets) + int(across)


def meet(targets, across=False):
    pl.semaphore_wait(*greet(targets, across))


def ring_targets(place):
    found = [place.at(dcore=1)]
    for step in range(1, SIDE):
        found += [place.at(dx=step), place.at(dz=step)]
    return found


def sender(target, src, dst, send_sem, recv_sem):
    return pltpu.make_async_remote_copy(
        src_ref=src,
        dst_ref=dst,
        send_sem=send_sem,
        recv_sem=recv_sem,
        device_id={"ctx": target},
        device_id_type=pl.DeviceIdType.MESH,
    )


def wide(value):
    return value.astype(jnp.float32)


class Sends:
    def __init__(self, place, sems):
        self.place, self.sems, self.started = place, sems, []

    def go(self, target, src, dst, recv_sem):
        copy = sender(target, src, dst, self.sems.at[len(self.started)], recv_sem)
        copy.start()
        self.started.append(copy)
        return copy

    def across(self, src, dst, recv_sem):
        copy = pltpu.make_async_remote_copy(
            src_ref=src,
            dst_ref=dst,
            send_sem=self.sems.at[len(self.started)],
            recv_sem=recv_sem,
            device_id={"mp": 1 - lax.axis_index("mp")},
            device_id_type=pl.DeviceIdType.MESH,
        )
        copy.start()
        self.started.append(copy)

    def landed(self, view, sem):
        sender(self.place.me, view, view, sem, sem).wait_recv()

    def finish(self):
        for copy in self.started:
            copy.wait_send()


def gather_kernel(
    tokens_ref, gain_ref, w_query_ref, w_key_ref, w_value_ref,
    normed_ref, rows_ref, out_ref,
    block_ref, given, other, local_sem, send_sem, ring_recv, twin_recv, swap_recv,
):
    place = Place()
    barrier = greet(ring_targets(place) + [place.at(dy=1)])
    sends = Sends(place, send_sem)
    half_rows = block_ref.shape[1] // 2
    sub_rows = half_rows // 2
    first = place.y == 0
    width = GROUP * HEAD
    floats_in = wide(tokens_ref[...])
    scale = lax.rsqrt(jnp.mean(floats_in * floats_in, axis=1, keepdims=True) + EPSILON)
    normed = (floats_in * scale * gain_ref[...][None]).astype(normed_ref.dtype)
    normed_ref[...] = normed
    kept = []
    for n, ref in enumerate((w_query_ref, w_key_ref, w_value_ref)):
        made = contract(normed, ref[...], 1, 0).astype(given.dtype)
        kept.append(jnp.where(first, made[:, :width], made[:, width:]))
        given[n] = jnp.where(first, made[:, width:], made[:, :width])

    def rows_at(half, start=0, count=half_rows):
        side = place.y if half == 0 else 1 - place.y
        return pl.ds(pl.multiple_of(side * half_rows + start, sub_rows), count)

    def put(half, query, key, value):
        rows_ref[rows_at(half)] = query
        for head in range(GROUP):
            lanes = slice(head * HEAD, (head + 1) * HEAD)
            block_ref[head, rows_at(half)] = jnp.concatenate(
                [key[:, lanes], value[:, lanes]], axis=1
            )

    put(0, *kept)
    pl.semaphore_wait(*barrier)
    sends.go(place.at(dy=1), given, other, swap_recv)

    def rows_of(half, piece):
        if piece is None:
            return rows_at(half)
        return rows_at(half, piece * sub_rows, sub_rows)

    def view(half, first, second, core, piece=None):
        x, z = (second, first) if half == 0 else (first, second)
        slot = (place.along(0, x) * SIDE + place.along(1, z)) * 2 + core
        return out_ref.at[slot, :, rows_of(half, piece)]

    def held(half, first, second, piece=None):
        if first == 0 and second == 0:
            return block_ref.at[:, rows_of(half, piece)]
        return view(half, first, second, place.core, piece)

    def shift(half, first, second, stage, step, piece=None):
        axis = 1 - half if stage == 0 else half
        if stage == 0:
            slot = ((first - step) % SIDE, second)
        else:
            slot = (first, (second - step) % SIDE)
        sends.go(
            place.turned(axis, step % SIDE),
            held(half, first, second, piece),
            view(half, first, second, place.core, piece),
            ring_recv.at[half, slot[0], slot[1], piece or 0],
        )

    def to_twin(half, first, second):
        sends.go(
            place.at(dcore=1),
            held(half, first, second),
            view(half, first, second, place.core),
            twin_recv.at[half, first, second],
        )

    def wait(half, first, second):
        if second == 2:
            for piece in range(2):
                sends.landed(
                    view(half, first, second, place.core, piece),
                    ring_recv.at[half, first, second, piece],
                )
        else:
            sends.landed(
                view(half, first, second, place.core), ring_recv.at[half, first, second, 0]
            )

    def relay(half, first, second):
        if second == SIDE - 1:
            shift(half, first, second, 1, 1, 0)
        elif second == 1:
            shift(half, first, second, 1, -1, 1)

    for half in range(2):
        if half == 1:
            sends.landed(other, swap_recv)
            put(1, other[0], other[1], other[2])
        for stage in range(2):
            for step in (1, -1, 2)[: 3 - stage]:
                shift(half, 0, 0, stage, step)
        to_twin(half, 0, 0)
    own = pltpu.make_async_copy(
        block_ref, out_ref.at[(place.x * SIDE + place.z) * 2 + place.core], local_sem
    )
    own.start()
    order = [(3, 0), (1, 0), (0, 3), (0, 1), (2, 0), (3, 3), (3, 1), (1, 3), (1, 1), (0, 2)]
    order += [(3, 2), (1, 2), (2, 3), (2, 1), (2, 2)]
    for first, second in order:
        for half in range(2):
            wait(half, first, second)
            if second == 0:
                for step in (1, -1):
                    shift(half, first, second, 1, step)
            else:
                relay(half, first, second)
            to_twin(half, first, second)
    for first, second in [(0, 0)] + order:
        for half in range(2):
            sends.landed(
                view(half, first, second, 1 - place.core), twin_recv.at[half, first, second]
            )
    own.wait()
    sends.finish()


def gather_plane(tokens, gain, w_query, w_key, w_value):
    kind = tokens.dtype
    tok_rows = tokens.shape[0]
    width = GROUP * HEAD
    block = (GROUP, 2 * tok_rows, 2 * HEAD)
    shape = jax.ShapeDtypeStruct
    sem = pltpu.SemaphoreType.DMA
    return pl.pallas_call(
        gather_kernel,
        out_shape=(
            shape(tokens.shape, kind),
            shape((2 * tok_rows, width), kind),
            shape((2 * SIDE * SIDE,) + block, kind),
        ),
        in_specs=[VMEM] * 5,
        out_specs=(VMEM, VMEM, ANYWHERE),
        scratch_shapes=[
            pltpu.VMEM(block, kind),
            pltpu.VMEM((3, tok_rows, width), kind),
            pltpu.VMEM((3, tok_rows, width), kind),
            sem, sem((73,)), sem((2, SIDE, SIDE, 2)), sem((2, SIDE, SIDE)), sem,
        ],
        compiler_params=pltpu.CompilerParams(
            collective_id=1, has_side_effects=True, vmem_limit_bytes=60 * 1024 * 1024
        ),
        name="gather_plane",
    )(tokens, gain, w_query, w_key, w_value)


def ring_sum(sends, axis_of, sums, via, landing, via_recv, land_recv, ready):
    place = sends.place
    rows = sums.shape[-2] // 2
    middle = (slice(None),) * (len(sums.shape) - 4)

    def cut(ref, index, piece):
        return ref.at[index + middle + (pl.ds(piece * rows, rows),)]

    for half in range(2):
        ready(half, 2)
        for piece, step in ((0, 1), (1, SIDE - 1)):
            sends.go(
                place.turned(axis_of(half), step),
                cut(sums, (half, 2), piece),
                via.at[half, piece],
                via_recv.at[half, piece],
            )
    for half in range(2):
        for piece, step in ((0, 1), (1, SIDE - 1)):
            ready(half, step)
            sends.go(
                place.turned(axis_of(half), step),
                cut(sums, (half, step), 1 - piece),
                cut(landing, (half, piece), 1 - piece),
                land_recv.at[half, piece, 1 - piece],
            )
    for half in range(2):
        ready(half, 0)
    for half in range(2):
        for piece, step in ((0, 1), (1, SIDE - 1)):
            sends.landed(via.at[half, piece], via_recv.at[half, piece])
            spot = (half, step) + middle + (slice(piece * rows, (piece + 1) * rows),)
            sums[spot] = (wide(sums[spot]) + wide(via[half, piece])).astype(sums.dtype)
            sends.go(
                place.turned(axis_of(half), step),
                cut(sums, (half, step), piece),
                cut(landing, (half, piece), piece),
                land_recv.at[half, piece, piece],
            )

    def finish(half):
        for piece in range(2):
            for part in (1 - piece, piece):
                sends.landed(cut(landing, (half, piece), part), land_recv.at[half, piece, part])

    return finish


def ring_sum_direct(sends, axis_of, sums, landing, land_recv, ready):
    for step in (2, 1, 3):
        for half in range(2):
            ready(half, step)
            sends.go(
                sends.place.turned(axis_of(half), step),
                sums.at[half, step],
                landing.at[half, step - 1],
                land_recv.at[half, step - 1],
            )
    for half in range(2):
        ready(half, 0)

    def finish(half):
        for step in range(1, SIDE):
            sends.landed(landing.at[half, step - 1], land_recv.at[half, step - 1])

    return finish


def scatter_kernel(
    parts_ref, rows_ref, out_ref, mine, twin, sums, via_one, land_one, halves, land_two,
    both, other, rows_other,
    local_sem, send_sem, twin_recv, via_one_recv, land_one_recv, land_two_recv,
    far_recv,
):
    place = Place()
    half_rows = parts_ref.shape[4] // 2

    def source(half, group, core):
        rows = pl.ds(half * half_rows, half_rows)
        if half == 0:
            return parts_ref.at[group, :, core, :, rows]
        return parts_ref.at[:, group, core, :, rows]

    barrier = greet(ring_targets(place) + [place.at(dy=1)])
    loads = {}
    order = (2, 1, 3, 0)
    for step in order:
        for half in range(2):
            loads[half, step] = pltpu.make_async_copy(
                source(half, place.along(half, step), place.core),
                mine.at[half, step],
                local_sem.at[half, step],
            )
            loads[half, step].start()
    pl.semaphore_wait(*barrier)
    sends = Sends(place, send_sem)
    their_rows = pl.ds(pl.multiple_of((1 - place.y) * half_rows, half_rows), half_rows)
    sends.go(place.at(dy=1), rows_ref.at[their_rows], rows_other, far_recv.at[1])
    for step in order:
        for half in range(2):
            sends.go(
                place.at(dcore=1),
                source(half, place.along(half, step), 1 - place.core),
                twin.at[half, step],
                twin_recv.at[half, step],
            )

    def ready_one(half, step):
        loads[half, step].wait()
        sends.landed(twin.at[half, step], twin_recv.at[half, step])
        sums[half, step] = (wide(mine[half, step]) + wide(twin[half, step])).astype(sums.dtype)

    done_one = ring_sum(
        sends, lambda half: half, sums, via_one, land_one, via_one_recv, land_one_recv, ready_one
    )
    arrived = set()

    def ready_two(half, step):
        if half not in arrived:
            arrived.add(half)
            done_one(half)
        spot = place.along(1 - half, step)
        total = wide(sums[half, 0, spot])
        for side in range(2):
            total = total + wide(land_one[half, side, spot])
        halves[half, step] = total.astype(halves.dtype)

    done_two = ring_sum_direct(
        sends, lambda half: 1 - half, halves, land_two, land_two_recv, ready_two
    )
    for half in range(2):
        done_two(half)
        total = wide(halves[half, 0])
        for side in range(SIDE - 1):
            total = total + wide(land_two[half, side])
        total = total.astype(both.dtype)
        parts = [total[head, :, :HEAD] for head in range(GROUP)]
        parts += [total[head, :, HEAD:] for head in range(GROUP)]
        both[half] = jnp.concatenate(parts, axis=1)
    sends.go(place.at(dy=1), both.at[1 - place.y], other, far_recv.at[0])
    width = GROUP * HEAD
    mine_rows = pl.ds(pl.multiple_of(place.y * half_rows, half_rows), half_rows)
    kept = jnp.concatenate([rows_ref[mine_rows], both[place.y]], axis=1)
    sends.landed(rows_other, far_recv.at[1])
    sends.landed(other, far_recv.at[0])
    received = jnp.concatenate([rows_other[...], other[...]], axis=1)
    low = jnp.where(place.y == 0, kept, received)
    high = jnp.where(place.y == 0, received, kept)
    parts = []
    for n in range(3):
        parts += [low[:, n * width : (n + 1) * width], high[:, n * width : (n + 1) * width]]
    out_ref[...] = jnp.concatenate(parts, axis=1)
    sends.finish()


def scatter_plane(parts, rows_grad):
    heads, rows, lanes = parts.shape[1:]
    piece = (heads, rows // 2, lanes)
    small = (heads, rows // 4, lanes)
    kind = parts.dtype
    sem = pltpu.SemaphoreType.DMA
    return pl.pallas_call(
        scatter_kernel,
        out_shape=jax.ShapeDtypeStruct((rows // 2, 6 * rows_grad.shape[1]), kind),
        in_specs=[ANYWHERE, VMEM],
        out_specs=pl.BlockSpec(memory_space=pltpu.VMEM),
        scratch_shapes=[
            pltpu.VMEM((2, SIDE, SIDE) + piece, kind),
            pltpu.VMEM((2, SIDE, SIDE) + piece, kind),
            pltpu.VMEM((2, SIDE, SIDE) + piece, kind),
            pltpu.VMEM((2, 2, SIDE) + small, kind),
            pltpu.VMEM((2, 2, SIDE) + piece, kind),
            pltpu.VMEM((2, SIDE) + piece, kind),
            pltpu.VMEM((2, SIDE - 1) + piece, kind),
            pltpu.VMEM((2, rows // 2, 2 * rows_grad.shape[1]), kind),
            pltpu.VMEM((rows // 2, 2 * rows_grad.shape[1]), kind),
            pltpu.VMEM((rows // 2, rows_grad.shape[1]), kind),
            sem((2, SIDE)), sem((34,)), sem((2, SIDE)),
            sem((2, 2)), sem((2, 2, 2)), sem((2, SIDE - 1)), sem((2,)),
        ],
        compiler_params=pltpu.CompilerParams(
            collective_id=2, has_side_effects=True, vmem_limit_bytes=60 * 1024 * 1024
        ),
        name="scatter_plane",
    )(parts.reshape((SIDE, SIDE, 2) + parts.shape[1:]), rows_grad)


LANES = 128
UNIT = 16
UNITS = 9
BLOCK_ROWS = UNIT * (UNITS + 1)


def runs(slab_rows):
    found, unit = [], 0
    for slab, rows in enumerate(slab_rows):
        row = 0
        while row < rows:
            block, inside = divmod(unit, UNITS)
            take = min(UNITS - inside, (rows - row) // UNIT)
            found.append((slab, row, block, inside * UNIT, take * UNIT))
            row += take * UNIT
            unit += take
    return found


def block_at(block):
    return block // 32, block // 16 % 2, block // 4 % 4, block % 4


def weights_kernel(
    normed_ref, grads_ref, context_ref, attended_ref, router_ref, slab_ref, ffn_ref, w_query_ref,
    w_key_ref, w_value_ref, tokens_ref, hidden_ref, gain_ref,
    full, input_ref,
    share, share_other, parts, twin, sums, via_one, land_one, halves, land_two, other,
    send_sem, twin_recv, via_one_recv, land_one_recv, land_two_recv,
    far_recv, far_back_recv, two_back_recv, one_back_recv, twin_back_recv, share_recv,
):
    place = Place()
    width = context_ref.shape[1]
    barrier = greet(ring_targets(place) + [place.at(dy=1)], True)
    sends = Sends(place, send_sem)
    partial = jnp.zeros(share.shape, jnp.float32)
    for n, ref in enumerate((w_query_ref, w_key_ref, w_value_ref)):
        partial = partial + contract(grads_ref[:, n * width : (n + 1) * width], ref[...], 1, 1)
    share[...] = partial.astype(share.dtype)
    pl.semaphore_wait(*barrier)
    sends.across(share, share_other, share_recv)
    slabs, table = slab_table(normed_ref.shape[1], width)
    operands = ((normed_ref, grads_ref), (context_ref, attended_ref))
    for index, (output, lane) in enumerate(slabs):
        left, right = operands[output // 3]
        lane = lane if output == 3 else output * width + lane
        grad = contract(left[...], right[:, lane : lane + LANES], 0, 0).astype(parts.dtype)
        for slab, row, block, inside, rows in table:
            if slab == index:
                parts[block_at(block) + (slice(inside, inside + rows),)] = grad[row : row + rows]
    sends.landed(share_other, share_recv)
    grad_normed = wide(share[...]) + wide(share_other[...])
    floats_in = wide(tokens_ref[...])
    scale = lax.rsqrt(jnp.mean(floats_in * floats_in, axis=1, keepdims=True) + EPSILON)
    scaled = gain_ref[...][None] * grad_normed
    input_ref[...] = (
        hidden_ref[...]
        + scale * scaled
        - floats_in * scale**3 * jnp.mean(scaled * floats_in, axis=1, keepdims=True)
    )
    gain_sum = jnp.sum(grad_normed * floats_in * scale, axis=0, keepdims=True)
    tall = router_ref.shape[0] // 2
    router = jnp.concatenate([router_ref[:tall], router_ref[tall:]], axis=1)
    lines = [
        line[:, n : n + LANES]
        for line in (gain_sum, ffn_ref[...])
        for n in range(0, gain_sum.shape[1], LANES)
    ]
    lines.append(jnp.zeros((UNIT - len(lines), LANES), jnp.float32))
    small = [router[n : n + UNIT] for n in range(0, tall, UNIT)]
    small += [slab_ref[n : n + UNIT] for n in range(0, slab_ref.shape[0], UNIT)]
    small.append(jnp.concatenate(lines, axis=0))
    for block in range(64):
        part = small[block] if block < len(small) else jnp.zeros((UNIT, LANES), jnp.float32)
        parts[block_at(block) + (slice(UNIT * UNITS, BLOCK_ROWS),)] = part.astype(parts.dtype)

    order = (2, 1, 3, 0)
    for step in order:
        for half in range(2):
            sends.go(
                place.at(dcore=1),
                parts.at[half, 1 - place.core, place.along(half, step)],
                twin.at[half, step],
                twin_recv.at[half, step],
            )

    def ready_one(half, step):
        sends.landed(twin.at[half, step], twin_recv.at[half, step])
        own = parts[half, place.core, place.along(half, step)]
        sums[half, step] = (wide(own) + wide(twin[half, step])).astype(sums.dtype)

    done_one = ring_sum(
        sends, lambda half: half, sums, via_one, land_one, via_one_recv, land_one_recv, ready_one
    )
    arrived = set()

    def ready_two(half, step):
        if half not in arrived:
            arrived.add(half)
            done_one(half)
        spot = place.along(1 - half, step)
        total = wide(sums[half, 0, spot])
        for side in range(2):
            total = total + wide(land_one[half, side, spot])
        halves[half, step] = total.astype(halves.dtype)

    done_two = ring_sum_direct(
        sends, lambda half: 1 - half, halves, land_two, land_two_recv, ready_two
    )
    low = BLOCK_ROWS // 2
    for half in range(2):
        done_two(half)
        total = wide(halves[half, 0])
        for side in range(SIDE - 1):
            total = total + wide(land_two[half, side])
        halves[half, 0] = total.astype(halves.dtype)
        sends.go(
            place.at(dy=1),
            halves.at[half, 0, pl.ds(pl.multiple_of((1 - place.y) * low, UNIT), low)],
            other.at[half],
            far_recv.at[half],
        )

    def spot(half, core, first, second, rows=None):
        place_of = (half, core, place.along(half, first), place.along(1 - half, second))
        return full.at[place_of] if rows is None else full.at[place_of + (rows,)]

    def y_rows(y):
        return pl.ds(pl.multiple_of(y * low, UNIT), low)

    for half in range(2):
        sends.landed(other.at[half], far_recv.at[half])
        total = wide(halves[half, 0, y_rows(place.y)]) + wide(other[half])
        full[
            half, place.core, place.along(half, 0), place.along(1 - half, 0), y_rows(place.y)
        ] = total.astype(full.dtype)
        view = spot(half, place.core, 0, 0, y_rows(place.y))
        sends.go(place.at(dy=1), view, view, far_back_recv.at[half])

    subs = [pl.ds(piece * low, low) for piece in range(2)]
    for half in range(2):
        sends.landed(
            spot(half, place.core, 0, 0, y_rows(1 - place.y)), far_back_recv.at[half]
        )
        view = spot(half, place.core, 0, 0)
        for step in range(1, SIDE):
            sends.go(
                place.turned(1 - half, step), view, view, two_back_recv.at[half, SIDE - step]
            )

    def group(half, core, first, rows=None):
        if rows is None:
            return full.at[half, core, place.along(half, first)]
        return full.at[half, core, place.along(half, first), :, rows]

    for half in range(2):
        for step in range(1, SIDE):
            sends.landed(spot(half, place.core, 0, step), two_back_recv.at[half, step])
        view = group(half, place.core, 0)
        for step in (1, SIDE - 1):
            sends.go(place.turned(half, step), view, view, one_back_recv.at[half, SIDE - step, 0])
        sends.go(place.at(dcore=1), view, view, twin_back_recv.at[half, 0])
    for half in range(2):
        for piece, step in ((0, 1), (1, SIDE - 1)):
            view = group(half, place.core, SIDE - step)
            sends.landed(view, one_back_recv.at[half, SIDE - step, 0])
            part = group(half, place.core, SIDE - step, subs[piece])
            sends.go(place.turned(half, step), part, part, one_back_recv.at[half, 2, piece])
            sends.go(place.at(dcore=1), view, view, twin_back_recv.at[half, SIDE - step])
    for half in range(2):
        for piece in range(2):
            sends.landed(group(half, place.core, 2, subs[piece]), one_back_recv.at[half, 2, piece])
        view = group(half, place.core, 2)
        sends.go(place.at(dcore=1), view, view, twin_back_recv.at[half, 2])
    for first in (0, 3, 1, 2):
        for half in range(2):
            sends.landed(group(half, 1 - place.core, first), twin_back_recv.at[half, first])

    sends.finish()


def slab_table(tall, width):
    slabs = [(output, lane) for output in range(3) for lane in range(0, width, LANES)]
    slabs += [(3, lane) for lane in range(0, tall, LANES)]
    return slabs, runs([tall if output < 3 else width for output, _ in slabs])


def unpack_kernel(
    full, input_ref, mixed_ref,
    query_ref, key_ref, value_ref, proj_ref, router_ref, slab_ref, gains_ref, grad_input_ref,
    mixed_out_ref,
):
    grad_input_ref[...] = input_ref[...]
    mixed_out_ref[...] = mixed_ref[...]
    slabs, table = slab_table(query_ref.shape[0], query_ref.shape[1])
    for slab, row, block, inside, rows in table:
        output, lane = slabs[slab]
        ref = (query_ref, key_ref, value_ref, proj_ref)[output]
        ref[row : row + rows, lane : lane + LANES] = wide(
            full[block_at(block) + (slice(inside, inside + rows),)]
        )
    experts = router_ref.shape[0]
    tall = router_ref.shape[1] // 2

    def small(block):
        return wide(full[block_at(block) + (slice(UNIT * UNITS, BLOCK_ROWS),)])

    base = tall // UNIT
    turned = jnp.concatenate([small(block) for block in range(base)], axis=0).T
    router_ref[:, :tall] = turned[:experts]
    router_ref[:, tall:] = turned[experts:]
    heads, buckets = slab_ref.shape
    slab = [small(base + block) for block in range(buckets // UNIT)]
    slab_ref[...] = jnp.concatenate(slab, axis=0).T[:heads]
    gains_ref[...] = small(base + buckets // UNIT)


def weight_totals(
    normed, grads, context, attended, grad_router, slab, grad_ffn, weights, tokens, grad_hidden,
    gain, mixed,
):
    kind = jnp.bfloat16
    tall = normed.shape[1]
    local = context.shape[1]
    piece = (BLOCK_ROWS, LANES)
    part = (BLOCK_ROWS // 2, LANES)
    sem = pltpu.SemaphoreType.DMA
    floats = functools.partial(jax.ShapeDtypeStruct, dtype=jnp.float32)
    full, grad_input = pl.pallas_call(
        weights_kernel,
        out_shape=(
            jax.ShapeDtypeStruct((2, 2, SIDE, SIDE) + piece, kind),
            floats(tokens.shape),
        ),
        in_specs=[VMEM] * 13,
        out_specs=(VMEM,) * 2,
        scratch_shapes=[
            pltpu.VMEM(tokens.shape, kind),
            pltpu.VMEM(tokens.shape, kind),
            pltpu.VMEM((2, 2, SIDE, SIDE) + piece, kind),
            pltpu.VMEM((2, SIDE, SIDE) + piece, kind),
            pltpu.VMEM((2, SIDE, SIDE) + piece, kind),
            pltpu.VMEM((2, 2, SIDE) + part, kind),
            pltpu.VMEM((2, 2, SIDE) + piece, kind),
            pltpu.VMEM((2, SIDE) + piece, kind),
            pltpu.VMEM((2, SIDE - 1) + piece, kind),
            pltpu.VMEM((2,) + part, kind),
            sem((64,)), sem((2, SIDE)),
            sem((2, 2)), sem((2, 2, 2)), sem((2, SIDE - 1)),
            sem((2,)), sem((2,)), sem((2, SIDE)), sem((2, SIDE, 2)), sem((2, SIDE)), sem,
        ],
        compiler_params=pltpu.CompilerParams(
            collective_id=3, has_side_effects=True, vmem_limit_bytes=60 * 1024 * 1024
        ),
        name="weight_totals",
    )(
        normed, grads, context, attended, grad_router, slab, grad_ffn, *weights, tokens,
        grad_hidden, gain,
    )
    return pl.pallas_call(
        unpack_kernel,
        out_shape=(
            floats((tall, local)),
            floats((tall, local)),
            floats((tall, local)),
            floats((local, tall)),
            floats(grad_router.shape[::-1]),
            floats((local // HEAD, slab.shape[0])),
            floats((UNIT, LANES)),
            floats(tokens.shape),
            jax.ShapeDtypeStruct(tokens.shape, kind),
        ),
        in_specs=[VMEM] * 3,
        out_specs=(VMEM,) * 9,
        compiler_params=pltpu.CompilerParams(vmem_limit_bytes=60 * 1024 * 1024),
        name="unpack",
    )(full, grad_input, mixed)


QUARTERS = 4
STRIDE = 11


def gelu_pair(values):
    root = 0.7978845608028654
    cubic = 0.044715
    square = values * values
    bend = jnp.tanh(root * values * (1.0 + cubic * square))
    active = 0.5 * values * (1.0 + bend)
    slope = 0.5 * (1.0 + bend) + 0.5 * values * (1.0 - bend * bend) * root * (
        1.0 + 3.0 * cubic * square
    )
    return active, slope


def middle_kernel(
    both_ref, tokens_ref, cotangent_ref, proj_ref, gain_ref, router_ref, route_ref, slot_ref,
    w_in_hbm, w_out_hbm,
    mixed_ref, hidden_ref, attended_ref, context_ref, grad_both_ref, grad_router_ref,
    grad_gain_ref, rows_in_ref, rows_grad_ref, activ_ref, grad_pre_ref,
    w_in, w_out, swapped, share, share_other, order, order_t, gather_t, send_one, recv_one,
    send_two, recv_two, sums, sums_other, given,
    load_sem, send_sem, one_send, one_recv, two_send, two_recv, swap_recv, share_recv,
    sums_recv, back_recv,
):
    place = Place()
    me = place.me
    count = 2 * 2 * SIDE * SIDE
    loads = [
        pltpu.make_async_copy(w_in_hbm, w_in, load_sem.at[0]),
        pltpu.make_async_copy(w_out_hbm, w_out, load_sem.at[1]),
    ]
    for load in loads:
        load.start()
    barrier = pltpu.get_barrier_semaphore()

    @pl.loop(1, count)
    def _(step):
        pl.semaphore_signal(
            barrier,
            inc=1,
            device_id={"ctx": lax.rem(me + step, count)},
            device_id_type=pl.DeviceIdType.MESH,
        )

    pl.semaphore_signal(
        barrier,
        inc=1,
        device_id={"mp": 1 - lax.axis_index("mp")},
        device_id_type=pl.DeviceIdType.MESH,
    )
    pl.semaphore_wait(barrier, count)
    sends = Sends(place, send_sem)
    tok_rows = tokens_ref.shape[0]
    first = place.y == 0

    mine = pl.ds(pl.multiple_of(place.y * tok_rows, tok_rows), tok_rows)
    theirs = pl.ds(pl.multiple_of((1 - place.y) * tok_rows, tok_rows), tok_rows)
    sends.go(place.at(dy=1), both_ref.at[theirs], swapped, swap_recv)
    kept = both_ref[mine]
    sends.landed(swapped, swap_recv)
    received = swapped[...]
    context = jnp.concatenate(
        [jnp.where(first, kept, received), jnp.where(first, received, kept)], axis=1
    )
    context_ref[...] = context
    share[...] = contract(context, proj_ref[...], 1, 0).astype(share.dtype)
    sends.across(share, share_other, share_recv)
    spots = tok_rows * QUARTERS
    cells = 16 * count
    route = route_ref[...].astype(jnp.float32)
    spot = route * 16.0 + slot_ref[...].astype(jnp.float32)
    square = (tok_rows, tok_rows)
    diagonal = lax.broadcasted_iota(jnp.int32, square, 0) == lax.broadcasted_iota(
        jnp.int32, square, 1
    )

    def column(line):
        return jnp.sum(jnp.where(diagonal, line, 0.0), axis=1, keepdims=True).astype(jnp.int32)

    spot_row = jnp.concatenate(
        [spot.astype(jnp.int32) + 4 * n for n in range(QUARTERS)], axis=1
    )
    spot_col = column(spot)
    gather = jnp.where(
        lax.broadcasted_iota(jnp.int32, (cells, spots), 0) == spot_row, 1.0, 0.0
    ).astype(jnp.bfloat16)
    sends.landed(share_other, share_recv)
    hidden = wide(tokens_ref[...]) + (wide(share[...]) + wide(share_other[...]))
    scale = lax.rsqrt(jnp.mean(hidden * hidden, axis=1, keepdims=True) + EPSILON)
    normed = hidden * scale * gain_ref[...][None]
    logits = lax.dot_general(
        normed, router_ref[...], (((1,), (1,)), ((), ())), precision=PRECISE,
        preferred_element_type=jnp.float32,
    )
    shifted = jnp.exp(logits - jnp.max(logits, axis=1, keepdims=True))
    probs = shifted / jnp.sum(shifted, axis=1, keepdims=True)
    chosen = jnp.where(
        column(route) == lax.broadcasted_iota(jnp.int32, probs.shape, 1), 1.0, 0.0
    )
    gate = jnp.sum(probs * chosen, axis=1, keepdims=True)
    grad_y = wide(cotangent_ref[...])
    width = 2 * tokens_ref.shape[1] // QUARTERS
    payload = [normed[:, :width], normed[:, width:]]
    payload += [gate * grad_y[:, :width], gate * grad_y[:, width:]]
    payload = jnp.concatenate(payload, axis=0).astype(jnp.bfloat16)
    send_one[...] = (
        contract(gather, payload, 1, 0).astype(send_one.dtype).reshape(send_one.shape)
    )

    def exchange(src, dst, send, recv):
        @pl.loop(1, count)
        def _(step):
            target = lax.rem(me + step * STRIDE, count)
            sender(target, src.at[target], dst.at[me], send, recv).start()

        dst[me] = src[me]

    def arrive(dst, recv):
        others = dst.at[pl.ds(0, count - 1)]
        sends.landed(others, recv)

    exchange(send_one, recv_one, one_send, one_recv)
    rows = cells // QUARTERS

    def cell_of(index):
        row = index & (rows - 1)
        return (row >> 2) * 16 + (index >> 8) * 4 + (row & 3)

    down = lax.broadcasted_iota(jnp.int32, (cells, cells), 0)
    right = lax.broadcasted_iota(jnp.int32, (cells, cells), 1)
    order[...] = jnp.where(cell_of(down) == right, 1.0, 0.0).astype(order.dtype)
    order_t[...] = jnp.where(down == cell_of(right), 1.0, 0.0).astype(order_t.dtype)
    cell = lax.broadcasted_iota(jnp.int32, (tok_rows, cells), 1)
    for n in range(QUARTERS):
        gather_t[n * tok_rows : (n + 1) * tok_rows] = jnp.where(
            spot_col + 4 * n == cell, 1.0, 0.0
        ).astype(gather_t.dtype)
    for load in loads:
        load.wait()
    arrive(recv_one, one_recv)

    got = contract(order[...], recv_one[...].reshape(cells, width), 1, 0).astype(jnp.bfloat16)
    rows_in_ref[...] = jnp.concatenate([got[:rows], got[rows : 2 * rows]], axis=1)
    rows_grad_ref[...] = jnp.concatenate([got[2 * rows : 3 * rows], got[3 * rows :]], axis=1)
    hidden_units = w_in.shape[1]
    chunk = hidden_units // 3
    out = jnp.zeros(rows_in_ref.shape, jnp.float32)
    back = jnp.zeros(rows_in_ref.shape, jnp.float32)
    for start in range(0, hidden_units, chunk):
        units = slice(start, start + chunk)
        active, slope = gelu_pair(contract(rows_in_ref[...], w_in[:, units], 1, 0))
        active = active.astype(jnp.bfloat16)
        activ_ref[:, units] = active
        out = out + contract(active, w_out[units], 1, 0)
        grad_pre = (contract(rows_grad_ref[...], w_out[units], 1, 1) * slope).astype(jnp.bfloat16)
        grad_pre_ref[:, units] = grad_pre
        back = back + contract(grad_pre, w_in[:, units], 1, 1)
    whole = [out[:, :width], out[:, width:], back[:, :width], back[:, width:]]
    whole = jnp.concatenate(whole, axis=0).astype(jnp.bfloat16)
    send_two[...] = (
        contract(order_t[...], whole, 1, 0).astype(send_two.dtype).reshape(send_two.shape)
    )
    exchange(send_two, recv_two, two_send, two_recv)
    arrive(recv_two, two_recv)
    sums[...] = contract(gather_t[...], recv_two[...].reshape(cells, width), 1, 0).astype(
        sums.dtype
    )
    sends.across(sums, sums_other, sums_recv)
    sends.landed(sums_other, sums_recv)
    total = wide(sums[...]) + wide(sums_other[...])
    parts = [total[n * tok_rows : (n + 1) * tok_rows] for n in range(QUARTERS)]
    expert_rows = jnp.concatenate(parts[:2], axis=1).astype(jnp.bfloat16).astype(jnp.float32)
    grad_sent = jnp.concatenate(parts[2:], axis=1).astype(jnp.bfloat16).astype(jnp.float32)

    mixed_ref[...] = (hidden + gate * expert_rows).astype(mixed_ref.dtype)
    grad_gate = jnp.sum(grad_y * expert_rows, axis=1, keepdims=True)
    grad_logits = grad_gate * gate * (chosen - probs)
    grad_router_ref[...] = lax.dot_general(
        normed, grad_logits, (((0,), (0,)), ((), ())), precision=PRECISE,
        preferred_element_type=jnp.float32,
    )
    grad_normed = grad_sent + lax.dot_general(
        grad_logits, router_ref[...], (((1,), (0,)), ((), ())), precision=PRECISE,
        preferred_element_type=jnp.float32,
    )
    scaled = gain_ref[...][None] * grad_normed
    grad_gain_ref[...] = jnp.sum(grad_normed * hidden * scale, axis=0, keepdims=True)
    grad_hidden = (
        grad_y
        + scale * scaled
        - hidden * scale**3 * jnp.mean(scaled * hidden, axis=1, keepdims=True)
    )
    hidden_ref[...] = grad_hidden
    attended = grad_hidden.astype(jnp.bfloat16)
    attended_ref[...] = attended
    grad_context = contract(attended, proj_ref[...], 1, 1).astype(jnp.bfloat16)
    half = grad_context.shape[1] // 2
    left, right_part = grad_context[:, :half], grad_context[:, half:]
    given[...] = jnp.where(first, right_part, left)
    grad_both_ref[mine] = jnp.where(first, left, right_part)
    sends.go(place.at(dy=1), given, grad_both_ref.at[mine], back_recv)
    sends.landed(grad_both_ref.at[theirs], back_recv)
    sends.finish()

    for src, send in ((send_one, one_send), (send_two, two_send)):
        others = src.at[pl.ds(0, count - 1)]
        sender(me, others, others, send, send).wait_send()


def middle(
    both, tokens, cotangent, w_proj, gain, router, w_in, w_out, route, slot
):
    kind = jnp.bfloat16
    tok_rows, wide_row = tokens.shape
    count = router.shape[0]
    rows = 4 * count
    hidden = w_in.shape[1]
    width = 2 * wide_row // QUARTERS
    spots = QUARTERS * tok_rows
    shape = jax.ShapeDtypeStruct
    sem = pltpu.SemaphoreType.DMA
    buffer = pltpu.VMEM((count, 16, width), kind)
    return pl.pallas_call(
        middle_kernel,
        out_shape=(
            shape(tokens.shape, kind),
            shape(tokens.shape, jnp.float32),
            shape(tokens.shape, kind),
            shape((tok_rows, 2 * both.shape[1]), kind),
            shape(both.shape, kind),
            shape(router.shape[::-1], jnp.float32),
            shape((1, wide_row), jnp.float32),
            shape((rows, wide_row), kind),
            shape((rows, wide_row), kind),
            shape((rows, hidden), kind),
            shape((rows, hidden), kind),
        ),
        in_specs=[VMEM] * 8 + [ANYWHERE] * 2,
        out_specs=(VMEM,) * 11,
        scratch_shapes=[
            pltpu.VMEM(w_in.shape, kind),
            pltpu.VMEM(w_out.shape, kind),
            pltpu.VMEM((tok_rows, both.shape[1]), kind),
            pltpu.VMEM(tokens.shape, kind),
            pltpu.VMEM(tokens.shape, kind),
            pltpu.VMEM((16 * count, 16 * count), kind),
            pltpu.VMEM((16 * count, 16 * count), kind),
            pltpu.VMEM((spots, 16 * count), kind),
            buffer, buffer, buffer, buffer,
            pltpu.VMEM((spots, width), kind),
            pltpu.VMEM((spots, width), kind),
            pltpu.VMEM((tok_rows, both.shape[1]), kind),
            sem((2,)), sem((4,)), sem, sem, sem, sem, sem, sem, sem, sem,
        ],
        compiler_params=pltpu.CompilerParams(
            collective_id=4, has_side_effects=True, vmem_limit_bytes=60 * 1024 * 1024
        ),
        name="middle",
    )(
        both, tokens, cotangent, w_proj, gain, router, route[None], slot[None], w_in, w_out,
    )


def shards(
    tokens,
    attn_gain,
    w_query,
    w_key,
    w_value,
    w_proj,
    rel_table,
    rel_bucket,
    ffn_gain,
    router,
    w_in,
    w_out,
    expert_route,
    expert_slot,
    cotangent,
):
    me = lax.axis_index("ctx")
    side = 2 * SIDE * SIDE
    place = jnp.stack([me % side, me // side]).astype(jnp.int32)
    normed, rows, held = gather_plane(tokens, attn_gain, w_query, w_key, w_value)

    buckets = jnp.pad(rel_bucket, (0, 1), constant_values=31).reshape(BLOCK, BLOCK)
    both, turned, lse, flipped, table, uneven = attend(place, rel_table.T, buckets, held, rows)
    (
        mixed, grad_hidden1, grad_attended, context, grad_both, grad_router, grad_ffn_gain,
        rows_in, rows_grad, activ, grad_pre,
    ) = middle(
        both, tokens, cotangent, w_proj, ffn_gain, router.T, w_in[0], w_out[0], expert_route,
        expert_slot,
    )
    grad_parts, grad_rows, slab, grad_expert_in, grad_expert_out = attend_back(
        place, uneven, table, held, rows, grad_both, turned, lse, flipped, rows_in, rows_grad,
        activ, grad_pre, rel_table.shape[0],
    )
    grads = scatter_plane(grad_parts, grad_rows)
    (
        grad_query, grad_key, grad_value, grad_proj, grad_router, grad_table, gains, grad_input,
        mixed,
    ) = weight_totals(
        normed, grads, context, grad_attended, grad_router, slab, grad_ffn_gain,
        (w_query, w_key, w_value), tokens, grad_hidden1, attn_gain, mixed,
    )
    lines = tokens.shape[1] // LANES
    return (
        mixed,
        grad_input,
        gains[:lines].reshape(-1),
        grad_query,
        grad_key,
        grad_value,
        grad_proj,
        grad_table.T,
        gains[lines : 2 * lines].reshape(-1),
        grad_router.T,
        grad_expert_in[None],
        grad_expert_out[None],
    )


def solution(mesh):
    return jax.shard_map(
        shards,
        mesh=mesh,
        in_specs=(
            P("ctx", None),
            P(),
            P(None, "mp"),
            P(None, "mp"),
            P(None, "mp"),
            P("mp", None),
            P(None, "mp"),
            P(),
            P(),
            P(),
            P("ctx", None, "mp"),
            P("ctx", "mp", None),
            P("ctx"),
            P("ctx"),
            P("ctx", None),
        ),
        out_specs=(
            P("ctx", None),
            P("ctx", None),
            P(),
            P(None, "mp"),
            P(None, "mp"),
            P(None, "mp"),
            P("mp", None),
            P(None, "mp"),
            P(),
            P(),
            P("ctx", None, "mp"),
            P("ctx", "mp", None),
        ),
        check_vma=False,
    )
```

```python
import functools
import jax
import jax.numpy as jnp
from jax import lax
from jax.experimental import pallas as pl
from jax.experimental.pallas import tpu as pltpu
from jax.sharding import PartitionSpec as P

HEAD = 64
GROUP = 3
BLOCK = 128
PAIR = 2 * BLOCK
FORWARD_SPAN = 8
BACKWARD_SPAN = 4
VMEM = pl.BlockSpec(memory_space=pltpu.VMEM)
SMEM = pl.BlockSpec(memory_space=pltpu.SMEM)
LARGE = pltpu.CompilerParams(vmem_limit_bytes=60 * 1024 * 1024)


def contract(left, right, left_dim, right_dim):
    return lax.dot_general(
        left,
        right,
        (((left_dim,), (right_dim,)), ((), ())),
        preferred_element_type=jnp.float32,
    )


def window_row(place, chunk, tile, half, span):
    return 63 - (span * chunk + tile // 2) + place + BLOCK // 4 * (half - tile % 2)


def tile_consts(table_ref, head, place, chunk, tile, span):
    parts = []
    for half in range(2):
        row = window_row(place, chunk, tile, half, span)
        parts.append(jnp.broadcast_to(table_ref[head, pl.ds(row, 1), 0:1], (1, BLOCK)))
    return jnp.concatenate(parts, axis=1)


def chunk_mixed(uneven_ref, place, chunk, span):
    mixed = 0
    for tile in range(2 * span):
        for half in range(2):
            mixed = mixed + uneven_ref[0, window_row(place, chunk, tile, half, span)]
    return mixed


def add_uneven(table_ref, uneven_ref, score_ref, place, chunk, span):
    for tile in range(2 * span):
        for half in range(2):
            row = window_row(place, chunk, tile, half, span)

            @pl.when(uneven_ref[0, row] > 0)
            def _():
                for head in range(GROUP):
                    window = jnp.concatenate(
                        [table_ref[head, pl.ds(row, 1), :], table_ref[head, pl.ds(row + 1, 1), :]],
                        axis=1,
                    )
                    window = window - window[:, 0:1]
                    grid = pltpu.roll(
                        jnp.broadcast_to(window, (BLOCK, PAIR)),
                        BLOCK,
                        1,
                        stride=1,
                        stride_axis=0,
                    )[:, :BLOCK]
                    rows = slice(tile * BLOCK, (tile + 1) * BLOCK)
                    cols = slice(half * BLOCK, (half + 1) * BLOCK)
                    score_ref[head, rows, cols] += grid


def stream(keys_hbm, held_ref, sems, span):
    def copy(chunk):
        slot = lax.rem(chunk, 2)
        return pltpu.make_async_copy(
            keys_hbm.at[pl.ds(chunk * span, span)], held_ref.at[slot], sems.at[slot]
        )

    return copy


def head_columns(ref, head):
    return ref[:, head * HEAD : (head + 1) * HEAD]


def turn(values):
    return values.astype(jnp.float32).T


def fill_turned(dst_ref, src_ref, first):
    for head in range(GROUP):
        part = turn(head_columns(src_ref, head))
        none = jnp.zeros_like(part)
        parts = [part, none] if first else [none, part]
        dst_ref[head] = jnp.concatenate(parts, axis=0).astype(dst_ref.dtype)


def fill_padded(dst_ref, src_ref, first):
    for head in range(GROUP):
        part = head_columns(src_ref, head)
        none = jnp.zeros_like(part)
        parts = [part, none] if first else [none, part]
        dst_ref[head] = jnp.concatenate(parts, axis=1)


def side_by_side(parts):
    return jnp.concatenate([turn(part) for part in parts], axis=1).astype(jnp.bfloat16)


def flip_both(values):
    down = lax.broadcasted_iota(jnp.int32, (BLOCK, BLOCK), 0)
    right = lax.broadcasted_iota(jnp.int32, (BLOCK, BLOCK), 1)
    anti = jnp.where(down + right == BLOCK - 1, 1.0, 0.0).astype(jnp.bfloat16)
    once = contract(anti, values.astype(jnp.float32).astype(jnp.bfloat16), 1, 0)
    return contract(once.astype(jnp.bfloat16), anti, 1, 0).astype(jnp.int32)


def line_of(column):
    down = lax.broadcasted_iota(jnp.int32, (BLOCK, BLOCK), 0)
    right = lax.broadcasted_iota(jnp.int32, (BLOCK, BLOCK), 1)
    return jnp.sum(jnp.where(down == right, column, 0.0), axis=0, keepdims=True)


def shifted_up(column):
    return jnp.concatenate([column[1:], column[-1:]], axis=0)


def forward_kernel(
    place_ref, rel_ref, buckets_ref, keys_hbm, rows_ref,
    out_ref, turned_ref, lse_ref, flipped_ref, table_ref, uneven_out_ref,
    held_ref, held_sem, uneven_ref, uneven_sem,
    query_ref, best_ref, sum_ref, total_ref, score_ref,
):
    place = place_ref[0]
    span = FORWARD_SPAN
    tiles, length = 2 * span, PAIR * span
    fetch = stream(keys_hbm, held_ref, held_sem, span)
    chunks = keys_hbm.shape[0] // span
    fetch(0).start()
    flipped = flip_both(buckets_ref[...])
    flipped_ref[...] = flipped
    floats = flipped.astype(jnp.float32)
    high = jnp.max(floats, axis=1, keepdims=True)
    low = jnp.min(floats, axis=1, keepdims=True)
    high = jnp.maximum(high, shifted_up(high))
    low = jnp.minimum(low, shifted_up(low))
    uneven_out_ref[...] = line_of(jnp.where(high > low, 1.0, 0.0)).astype(jnp.int32)
    flags = pltpu.make_async_copy(uneven_out_ref, uneven_ref, uneven_sem)
    flags.start()
    for head in range(GROUP):
        values = jnp.zeros((BLOCK, BLOCK), jnp.float32)
        for bucket in range(rel_ref.shape[1]):
            value = rel_ref[place_ref[1] * GROUP + head, bucket]
            values = jnp.where(flipped == bucket, value, values)
        table_ref[head] = values
    fill_turned(query_ref, rows_ref, True)
    flags.wait()
    best_ref[...] = jnp.full_like(best_ref, -1e30)
    sum_ref[...] = jnp.zeros_like(sum_ref)
    total_ref[...] = jnp.zeros_like(total_ref)

    def rest(chunk, head, held, scores):
        consts = [tile_consts(table_ref, head, place, chunk, tile, span) for tile in range(tiles)]
        old = best_ref[head]
        new = old
        for tile in range(tiles):
            part = scores[tile * BLOCK : (tile + 1) * BLOCK]
            new = jnp.maximum(new, jnp.max(part, axis=0, keepdims=True) + consts[tile])
        decay = jnp.exp(old - new)
        weights = [
            jnp.exp(scores[tile * BLOCK : (tile + 1) * BLOCK] - (new - consts[tile]))
            for tile in range(tiles)
        ]
        weights = jnp.concatenate(weights, axis=0)
        sum_ref[head] = sum_ref[head] * decay + jnp.sum(weights, axis=0, keepdims=True)
        best_ref[head] = new
        total_ref[head] = total_ref[head] * decay + contract(
            held, weights.astype(jnp.bfloat16), 0, 0
        )

    @pl.loop(0, chunks)
    def _(chunk):
        slot = lax.rem(chunk, 2)
        fetch(chunk).wait()

        @pl.when(chunk + 1 < chunks)
        def _():
            fetch(chunk + 1).start()

        def held_of(head):
            return held_ref[slot, :, head].reshape(length, 2 * HEAD)

        mixed = chunk_mixed(uneven_ref, place, chunk, span)

        @pl.when(mixed == 0)
        def _():
            helds = [held_of(head) for head in range(GROUP)]
            scores = [contract(helds[head], query_ref[head], 1, 0) for head in range(GROUP)]
            for head in range(GROUP):
                rest(chunk, head, helds[head], scores[head])

        @pl.when(mixed > 0)
        def _():
            for head in range(GROUP):
                score_ref[head] = contract(held_of(head), query_ref[head], 1, 0)
            add_uneven(table_ref, uneven_ref, score_ref, place, chunk, span)
            for head in range(GROUP):
                rest(chunk, head, held_of(head), score_ref[head])

    for head in range(GROUP):
        turned_ref[head] = total_ref[head][HEAD:] / sum_ref[head]
    out_ref[...] = side_by_side([turned_ref[head] for head in range(GROUP)])
    for head in range(GROUP):
        lse_ref[head] = best_ref[head] + jnp.log(sum_ref[head])


def backward_kernel(
    place_ref, uneven_ref, table_ref, keys_hbm, rows_ref, grads_ref, turned_ref, lse_ref,
    flipped_ref, rows_in_ref, rows_grad_ref, activ_ref, grad_pre_ref,
    grad_keys_hbm, grad_rows_ref, slab_ref, expert_in_hbm, expert_out_hbm,
    held_ref, held_sem, grad_keys_ref, grad_keys_sem, expert_in, expert_out, expert_sem, offsets_ref, query_t_ref, grad_t_ref, query_ref, grad_ref, delta_ref, grad_query_ref, score_ref,
):
    place = place_ref[0]
    span = BACKWARD_SPAN
    tiles, length = 2 * span, PAIR * span
    fetch = stream(keys_hbm, held_ref, held_sem, span)
    chunks = keys_hbm.shape[0] // span
    fetch(0).start()

    def give(chunk):
        slot = lax.rem(chunk, 2)
        return pltpu.make_async_copy(
            grad_keys_ref.at[slot],
            grad_keys_hbm.at[pl.ds(chunk * span, span)],
            grad_keys_sem.at[slot],
        )

    expert_in[...] = contract(rows_in_ref[...], grad_pre_ref[...], 0, 0)
    expert_out[...] = contract(activ_ref[...], rows_grad_ref[...], 0, 0)
    stores = [
        pltpu.make_async_copy(expert_in, expert_in_hbm, expert_sem.at[0]),
        pltpu.make_async_copy(expert_out, expert_out_hbm, expert_sem.at[1]),
    ]
    for store in stores:
        store.start()
    fill_turned(query_t_ref, rows_ref, True)
    fill_turned(grad_t_ref, grads_ref, False)
    fill_padded(query_ref, rows_ref, True)
    fill_padded(grad_ref, grads_ref, False)
    for head in range(GROUP):
        delta_ref[head] = jnp.sum(
            grad_t_ref[head][HEAD:].astype(jnp.float32) * turned_ref[head], axis=0, keepdims=True
        )
    grad_query_ref[...] = jnp.zeros_like(grad_query_ref)
    offsets_ref[...] = jnp.zeros_like(offsets_ref)

    def rest(chunk, head, held, scores, grads):
        probs = jnp.concatenate(
            [
                jnp.exp(
                    scores[tile * BLOCK : (tile + 1) * BLOCK]
                    - (lse_ref[head] - tile_consts(table_ref, head, place, chunk, tile, span))
                )
                for tile in range(tiles)
            ],
            axis=0,
        )
        slopes = probs * (grads - delta_ref[head])
        rounded = slopes.astype(jnp.bfloat16)
        part = contract(rounded, query_ref[head], 1, 0) + contract(
            probs.astype(jnp.bfloat16), grad_ref[head], 1, 0
        )
        grad_keys_ref[lax.rem(chunk, 2), :, head] = part.astype(grad_keys_ref.dtype).reshape(
            span, PAIR, 2 * HEAD
        )
        grad_query_ref[head] += contract(held, rounded, 0, 0)
        return slopes

    def put_even(chunk, head, tile, half, slopes):
        row = window_row(place, chunk, tile, half, span)
        offsets_ref[head, pl.ds(row, 1), :] += jnp.sum(slopes, axis=0, keepdims=True)

    def put_uneven(chunk, head, tile, half, slopes):
        row = window_row(place, chunk, tile, half, span)
        wide = jnp.concatenate([slopes, jnp.zeros_like(slopes)], axis=1)
        folded = jnp.zeros((8, PAIR), jnp.float32)
        for group in range(BLOCK // 8):
            folded = folded + pltpu.roll(
                wide[group * 8 : (group + 1) * 8], (BLOCK - 8 * group) % PAIR, 1
            )
        line = jnp.zeros((1, PAIR), jnp.float32)
        for step in range(8):
            line = line + pltpu.roll(folded, (PAIR - step) % PAIR, 1)[step : step + 1]
        offsets_ref[head, pl.ds(row, 1), :] += line[:, :BLOCK]
        offsets_ref[head, pl.ds(row + 1, 1), :] += line[:, BLOCK:]

    @pl.loop(0, chunks)
    def _(chunk):
        slot = lax.rem(chunk, 2)
        fetch(chunk).wait()

        @pl.when(chunk + 1 < chunks)
        def _():
            fetch(chunk + 1).start()

        def held_of(head):
            return held_ref[slot, :, head].reshape(length, 2 * HEAD)

        @pl.when(chunk >= 2)
        def _():
            give(chunk - 2).wait()

        mixed = chunk_mixed(uneven_ref, place, chunk, span)

        @pl.when(mixed == 0)
        def _():
            helds = [held_of(head) for head in range(GROUP)]
            scores = [contract(helds[head], query_t_ref[head], 1, 0) for head in range(GROUP)]
            grads = [contract(helds[head], grad_t_ref[head], 1, 0) for head in range(GROUP)]
            for head in range(GROUP):
                slopes = rest(chunk, head, helds[head], scores[head], grads[head])
                for tile in range(tiles):
                    for half in range(2):
                        part = slopes[
                            tile * BLOCK : (tile + 1) * BLOCK, half * BLOCK : (half + 1) * BLOCK
                        ]
                        put_even(chunk, head, tile, half, part)

        @pl.when(mixed > 0)
        def _():
            for head in range(GROUP):
                score_ref[head] = contract(held_of(head), query_t_ref[head], 1, 0)
            add_uneven(table_ref, uneven_ref, score_ref, place, chunk, span)
            for head in range(GROUP):
                held = held_of(head)
                grads = contract(held, grad_t_ref[head], 1, 0)
                score_ref[head] = rest(chunk, head, held, score_ref[head], grads)
            for tile in range(tiles):
                for half in range(2):
                    rows = slice(tile * BLOCK, (tile + 1) * BLOCK)
                    cols = slice(half * BLOCK, (half + 1) * BLOCK)
                    uneven = uneven_ref[0, window_row(place, chunk, tile, half, span)]

                    @pl.when(uneven == 0)
                    def _():
                        for head in range(GROUP):
                            put_even(chunk, head, tile, half, score_ref[head, rows, cols])

                    @pl.when(uneven > 0)
                    def _():
                        for head in range(GROUP):
                            put_uneven(chunk, head, tile, half, score_ref[head, rows, cols])

        give(chunk).start()

    for chunk in (chunks - 2, chunks - 1):
        give(chunk).wait()
    grad_rows_ref[...] = side_by_side([grad_query_ref[head][:HEAD] for head in range(GROUP)])
    lanes = lax.broadcasted_iota(jnp.int32, (1, BLOCK), 1)
    for bucket in range(slab_ref.shape[0]):
        hit = flipped_ref[...] == bucket
        line = jnp.zeros((1, BLOCK), jnp.float32)
        for head in range(GROUP):
            part = jnp.sum(jnp.where(hit, offsets_ref[head], 0.0), axis=0, keepdims=True)
            part = jnp.sum(part, axis=1, keepdims=True)
            line = jnp.where(lanes == place_ref[1] * GROUP + head, part, line)
        slab_ref[pl.ds(bucket, 1)] = line
    for store in stores:
        store.wait()


def attend(place, rel_table, buckets, keys, rows):
    shape = jax.ShapeDtypeStruct
    anywhere = pl.BlockSpec(memory_space=pl.ANY)
    return pl.pallas_call(
        forward_kernel,
        out_shape=(
            shape(rows.shape, jnp.bfloat16),
            shape((GROUP, HEAD, PAIR), jnp.float32),
            shape((GROUP, 1, PAIR), jnp.float32),
            shape((BLOCK, BLOCK), jnp.int32),
            shape((GROUP, BLOCK, BLOCK), jnp.float32),
            shape((1, BLOCK), jnp.int32),
        ),
        in_specs=[SMEM, SMEM, VMEM, anywhere, VMEM],
        out_specs=(VMEM,) * 6,
        scratch_shapes=[
            pltpu.VMEM((2, FORWARD_SPAN) + keys.shape[1:], keys.dtype),
            pltpu.SemaphoreType.DMA((2,)),
            pltpu.SMEM((1, BLOCK), jnp.int32),
            pltpu.SemaphoreType.DMA,
            pltpu.VMEM((GROUP, 2 * HEAD, PAIR), jnp.bfloat16),
            pltpu.VMEM((GROUP, 1, PAIR), jnp.float32),
            pltpu.VMEM((GROUP, 1, PAIR), jnp.float32),
            pltpu.VMEM((GROUP, 2 * HEAD, PAIR), jnp.float32),
            pltpu.VMEM((GROUP, FORWARD_SPAN * PAIR, PAIR), jnp.float32),
        ],
        compiler_params=LARGE,
        name="attend",
    )(place, rel_table, buckets, keys, rows)


def attend_back(
    place, uneven, table, keys, rows, grads, turned, lse, flipped, rows_in, rows_grad, activ,
    grad_pre, buckets,
):
    shape = jax.ShapeDtypeStruct
    wide_row, hidden = rows_in.shape[1], activ.shape[1]
    anywhere = pl.BlockSpec(memory_space=pl.ANY)
    return pl.pallas_call(
        backward_kernel,
        out_shape=(
            shape(keys.shape, jnp.bfloat16),
            shape(rows.shape, jnp.bfloat16),
            shape((buckets, BLOCK), jnp.float32),
            shape((wide_row, hidden), jnp.float32),
            shape((hidden, wide_row), jnp.float32),
        ),
        in_specs=[SMEM, SMEM, VMEM, anywhere] + [VMEM] * 9,
        out_specs=(anywhere, VMEM, VMEM, anywhere, anywhere),
        scratch_shapes=[
            pltpu.VMEM((2, BACKWARD_SPAN) + keys.shape[1:], keys.dtype),
            pltpu.SemaphoreType.DMA((2,)),
            pltpu.VMEM((2, BACKWARD_SPAN) + keys.shape[1:], keys.dtype),
            pltpu.SemaphoreType.DMA((2,)),
            pltpu.VMEM((wide_row, hidden), jnp.float32),
            pltpu.VMEM((hidden, wide_row), jnp.float32),
            pltpu.SemaphoreType.DMA((2,)),
            pltpu.VMEM((GROUP, BLOCK, BLOCK), jnp.float32),
            pltpu.VMEM((GROUP, 2 * HEAD, PAIR), jnp.bfloat16),
            pltpu.VMEM((GROUP, 2 * HEAD, PAIR), jnp.bfloat16),
            pltpu.VMEM((GROUP, PAIR, 2 * HEAD), jnp.bfloat16),
            pltpu.VMEM((GROUP, PAIR, 2 * HEAD), jnp.bfloat16),
            pltpu.VMEM((GROUP, 1, PAIR), jnp.float32),
            pltpu.VMEM((GROUP, 2 * HEAD, PAIR), jnp.float32),
            pltpu.VMEM((GROUP, BACKWARD_SPAN * PAIR, PAIR), jnp.float32),
        ],
        compiler_params=LARGE,
        name="attend_back",
    )(
        place, uneven, table, keys, rows, grads, turned, lse, flipped, rows_in, rows_grad, activ,
        grad_pre,
    )


EPSILON = 1e-06
PRECISE = lax.Precision.HIGHEST
ANYWHERE = pl.BlockSpec(memory_space=pl.ANY)
SIDE = 4


class Place:
    def __init__(self):
        self.me = lax.axis_index("ctx")
        self.core = lax.rem(self.me, 2)
        self.z = lax.rem(self.me // 2, SIDE)
        self.x = lax.rem(self.me // (2 * SIDE), SIDE)
        self.y = self.me // (2 * SIDE * SIDE)

    def at(self, dx=0, dz=0, dcore=0, dy=0):
        x = lax.rem(self.x + dx, SIDE)
        z = lax.rem(self.z + dz, SIDE)
        core = lax.rem(self.core + dcore, 2)
        y = lax.rem(self.y + dy, 2)
        return ((y * SIDE + x) * SIDE + z) * 2 + core

    def turned(self, axis, step):
        return self.at(dx=step) if axis == 0 else self.at(dz=step)

    def along(self, axis, step):
        return lax.rem((self.x if axis == 0 else self.z) + step, SIDE)


def greet(targets, across=False):
    barrier = pltpu.get_barrier_semaphore()
    if across:
        pl.semaphore_signal(
            barrier,
            inc=1,
            device_id={"mp": 1 - lax.axis_index("mp")},
            device_id_type=pl.DeviceIdType.MESH,
        )
    for target in targets:
        pl.semaphore_signal(
            barrier, inc=1, device_id={"ctx": target}, device_id_type=pl.DeviceIdType.MESH
        )
    return barrier, len(targets) + int(across)


def meet(targets, across=False):
    pl.semaphore_wait(*greet(targets, across))


def ring_targets(place):
    found = [place.at(dcore=1)]
    for step in range(1, SIDE):
        found += [place.at(dx=step), place.at(dz=step)]
    return found


def sender(target, src, dst, send_sem, recv_sem):
    return pltpu.make_async_remote_copy(
        src_ref=src,
        dst_ref=dst,
        send_sem=send_sem,
        recv_sem=recv_sem,
        device_id={"ctx": target},
        device_id_type=pl.DeviceIdType.MESH,
    )


def wide(value):
    return value.astype(jnp.float32)


class Sends:
    def __init__(self, place, sems):
        self.place, self.sems, self.started = place, sems, []

    def go(self, target, src, dst, recv_sem):
        copy = sender(target, src, dst, self.sems.at[len(self.started)], recv_sem)
        copy.start()
        self.started.append(copy)
        return copy

    def across(self, src, dst, recv_sem):
        copy = pltpu.make_async_remote_copy(
            src_ref=src,
            dst_ref=dst,
            send_sem=self.sems.at[len(self.started)],
            recv_sem=recv_sem,
            device_id={"mp": 1 - lax.axis_index("mp")},
            device_id_type=pl.DeviceIdType.MESH,
        )
        copy.start()
        self.started.append(copy)

    def landed(self, view, sem):
        sender(self.place.me, view, view, sem, sem).wait_recv()

    def finish(self):
        for copy in self.started:
            copy.wait_send()


def gather_kernel(
    tokens_ref, gain_ref, w_query_ref, w_key_ref, w_value_ref,
    normed_ref, rows_ref, out_ref,
    block_ref, given, other, local_sem, send_sem, ring_recv, twin_recv, swap_recv,
):
    place = Place()
    barrier = greet(ring_targets(place) + [place.at(dy=1)])
    sends = Sends(place, send_sem)
    half_rows = block_ref.shape[1] // 2
    sub_rows = half_rows // 2
    first = place.y == 0
    width = GROUP * HEAD
    floats_in = wide(tokens_ref[...])
    scale = lax.rsqrt(jnp.mean(floats_in * floats_in, axis=1, keepdims=True) + EPSILON)
    normed = (floats_in * scale * gain_ref[...][None]).astype(normed_ref.dtype)
    normed_ref[...] = normed
    kept = []
    for n, ref in enumerate((w_query_ref, w_key_ref, w_value_ref)):
        made = contract(normed, ref[...], 1, 0).astype(given.dtype)
        kept.append(jnp.where(first, made[:, :width], made[:, width:]))
        given[n] = jnp.where(first, made[:, width:], made[:, :width])

    def rows_at(half, start=0, count=half_rows):
        side = place.y if half == 0 else 1 - place.y
        return pl.ds(pl.multiple_of(side * half_rows + start, sub_rows), count)

    def put(half, query, key, value):
        rows_ref[rows_at(half)] = query
        for head in range(GROUP):
            lanes = slice(head * HEAD, (head + 1) * HEAD)
            block_ref[head, rows_at(half)] = jnp.concatenate(
                [key[:, lanes], value[:, lanes]], axis=1
            )

    put(0, *kept)
    pl.semaphore_wait(*barrier)
    sends.go(place.at(dy=1), given, other, swap_recv)

    def rows_of(half, piece):
        if piece is None:
            return rows_at(half)
        return rows_at(half, piece * sub_rows, sub_rows)

    def view(half, first, second, core, piece=None):
        x, z = (second, first) if half == 0 else (first, second)
        slot = (place.along(0, x) * SIDE + place.along(1, z)) * 2 + core
        return out_ref.at[slot, :, rows_of(half, piece)]

    def held(half, first, second, piece=None):
        if first == 0 and second == 0:
            return block_ref.at[:, rows_of(half, piece)]
        return view(half, first, second, place.core, piece)

    def shift(half, first, second, stage, step, piece=None):
        axis = 1 - half if stage == 0 else half
        if stage == 0:
            slot = ((first - step) % SIDE, second)
        else:
            slot = (first, (second - step) % SIDE)
        sends.go(
            place.turned(axis, step % SIDE),
            held(half, first, second, piece),
            view(half, first, second, place.core, piece),
            ring_recv.at[half, slot[0], slot[1], piece or 0],
        )

    def whole(dx, dz, core):
        return out_ref.at[(place.along(0, dx) * SIDE + place.along(1, dz)) * 2 + core]

    def to_twin(dx, dz):
        src = block_ref if dx == 0 and dz == 0 else whole(dx, dz, place.core)
        sends.go(place.at(dcore=1), src, whole(dx, dz, place.core), twin_recv.at[dx, dz])

    def wait(half, first, second):
        if second == 2:
            for piece in range(2):
                sends.landed(
                    view(half, first, second, place.core, piece),
                    ring_recv.at[half, first, second, piece],
                )
        else:
            sends.landed(
                view(half, first, second, place.core), ring_recv.at[half, first, second, 0]
            )

    def relay(half, first, second):
        if second == SIDE - 1:
            shift(half, first, second, 1, 1, 0)
        elif second == 1:
            shift(half, first, second, 1, -1, 1)

    for half in range(2):
        if half == 1:
            sends.landed(other, swap_recv)
            put(1, other[0], other[1], other[2])
        for stage in range(2):
            for step in (1, -1, 2)[: 3 - stage]:
                shift(half, 0, 0, stage, step)
    to_twin(0, 0)
    own = pltpu.make_async_copy(
        block_ref, out_ref.at[(place.x * SIDE + place.z) * 2 + place.core], local_sem
    )
    own.start()
    order = [(3, 0), (1, 0), (0, 3), (0, 1), (2, 0), (3, 3), (3, 1), (1, 3), (1, 1), (0, 2)]
    order += [(3, 2), (1, 2), (2, 3), (2, 1), (2, 2)]
    passed = set()
    for first, second in order:
        for half in range(2):
            wait(half, first, second)
            if second == 0:
                for step in (1, -1):
                    shift(half, first, second, 1, step)
            else:
                relay(half, first, second)
        passed.add((first, second))
        if (second, first) in passed:
            for dx, dz in sorted({(first, second), (second, first)}):
                to_twin(dx, dz)
    for dx, dz in [(0, 0)] + order:
        sends.landed(whole(dx, dz, 1 - place.core), twin_recv.at[dx, dz])
    own.wait()
    sends.finish()


def gather_plane(tokens, gain, w_query, w_key, w_value):
    kind = tokens.dtype
    tok_rows = tokens.shape[0]
    width = GROUP * HEAD
    block = (GROUP, 2 * tok_rows, 2 * HEAD)
    shape = jax.ShapeDtypeStruct
    sem = pltpu.SemaphoreType.DMA
    return pl.pallas_call(
        gather_kernel,
        out_shape=(
            shape(tokens.shape, kind),
            shape((2 * tok_rows, width), kind),
            shape((2 * SIDE * SIDE,) + block, kind),
        ),
        in_specs=[VMEM] * 5,
        out_specs=(VMEM, VMEM, ANYWHERE),
        scratch_shapes=[
            pltpu.VMEM(block, kind),
            pltpu.VMEM((3, tok_rows, width), kind),
            pltpu.VMEM((3, tok_rows, width), kind),
            sem, sem((73,)), sem((2, SIDE, SIDE, 2)), sem((SIDE, SIDE)), sem,
        ],
        compiler_params=pltpu.CompilerParams(
            collective_id=1, has_side_effects=True, vmem_limit_bytes=60 * 1024 * 1024
        ),
        name="gather_plane",
    )(tokens, gain, w_query, w_key, w_value)


def ring_sum(sends, axis_of, sums, via, landing, via_recv, land_recv, ready):
    place = sends.place
    rows = sums.shape[-2] // 2
    middle = (slice(None),) * (len(sums.shape) - 4)

    def cut(ref, index, piece):
        return ref.at[index + middle + (pl.ds(piece * rows, rows),)]

    for half in range(2):
        ready(half, 2)
        for piece, step in ((0, 1), (1, SIDE - 1)):
            sends.go(
                place.turned(axis_of(half), step),
                cut(sums, (half, 2), piece),
                via.at[half, piece],
                via_recv.at[half, piece],
            )
    for half in range(2):
        for piece, step in ((0, 1), (1, SIDE - 1)):
            ready(half, step)
            sends.go(
                place.turned(axis_of(half), step),
                cut(sums, (half, step), 1 - piece),
                cut(landing, (half, piece), 1 - piece),
                land_recv.at[half, piece, 1 - piece],
            )
    for half in range(2):
        ready(half, 0)
    for half in range(2):
        for piece, step in ((0, 1), (1, SIDE - 1)):
            sends.landed(via.at[half, piece], via_recv.at[half, piece])
            spot = (half, step) + middle + (slice(piece * rows, (piece + 1) * rows),)
            sums[spot] = (wide(sums[spot]) + wide(via[half, piece])).astype(sums.dtype)
            sends.go(
                place.turned(axis_of(half), step),
                cut(sums, (half, step), piece),
                cut(landing, (half, piece), piece),
                land_recv.at[half, piece, piece],
            )

    def finish(half):
        for piece in range(2):
            for part in (1 - piece, piece):
                sends.landed(cut(landing, (half, piece), part), land_recv.at[half, piece, part])

    return finish


def ring_sum_direct(sends, axis_of, sums, landing, land_recv, ready):
    for step in (2, 1, 3):
        for half in range(2):
            ready(half, step)
            sends.go(
                sends.place.turned(axis_of(half), step),
                sums.at[half, step],
                landing.at[half, step - 1],
                land_recv.at[half, step - 1],
            )
    for half in range(2):
        ready(half, 0)

    def finish(half):
        for step in range(1, SIDE):
            sends.landed(landing.at[half, step - 1], land_recv.at[half, step - 1])

    return finish


def scatter_kernel(
    parts_ref, rows_ref, out_ref, mine, twin, sums, via_one, land_one, halves, land_two,
    both, other, rows_other,
    local_sem, send_sem, twin_recv, via_one_recv, land_one_recv, land_two_recv,
    far_recv,
):
    place = Place()
    half_rows = parts_ref.shape[4] // 2

    def source(half, group, core):
        rows = pl.ds(half * half_rows, half_rows)
        if half == 0:
            return parts_ref.at[group, :, core, :, rows]
        return parts_ref.at[:, group, core, :, rows]

    barrier = greet(ring_targets(place) + [place.at(dy=1)])
    loads = {}
    order = (2, 1, 3, 0)
    for step in order:
        for half in range(2):
            loads[half, step] = pltpu.make_async_copy(
                source(half, place.along(half, step), place.core),
                mine.at[half, step],
                local_sem.at[half, step],
            )
            loads[half, step].start()
    pl.semaphore_wait(*barrier)
    sends = Sends(place, send_sem)
    their_rows = pl.ds(pl.multiple_of((1 - place.y) * half_rows, half_rows), half_rows)
    sends.go(place.at(dy=1), rows_ref.at[their_rows], rows_other, far_recv.at[1])
    for step in order:
        for half in range(2):
            sends.go(
                place.at(dcore=1),
                source(half, place.along(half, step), 1 - place.core),
                twin.at[half, step],
                twin_recv.at[half, step],
            )

    def ready_one(half, step):
        loads[half, step].wait()
        sends.landed(twin.at[half, step], twin_recv.at[half, step])
        sums[half, step] = (wide(mine[half, step]) + wide(twin[half, step])).astype(sums.dtype)

    done_one = ring_sum(
        sends, lambda half: half, sums, via_one, land_one, via_one_recv, land_one_recv, ready_one
    )
    arrived = set()

    def ready_two(half, step):
        if half not in arrived:
            arrived.add(half)
            done_one(half)
        spot = place.along(1 - half, step)
        total = wide(sums[half, 0, spot])
        for side in range(2):
            total = total + wide(land_one[half, side, spot])
        halves[half, step] = total.astype(halves.dtype)

    done_two = ring_sum_direct(
        sends, lambda half: 1 - half, halves, land_two, land_two_recv, ready_two
    )
    for half in range(2):
        done_two(half)
        total = wide(halves[half, 0])
        for side in range(SIDE - 1):
            total = total + wide(land_two[half, side])
        total = total.astype(both.dtype)
        parts = [total[head, :, :HEAD] for head in range(GROUP)]
        parts += [total[head, :, HEAD:] for head in range(GROUP)]
        both[half] = jnp.concatenate(parts, axis=1)
    sends.go(place.at(dy=1), both.at[1 - place.y], other, far_recv.at[0])
    width = GROUP * HEAD
    mine_rows = pl.ds(pl.multiple_of(place.y * half_rows, half_rows), half_rows)
    kept = jnp.concatenate([rows_ref[mine_rows], both[place.y]], axis=1)
    sends.landed(rows_other, far_recv.at[1])
    sends.landed(other, far_recv.at[0])
    received = jnp.concatenate([rows_other[...], other[...]], axis=1)
    low = jnp.where(place.y == 0, kept, received)
    high = jnp.where(place.y == 0, received, kept)
    parts = []
    for n in range(3):
        parts += [low[:, n * width : (n + 1) * width], high[:, n * width : (n + 1) * width]]
    out_ref[...] = jnp.concatenate(parts, axis=1)
    sends.finish()


def scatter_plane(parts, rows_grad):
    heads, rows, lanes = parts.shape[1:]
    piece = (heads, rows // 2, lanes)
    small = (heads, rows // 4, lanes)
    kind = parts.dtype
    sem = pltpu.SemaphoreType.DMA
    return pl.pallas_call(
        scatter_kernel,
        out_shape=jax.ShapeDtypeStruct((rows // 2, 6 * rows_grad.shape[1]), kind),
        in_specs=[ANYWHERE, VMEM],
        out_specs=pl.BlockSpec(memory_space=pltpu.VMEM),
        scratch_shapes=[
            pltpu.VMEM((2, SIDE, SIDE) + piece, kind),
            pltpu.VMEM((2, SIDE, SIDE) + piece, kind),
            pltpu.VMEM((2, SIDE, SIDE) + piece, kind),
            pltpu.VMEM((2, 2, SIDE) + small, kind),
            pltpu.VMEM((2, 2, SIDE) + piece, kind),
            pltpu.VMEM((2, SIDE) + piece, kind),
            pltpu.VMEM((2, SIDE - 1) + piece, kind),
            pltpu.VMEM((2, rows // 2, 2 * rows_grad.shape[1]), kind),
            pltpu.VMEM((rows // 2, 2 * rows_grad.shape[1]), kind),
            pltpu.VMEM((rows // 2, rows_grad.shape[1]), kind),
            sem((2, SIDE)), sem((34,)), sem((2, SIDE)),
            sem((2, 2)), sem((2, 2, 2)), sem((2, SIDE - 1)), sem((2,)),
        ],
        compiler_params=pltpu.CompilerParams(
            collective_id=2, has_side_effects=True, vmem_limit_bytes=60 * 1024 * 1024
        ),
        name="scatter_plane",
    )(parts.reshape((SIDE, SIDE, 2) + parts.shape[1:]), rows_grad)


LANES = 128
UNIT = 16
UNITS = 9
BLOCK_ROWS = UNIT * (UNITS + 1)


def runs(slab_rows):
    found, unit = [], 0
    for slab, rows in enumerate(slab_rows):
        row = 0
        while row < rows:
            block, inside = divmod(unit, UNITS)
            take = min(UNITS - inside, (rows - row) // UNIT)
            found.append((slab, row, block, inside * UNIT, take * UNIT))
            row += take * UNIT
            unit += take
    return found


def block_at(block):
    return block // 32, block // 16 % 2, block // 4 % 4, block % 4


def weights_kernel(
    normed_ref, grads_ref, context_ref, attended_ref, router_ref, slab_ref, ffn_ref, w_query_ref,
    w_key_ref, w_value_ref, tokens_ref, hidden_ref, gain_ref,
    full, input_ref,
    share, share_other, parts, twin, sums, via_one, land_one, halves, land_two, other,
    send_sem, twin_recv, via_one_recv, land_one_recv, land_two_recv,
    far_recv, far_back_recv, two_back_recv, one_back_recv, twin_back_recv, share_recv,
):
    place = Place()
    width = context_ref.shape[1]
    barrier = greet(ring_targets(place) + [place.at(dy=1)], True)
    sends = Sends(place, send_sem)
    partial = jnp.zeros(share.shape, jnp.float32)
    for n, ref in enumerate((w_query_ref, w_key_ref, w_value_ref)):
        partial = partial + contract(grads_ref[:, n * width : (n + 1) * width], ref[...], 1, 1)
    share[...] = partial.astype(share.dtype)
    pl.semaphore_wait(*barrier)
    sends.across(share, share_other, share_recv)
    slabs, table = slab_table(normed_ref.shape[1], width)
    operands = ((normed_ref, grads_ref), (context_ref, attended_ref))
    for index, (output, lane) in enumerate(slabs):
        left, right = operands[output // 3]
        lane = lane if output == 3 else output * width + lane
        grad = contract(left[...], right[:, lane : lane + LANES], 0, 0).astype(parts.dtype)
        for slab, row, block, inside, rows in table:
            if slab == index:
                parts[block_at(block) + (slice(inside, inside + rows),)] = grad[row : row + rows]
    sends.landed(share_other, share_recv)
    grad_normed = wide(share[...]) + wide(share_other[...])
    floats_in = wide(tokens_ref[...])
    scale = lax.rsqrt(jnp.mean(floats_in * floats_in, axis=1, keepdims=True) + EPSILON)
    scaled = gain_ref[...][None] * grad_normed
    input_ref[...] = (
        hidden_ref[...]
        + scale * scaled
        - floats_in * scale**3 * jnp.mean(scaled * floats_in, axis=1, keepdims=True)
    )
    gain_sum = jnp.sum(grad_normed * floats_in * scale, axis=0, keepdims=True)
    tall = router_ref.shape[0] // 2
    router = jnp.concatenate([router_ref[:tall], router_ref[tall:]], axis=1)
    lines = [
        line[:, n : n + LANES]
        for line in (gain_sum, ffn_ref[...])
        for n in range(0, gain_sum.shape[1], LANES)
    ]
    lines.append(jnp.zeros((UNIT - len(lines), LANES), jnp.float32))
    small = [router[n : n + UNIT] for n in range(0, tall, UNIT)]
    small += [slab_ref[n : n + UNIT] for n in range(0, slab_ref.shape[0], UNIT)]
    small.append(jnp.concatenate(lines, axis=0))
    for block in range(64):
        part = small[block] if block < len(small) else jnp.zeros((UNIT, LANES), jnp.float32)
        parts[block_at(block) + (slice(UNIT * UNITS, BLOCK_ROWS),)] = part.astype(parts.dtype)

    order = (2, 1, 3, 0)
    for step in order:
        for half in range(2):
            sends.go(
                place.at(dcore=1),
                parts.at[half, 1 - place.core, place.along(half, step)],
                twin.at[half, step],
                twin_recv.at[half, step],
            )

    def ready_one(half, step):
        sends.landed(twin.at[half, step], twin_recv.at[half, step])
        own = parts[half, place.core, place.along(half, step)]
        sums[half, step] = (wide(own) + wide(twin[half, step])).astype(sums.dtype)

    done_one = ring_sum(
        sends, lambda half: half, sums, via_one, land_one, via_one_recv, land_one_recv, ready_one
    )
    arrived = set()

    def ready_two(half, step):
        if half not in arrived:
            arrived.add(half)
            done_one(half)
        spot = place.along(1 - half, step)
        total = wide(sums[half, 0, spot])
        for side in range(2):
            total = total + wide(land_one[half, side, spot])
        halves[half, step] = total.astype(halves.dtype)

    done_two = ring_sum_direct(
        sends, lambda half: 1 - half, halves, land_two, land_two_recv, ready_two
    )
    low = BLOCK_ROWS // 2
    for half in range(2):
        done_two(half)
        total = wide(halves[half, 0])
        for side in range(SIDE - 1):
            total = total + wide(land_two[half, side])
        halves[half, 0] = total.astype(halves.dtype)
        sends.go(
            place.at(dy=1),
            halves.at[half, 0, pl.ds(pl.multiple_of((1 - place.y) * low, UNIT), low)],
            other.at[half],
            far_recv.at[half],
        )

    def spot(half, core, first, second, rows=None):
        place_of = (half, core, place.along(half, first), place.along(1 - half, second))
        return full.at[place_of] if rows is None else full.at[place_of + (rows,)]

    def y_rows(y):
        return pl.ds(pl.multiple_of(y * low, UNIT), low)

    for half in range(2):
        sends.landed(other.at[half], far_recv.at[half])
        total = wide(halves[half, 0, y_rows(place.y)]) + wide(other[half])
        full[
            half, place.core, place.along(half, 0), place.along(1 - half, 0), y_rows(place.y)
        ] = total.astype(full.dtype)
        view = spot(half, place.core, 0, 0, y_rows(place.y))
        sends.go(place.at(dy=1), view, view, far_back_recv.at[half])

    subs = [pl.ds(piece * low, low) for piece in range(2)]
    for half in range(2):
        sends.landed(
            spot(half, place.core, 0, 0, y_rows(1 - place.y)), far_back_recv.at[half]
        )
        view = spot(half, place.core, 0, 0)
        for step in range(1, SIDE):
            sends.go(
                place.turned(1 - half, step), view, view, two_back_recv.at[half, SIDE - step]
            )

    def group(half, core, first, rows=None):
        if rows is None:
            return full.at[half, core, place.along(half, first)]
        return full.at[half, core, place.along(half, first), :, rows]

    for half in range(2):
        for step in range(1, SIDE):
            sends.landed(spot(half, place.core, 0, step), two_back_recv.at[half, step])
        view = group(half, place.core, 0)
        for step in (1, SIDE - 1):
            sends.go(place.turned(half, step), view, view, one_back_recv.at[half, SIDE - step, 0])
        sends.go(place.at(dcore=1), view, view, twin_back_recv.at[half, 0])
    for half in range(2):
        for piece, step in ((0, 1), (1, SIDE - 1)):
            view = group(half, place.core, SIDE - step)
            sends.landed(view, one_back_recv.at[half, SIDE - step, 0])
            part = group(half, place.core, SIDE - step, subs[piece])
            sends.go(place.turned(half, step), part, part, one_back_recv.at[half, 2, piece])
            sends.go(place.at(dcore=1), view, view, twin_back_recv.at[half, SIDE - step])
    for half in range(2):
        for piece in range(2):
            sends.landed(group(half, place.core, 2, subs[piece]), one_back_recv.at[half, 2, piece])
        view = group(half, place.core, 2)
        sends.go(place.at(dcore=1), view, view, twin_back_recv.at[half, 2])
    for first in (0, 3, 1, 2):
        for half in range(2):
            sends.landed(group(half, 1 - place.core, first), twin_back_recv.at[half, first])

    sends.finish()


def slab_table(tall, width):
    slabs = [(output, lane) for output in range(3) for lane in range(0, width, LANES)]
    slabs += [(3, lane) for lane in range(0, tall, LANES)]
    return slabs, runs([tall if output < 3 else width for output, _ in slabs])


def unpack_kernel(
    full, input_ref, mixed_ref,
    query_ref, key_ref, value_ref, proj_ref, router_ref, slab_ref, gains_ref, grad_input_ref,
    mixed_out_ref,
):
    grad_input_ref[...] = input_ref[...]
    mixed_out_ref[...] = mixed_ref[...]
    slabs, table = slab_table(query_ref.shape[0], query_ref.shape[1])
    for slab, row, block, inside, rows in table:
        output, lane = slabs[slab]
        ref = (query_ref, key_ref, value_ref, proj_ref)[output]
        ref[row : row + rows, lane : lane + LANES] = wide(
            full[block_at(block) + (slice(inside, inside + rows),)]
        )
    experts = router_ref.shape[0]
    tall = router_ref.shape[1] // 2

    def small(block):
        return wide(full[block_at(block) + (slice(UNIT * UNITS, BLOCK_ROWS),)])

    base = tall // UNIT
    turned = jnp.concatenate([small(block) for block in range(base)], axis=0).T
    router_ref[:, :tall] = turned[:experts]
    router_ref[:, tall:] = turned[experts:]
    heads, buckets = slab_ref.shape
    slab = [small(base + block) for block in range(buckets // UNIT)]
    slab_ref[...] = jnp.concatenate(slab, axis=0).T[:heads]
    gains_ref[...] = small(base + buckets // UNIT)


def weight_totals(
    normed, grads, context, attended, grad_router, slab, grad_ffn, weights, tokens, grad_hidden,
    gain, mixed,
):
    kind = jnp.bfloat16
    tall = normed.shape[1]
    local = context.shape[1]
    piece = (BLOCK_ROWS, LANES)
    part = (BLOCK_ROWS // 2, LANES)
    sem = pltpu.SemaphoreType.DMA
    floats = functools.partial(jax.ShapeDtypeStruct, dtype=jnp.float32)
    full, grad_input = pl.pallas_call(
        weights_kernel,
        out_shape=(
            jax.ShapeDtypeStruct((2, 2, SIDE, SIDE) + piece, kind),
            floats(tokens.shape),
        ),
        in_specs=[VMEM] * 13,
        out_specs=(VMEM,) * 2,
        scratch_shapes=[
            pltpu.VMEM(tokens.shape, kind),
            pltpu.VMEM(tokens.shape, kind),
            pltpu.VMEM((2, 2, SIDE, SIDE) + piece, kind),
            pltpu.VMEM((2, SIDE, SIDE) + piece, kind),
            pltpu.VMEM((2, SIDE, SIDE) + piece, kind),
            pltpu.VMEM((2, 2, SIDE) + part, kind),
            pltpu.VMEM((2, 2, SIDE) + piece, kind),
            pltpu.VMEM((2, SIDE) + piece, kind),
            pltpu.VMEM((2, SIDE - 1) + piece, kind),
            pltpu.VMEM((2,) + part, kind),
            sem((64,)), sem((2, SIDE)),
            sem((2, 2)), sem((2, 2, 2)), sem((2, SIDE - 1)),
            sem((2,)), sem((2,)), sem((2, SIDE)), sem((2, SIDE, 2)), sem((2, SIDE)), sem,
        ],
        compiler_params=pltpu.CompilerParams(
            collective_id=3, has_side_effects=True, vmem_limit_bytes=60 * 1024 * 1024
        ),
        name="weight_totals",
    )(
        normed, grads, context, attended, grad_router, slab, grad_ffn, *weights, tokens,
        grad_hidden, gain,
    )
    return pl.pallas_call(
        unpack_kernel,
        out_shape=(
            floats((tall, local)),
            floats((tall, local)),
            floats((tall, local)),
            floats((local, tall)),
            floats(grad_router.shape[::-1]),
            floats((local // HEAD, slab.shape[0])),
            floats((UNIT, LANES)),
            floats(tokens.shape),
            jax.ShapeDtypeStruct(tokens.shape, kind),
        ),
        in_specs=[VMEM] * 3,
        out_specs=(VMEM,) * 9,
        compiler_params=pltpu.CompilerParams(vmem_limit_bytes=60 * 1024 * 1024),
        name="unpack",
    )(full, grad_input, mixed)


QUARTERS = 4
STRIDE = 11


def gelu_pair(values):
    root = 0.7978845608028654
    cubic = 0.044715
    square = values * values
    bend = jnp.tanh(root * values * (1.0 + cubic * square))
    active = 0.5 * values * (1.0 + bend)
    slope = 0.5 * (1.0 + bend) + 0.5 * values * (1.0 - bend * bend) * root * (
        1.0 + 3.0 * cubic * square
    )
    return active, slope


def middle_kernel(
    both_ref, tokens_ref, cotangent_ref, proj_ref, gain_ref, router_ref, route_ref, slot_ref,
    w_in_hbm, w_out_hbm,
    mixed_ref, hidden_ref, attended_ref, context_ref, grad_both_ref, grad_router_ref,
    grad_gain_ref, rows_in_ref, rows_grad_ref, activ_ref, grad_pre_ref,
    w_in, w_out, swapped, share, share_other, order, order_t, gather_t, send_one, recv_one,
    send_two, recv_two, sums, sums_other, given,
    load_sem, send_sem, one_send, one_recv, two_send, two_recv, swap_recv, share_recv,
    sums_recv, back_recv,
):
    place = Place()
    me = place.me
    count = 2 * 2 * SIDE * SIDE
    loads = [
        pltpu.make_async_copy(w_in_hbm, w_in, load_sem.at[0]),
        pltpu.make_async_copy(w_out_hbm, w_out, load_sem.at[1]),
    ]
    for load in loads:
        load.start()
    barrier = pltpu.get_barrier_semaphore()

    @pl.loop(1, count)
    def _(step):
        pl.semaphore_signal(
            barrier,
            inc=1,
            device_id={"ctx": lax.rem(me + step, count)},
            device_id_type=pl.DeviceIdType.MESH,
        )

    pl.semaphore_signal(
        barrier,
        inc=1,
        device_id={"mp": 1 - lax.axis_index("mp")},
        device_id_type=pl.DeviceIdType.MESH,
    )
    tok_rows = tokens_ref.shape[0]
    spots = tok_rows * QUARTERS
    cells = 16 * count
    route = route_ref[...].astype(jnp.float32)
    spot = route * 16.0 + slot_ref[...].astype(jnp.float32)
    square = (tok_rows, tok_rows)
    diagonal = lax.broadcasted_iota(jnp.int32, square, 0) == lax.broadcasted_iota(
        jnp.int32, square, 1
    )

    def column(line):
        return jnp.sum(jnp.where(diagonal, line, 0.0), axis=1, keepdims=True).astype(jnp.int32)

    spot_row = jnp.concatenate(
        [spot.astype(jnp.int32) + 4 * n for n in range(QUARTERS)], axis=1
    )
    spot_col = column(spot)
    gather = jnp.where(
        lax.broadcasted_iota(jnp.int32, (cells, spots), 0) == spot_row, 1.0, 0.0
    ).astype(jnp.bfloat16)
    pl.semaphore_wait(barrier, count)
    sends = Sends(place, send_sem)
    first = place.y == 0

    mine = pl.ds(pl.multiple_of(place.y * tok_rows, tok_rows), tok_rows)
    theirs = pl.ds(pl.multiple_of((1 - place.y) * tok_rows, tok_rows), tok_rows)
    sends.go(place.at(dy=1), both_ref.at[theirs], swapped, swap_recv)
    kept = both_ref[mine]
    sends.landed(swapped, swap_recv)
    received = swapped[...]
    context = jnp.concatenate(
        [jnp.where(first, kept, received), jnp.where(first, received, kept)], axis=1
    )
    context_ref[...] = context
    share[...] = contract(context, proj_ref[...], 1, 0).astype(share.dtype)
    sends.across(share, share_other, share_recv)
    sends.landed(share_other, share_recv)
    hidden = wide(tokens_ref[...]) + (wide(share[...]) + wide(share_other[...]))
    scale = lax.rsqrt(jnp.mean(hidden * hidden, axis=1, keepdims=True) + EPSILON)
    normed = hidden * scale * gain_ref[...][None]
    logits = lax.dot_general(
        normed, router_ref[...], (((1,), (1,)), ((), ())), precision=PRECISE,
        preferred_element_type=jnp.float32,
    )
    shifted = jnp.exp(logits - jnp.max(logits, axis=1, keepdims=True))
    probs = shifted / jnp.sum(shifted, axis=1, keepdims=True)
    chosen = jnp.where(
        column(route) == lax.broadcasted_iota(jnp.int32, probs.shape, 1), 1.0, 0.0
    )
    gate = jnp.sum(probs * chosen, axis=1, keepdims=True)
    grad_y = wide(cotangent_ref[...])
    width = 2 * tokens_ref.shape[1] // QUARTERS
    payload = [normed[:, :width], normed[:, width:]]
    payload += [gate * grad_y[:, :width], gate * grad_y[:, width:]]
    payload = jnp.concatenate(payload, axis=0).astype(jnp.bfloat16)
    send_one[...] = (
        contract(gather, payload, 1, 0).astype(send_one.dtype).reshape(send_one.shape)
    )

    def exchange(src, dst, send, recv):
        @pl.loop(1, count)
        def _(step):
            target = lax.rem(me + step * STRIDE, count)
            sender(target, src.at[target], dst.at[me], send, recv).start()

        dst[me] = src[me]

    def arrive(dst, recv):
        others = dst.at[pl.ds(0, count - 1)]
        sends.landed(others, recv)

    exchange(send_one, recv_one, one_send, one_recv)
    rows = cells // QUARTERS

    def cell_of(index):
        row = index & (rows - 1)
        return (row >> 2) * 16 + (index >> 8) * 4 + (row & 3)

    down = lax.broadcasted_iota(jnp.int32, (cells, cells), 0)
    right = lax.broadcasted_iota(jnp.int32, (cells, cells), 1)
    order[...] = jnp.where(cell_of(down) == right, 1.0, 0.0).astype(order.dtype)
    order_t[...] = jnp.where(down == cell_of(right), 1.0, 0.0).astype(order_t.dtype)
    cell = lax.broadcasted_iota(jnp.int32, (tok_rows, cells), 1)
    for n in range(QUARTERS):
        gather_t[n * tok_rows : (n + 1) * tok_rows] = jnp.where(
            spot_col + 4 * n == cell, 1.0, 0.0
        ).astype(gather_t.dtype)
    for load in loads:
        load.wait()
    arrive(recv_one, one_recv)

    got = contract(order[...], recv_one[...].reshape(cells, width), 1, 0).astype(jnp.bfloat16)
    rows_in_ref[...] = jnp.concatenate([got[:rows], got[rows : 2 * rows]], axis=1)
    rows_grad_ref[...] = jnp.concatenate([got[2 * rows : 3 * rows], got[3 * rows :]], axis=1)
    hidden_units = w_in.shape[1]
    chunk = hidden_units // 3
    out = jnp.zeros(rows_in_ref.shape, jnp.float32)
    back = jnp.zeros(rows_in_ref.shape, jnp.float32)
    for start in range(0, hidden_units, chunk):
        units = slice(start, start + chunk)
        active, slope = gelu_pair(contract(rows_in_ref[...], w_in[:, units], 1, 0))
        active = active.astype(jnp.bfloat16)
        activ_ref[:, units] = active
        out = out + contract(active, w_out[units], 1, 0)
        grad_pre = (contract(rows_grad_ref[...], w_out[units], 1, 1) * slope).astype(jnp.bfloat16)
        grad_pre_ref[:, units] = grad_pre
        back = back + contract(grad_pre, w_in[:, units], 1, 1)
    whole = [out[:, :width], out[:, width:], back[:, :width], back[:, width:]]
    whole = jnp.concatenate(whole, axis=0).astype(jnp.bfloat16)
    send_two[...] = (
        contract(order_t[...], whole, 1, 0).astype(send_two.dtype).reshape(send_two.shape)
    )
    exchange(send_two, recv_two, two_send, two_recv)
    arrive(recv_two, two_recv)
    sums[...] = contract(gather_t[...], recv_two[...].reshape(cells, width), 1, 0).astype(
        sums.dtype
    )
    sends.across(sums, sums_other, sums_recv)
    sends.landed(sums_other, sums_recv)
    total = wide(sums[...]) + wide(sums_other[...])
    parts = [total[n * tok_rows : (n + 1) * tok_rows] for n in range(QUARTERS)]
    expert_rows = jnp.concatenate(parts[:2], axis=1).astype(jnp.bfloat16).astype(jnp.float32)
    grad_sent = jnp.concatenate(parts[2:], axis=1).astype(jnp.bfloat16).astype(jnp.float32)

    mixed_ref[...] = (hidden + gate * expert_rows).astype(mixed_ref.dtype)
    grad_gate = jnp.sum(grad_y * expert_rows, axis=1, keepdims=True)
    grad_logits = grad_gate * gate * (chosen - probs)
    grad_router_ref[...] = lax.dot_general(
        normed, grad_logits, (((0,), (0,)), ((), ())), precision=PRECISE,
        preferred_element_type=jnp.float32,
    )
    grad_normed = grad_sent + lax.dot_general(
        grad_logits, router_ref[...], (((1,), (0,)), ((), ())), precision=PRECISE,
        preferred_element_type=jnp.float32,
    )
    scaled = gain_ref[...][None] * grad_normed
    grad_gain_ref[...] = jnp.sum(grad_normed * hidden * scale, axis=0, keepdims=True)
    grad_hidden = (
        grad_y
        + scale * scaled
        - hidden * scale**3 * jnp.mean(scaled * hidden, axis=1, keepdims=True)
    )
    hidden_ref[...] = grad_hidden
    attended = grad_hidden.astype(jnp.bfloat16)
    attended_ref[...] = attended
    grad_context = contract(attended, proj_ref[...], 1, 1).astype(jnp.bfloat16)
    half = grad_context.shape[1] // 2
    left, right_part = grad_context[:, :half], grad_context[:, half:]
    given[...] = jnp.where(first, right_part, left)
    grad_both_ref[mine] = jnp.where(first, left, right_part)
    sends.go(place.at(dy=1), given, grad_both_ref.at[mine], back_recv)
    sends.landed(grad_both_ref.at[theirs], back_recv)
    sends.finish()

    for src, send in ((send_one, one_send), (send_two, two_send)):
        others = src.at[pl.ds(0, count - 1)]
        sender(me, others, others, send, send).wait_send()


def middle(
    both, tokens, cotangent, w_proj, gain, router, w_in, w_out, route, slot
):
    kind = jnp.bfloat16
    tok_rows, wide_row = tokens.shape
    count = router.shape[0]
    rows = 4 * count
    hidden = w_in.shape[1]
    width = 2 * wide_row // QUARTERS
    spots = QUARTERS * tok_rows
    shape = jax.ShapeDtypeStruct
    sem = pltpu.SemaphoreType.DMA
    buffer = pltpu.VMEM((count, 16, width), kind)
    return pl.pallas_call(
        middle_kernel,
        out_shape=(
            shape(tokens.shape, kind),
            shape(tokens.shape, jnp.float32),
            shape(tokens.shape, kind),
            shape((tok_rows, 2 * both.shape[1]), kind),
            shape(both.shape, kind),
            shape(router.shape[::-1], jnp.float32),
            shape((1, wide_row), jnp.float32),
            shape((rows, wide_row), kind),
            shape((rows, wide_row), kind),
            shape((rows, hidden), kind),
            shape((rows, hidden), kind),
        ),
        in_specs=[VMEM] * 8 + [ANYWHERE] * 2,
        out_specs=(VMEM,) * 11,
        scratch_shapes=[
            pltpu.VMEM(w_in.shape, kind),
            pltpu.VMEM(w_out.shape, kind),
            pltpu.VMEM((tok_rows, both.shape[1]), kind),
            pltpu.VMEM(tokens.shape, kind),
            pltpu.VMEM(tokens.shape, kind),
            pltpu.VMEM((16 * count, 16 * count), kind),
            pltpu.VMEM((16 * count, 16 * count), kind),
            pltpu.VMEM((spots, 16 * count), kind),
            buffer, buffer, buffer, buffer,
            pltpu.VMEM((spots, width), kind),
            pltpu.VMEM((spots, width), kind),
            pltpu.VMEM((tok_rows, both.shape[1]), kind),
            sem((2,)), sem((4,)), sem, sem, sem, sem, sem, sem, sem, sem,
        ],
        compiler_params=pltpu.CompilerParams(
            collective_id=4, has_side_effects=True, vmem_limit_bytes=60 * 1024 * 1024
        ),
        name="middle",
    )(
        both, tokens, cotangent, w_proj, gain, router, route[None], slot[None], w_in, w_out,
    )


def shards(
    tokens,
    attn_gain,
    w_query,
    w_key,
    w_value,
    w_proj,
    rel_table,
    rel_bucket,
    ffn_gain,
    router,
    w_in,
    w_out,
    expert_route,
    expert_slot,
    cotangent,
):
    me = lax.axis_index("ctx")
    side = 2 * SIDE * SIDE
    place = jnp.stack([me % side, me // side]).astype(jnp.int32)
    normed, rows, held = gather_plane(tokens, attn_gain, w_query, w_key, w_value)

    buckets = jnp.pad(rel_bucket, (0, 1), constant_values=31).reshape(BLOCK, BLOCK)
    both, turned, lse, flipped, table, uneven = attend(place, rel_table.T, buckets, held, rows)
    (
        mixed, grad_hidden1, grad_attended, context, grad_both, grad_router, grad_ffn_gain,
        rows_in, rows_grad, activ, grad_pre,
    ) = middle(
        both, tokens, cotangent, w_proj, ffn_gain, router.T, w_in[0], w_out[0], expert_route,
        expert_slot,
    )
    grad_parts, grad_rows, slab, grad_expert_in, grad_expert_out = attend_back(
        place, uneven, table, held, rows, grad_both, turned, lse, flipped, rows_in, rows_grad,
        activ, grad_pre, rel_table.shape[0],
    )
    grads = scatter_plane(grad_parts, grad_rows)
    (
        grad_query, grad_key, grad_value, grad_proj, grad_router, grad_table, gains, grad_input,
        mixed,
    ) = weight_totals(
        normed, grads, context, grad_attended, grad_router, slab, grad_ffn_gain,
        (w_query, w_key, w_value), tokens, grad_hidden1, attn_gain, mixed,
    )
    lines = tokens.shape[1] // LANES
    return (
        mixed,
        grad_input,
        gains[:lines].reshape(-1),
        grad_query,
        grad_key,
        grad_value,
        grad_proj,
        grad_table.T,
        gains[lines : 2 * lines].reshape(-1),
        grad_router.T,
        grad_expert_in[None],
        grad_expert_out[None],
    )


def solution(mesh):
    return jax.shard_map(
        shards,
        mesh=mesh,
        in_specs=(
            P("ctx", None),
            P(),
            P(None, "mp"),
            P(None, "mp"),
            P(None, "mp"),
            P("mp", None),
            P(None, "mp"),
            P(),
            P(),
            P(),
            P("ctx", None, "mp"),
            P("ctx", "mp", None),
            P("ctx"),
            P("ctx"),
            P("ctx", None),
        ),
        out_specs=(
            P("ctx", None),
            P("ctx", None),
            P(),
            P(None, "mp"),
            P(None, "mp"),
            P(None, "mp"),
            P("mp", None),
            P(None, "mp"),
            P(),
            P(),
            P("ctx", None, "mp"),
            P("ctx", "mp", None),
        ),
        check_vma=False,
    )
```

```python
import functools
import jax
import jax.numpy as jnp
from jax import lax
from jax.experimental import pallas as pl
from jax.experimental.pallas import tpu as pltpu
from jax.sharding import PartitionSpec as P

HEAD = 64
GROUP = 3
BLOCK = 128
PAIR = 2 * BLOCK
FORWARD_SPAN = 8
BACKWARD_SPAN = 4
VMEM = pl.BlockSpec(memory_space=pltpu.VMEM)
SMEM = pl.BlockSpec(memory_space=pltpu.SMEM)
LARGE = pltpu.CompilerParams(vmem_limit_bytes=60 * 1024 * 1024)


def contract(left, right, left_dim, right_dim):
    return lax.dot_general(
        left,
        right,
        (((left_dim,), (right_dim,)), ((), ())),
        preferred_element_type=jnp.float32,
    )


def window_row(place, chunk, tile, half, span):
    return 63 - (span * chunk + tile // 2) + place + BLOCK // 4 * (half - tile % 2)


def tile_consts(table_ref, head, place, chunk, tile, span):
    parts = []
    for half in range(2):
        row = window_row(place, chunk, tile, half, span)
        parts.append(jnp.broadcast_to(table_ref[head, pl.ds(row, 1), 0:1], (1, BLOCK)))
    return jnp.concatenate(parts, axis=1)


def chunk_mixed(uneven_ref, place, chunk, span):
    mixed = 0
    for tile in range(2 * span):
        for half in range(2):
            mixed = mixed + uneven_ref[0, window_row(place, chunk, tile, half, span)]
    return mixed


def add_uneven(table_ref, uneven_ref, score_ref, place, chunk, span):
    for tile in range(2 * span):
        for half in range(2):
            row = window_row(place, chunk, tile, half, span)

            @pl.when(uneven_ref[0, row] > 0)
            def _():
                for head in range(GROUP):
                    window = jnp.concatenate(
                        [table_ref[head, pl.ds(row, 1), :], table_ref[head, pl.ds(row + 1, 1), :]],
                        axis=1,
                    )
                    window = window - window[:, 0:1]
                    grid = pltpu.roll(
                        jnp.broadcast_to(window, (BLOCK, PAIR)),
                        BLOCK,
                        1,
                        stride=1,
                        stride_axis=0,
                    )[:, :BLOCK]
                    rows = slice(tile * BLOCK, (tile + 1) * BLOCK)
                    cols = slice(half * BLOCK, (half + 1) * BLOCK)
                    score_ref[head, rows, cols] += grid


def stream(keys_hbm, held_ref, sems, span):
    def copy(chunk):
        slot = lax.rem(chunk, 2)
        return pltpu.make_async_copy(
            keys_hbm.at[pl.ds(chunk * span, span)], held_ref.at[slot], sems.at[slot]
        )

    return copy


def head_columns(ref, head):
    return ref[:, head * HEAD : (head + 1) * HEAD]


def turn(values):
    return values.astype(jnp.float32).T


def fill_turned(dst_ref, src_ref, first):
    for head in range(GROUP):
        part = turn(head_columns(src_ref, head))
        none = jnp.zeros_like(part)
        parts = [part, none] if first else [none, part]
        dst_ref[head] = jnp.concatenate(parts, axis=0).astype(dst_ref.dtype)


def fill_padded(dst_ref, src_ref, first):
    for head in range(GROUP):
        part = head_columns(src_ref, head)
        none = jnp.zeros_like(part)
        parts = [part, none] if first else [none, part]
        dst_ref[head] = jnp.concatenate(parts, axis=1)


def side_by_side(parts):
    return jnp.concatenate([turn(part) for part in parts], axis=1).astype(jnp.bfloat16)


def flip_both(values):
    down = lax.broadcasted_iota(jnp.int32, (BLOCK, BLOCK), 0)
    right = lax.broadcasted_iota(jnp.int32, (BLOCK, BLOCK), 1)
    anti = jnp.where(down + right == BLOCK - 1, 1.0, 0.0).astype(jnp.bfloat16)
    once = contract(anti, values.astype(jnp.float32).astype(jnp.bfloat16), 1, 0)
    return contract(once.astype(jnp.bfloat16), anti, 1, 0).astype(jnp.int32)


def line_of(column):
    down = lax.broadcasted_iota(jnp.int32, (BLOCK, BLOCK), 0)
    right = lax.broadcasted_iota(jnp.int32, (BLOCK, BLOCK), 1)
    return jnp.sum(jnp.where(down == right, column, 0.0), axis=0, keepdims=True)


def shifted_up(column):
    return jnp.concatenate([column[1:], column[-1:]], axis=0)


def forward_kernel(
    place_ref, rel_ref, buckets_ref, keys_hbm, rows_ref,
    out_ref, turned_ref, lse_ref, flipped_ref, table_ref, uneven_out_ref,
    held_ref, held_sem, uneven_ref, uneven_sem,
    query_ref, best_ref, sum_ref, total_ref, score_ref,
):
    place = place_ref[0]
    span = FORWARD_SPAN
    tiles, length = 2 * span, PAIR * span
    fetch = stream(keys_hbm, held_ref, held_sem, span)
    chunks = keys_hbm.shape[0] // span
    fetch(0).start()
    flipped = flip_both(buckets_ref[...])
    flipped_ref[...] = flipped
    floats = flipped.astype(jnp.float32)
    high = jnp.max(floats, axis=1, keepdims=True)
    low = jnp.min(floats, axis=1, keepdims=True)
    high = jnp.maximum(high, shifted_up(high))
    low = jnp.minimum(low, shifted_up(low))
    uneven_out_ref[...] = line_of(jnp.where(high > low, 1.0, 0.0)).astype(jnp.int32)
    flags = pltpu.make_async_copy(uneven_out_ref, uneven_ref, uneven_sem)
    flags.start()
    for head in range(GROUP):
        values = jnp.zeros((BLOCK, BLOCK), jnp.float32)
        for bucket in range(rel_ref.shape[1]):
            value = rel_ref[place_ref[1] * GROUP + head, bucket]
            values = jnp.where(flipped == bucket, value, values)
        table_ref[head] = values
    fill_turned(query_ref, rows_ref, True)
    flags.wait()
    best_ref[...] = jnp.full_like(best_ref, -1e30)
    sum_ref[...] = jnp.zeros_like(sum_ref)
    total_ref[...] = jnp.zeros_like(total_ref)

    def rest(chunk, head, held, scores):
        consts = [tile_consts(table_ref, head, place, chunk, tile, span) for tile in range(tiles)]
        old = best_ref[head]
        new = old
        for tile in range(tiles):
            part = scores[tile * BLOCK : (tile + 1) * BLOCK]
            new = jnp.maximum(new, jnp.max(part, axis=0, keepdims=True) + consts[tile])
        decay = jnp.exp(old - new)
        weights = [
            jnp.exp(scores[tile * BLOCK : (tile + 1) * BLOCK] - (new - consts[tile]))
            for tile in range(tiles)
        ]
        weights = jnp.concatenate(weights, axis=0)
        sum_ref[head] = sum_ref[head] * decay + jnp.sum(weights, axis=0, keepdims=True)
        best_ref[head] = new
        total_ref[head] = total_ref[head] * decay + contract(
            held, weights.astype(jnp.bfloat16), 0, 0
        )

    @pl.loop(0, chunks)
    def _(chunk):
        slot = lax.rem(chunk, 2)
        fetch(chunk).wait()

        @pl.when(chunk + 1 < chunks)
        def _():
            fetch(chunk + 1).start()

        def held_of(head):
            return held_ref[slot, :, head].reshape(length, 2 * HEAD)

        mixed = chunk_mixed(uneven_ref, place, chunk, span)

        @pl.when(mixed == 0)
        def _():
            helds = [held_of(head) for head in range(GROUP)]
            scores = [contract(helds[head], query_ref[head], 1, 0) for head in range(GROUP)]
            for head in range(GROUP):
                rest(chunk, head, helds[head], scores[head])

        @pl.when(mixed > 0)
        def _():
            for head in range(GROUP):
                score_ref[head] = contract(held_of(head), query_ref[head], 1, 0)
            add_uneven(table_ref, uneven_ref, score_ref, place, chunk, span)
            for head in range(GROUP):
                rest(chunk, head, held_of(head), score_ref[head])

    for head in range(GROUP):
        turned_ref[head] = total_ref[head][HEAD:] / sum_ref[head]
    out_ref[...] = side_by_side([turned_ref[head] for head in range(GROUP)])
    for head in range(GROUP):
        lse_ref[head] = best_ref[head] + jnp.log(sum_ref[head])


def backward_kernel(
    place_ref, uneven_ref, table_ref, keys_hbm, rows_ref, grads_ref, turned_ref, lse_ref,
    flipped_ref, rows_in_ref, rows_grad_ref, activ_ref, grad_pre_ref,
    grad_keys_hbm, grad_rows_ref, slab_ref, expert_in_hbm, expert_out_hbm,
    held_ref, held_sem, grad_keys_ref, grad_keys_sem, expert_in, expert_out, expert_sem, offsets_ref, query_t_ref, grad_t_ref, query_ref, grad_ref, delta_ref, grad_query_ref, score_ref,
):
    place = place_ref[0]
    span = BACKWARD_SPAN
    tiles, length = 2 * span, PAIR * span
    fetch = stream(keys_hbm, held_ref, held_sem, span)
    chunks = keys_hbm.shape[0] // span
    fetch(0).start()

    def give(chunk):
        slot = lax.rem(chunk, 2)
        return pltpu.make_async_copy(
            grad_keys_ref.at[slot],
            grad_keys_hbm.at[pl.ds(chunk * span, span)],
            grad_keys_sem.at[slot],
        )

    expert_in[...] = contract(rows_in_ref[...], grad_pre_ref[...], 0, 0)
    expert_out[...] = contract(activ_ref[...], rows_grad_ref[...], 0, 0)
    stores = [
        pltpu.make_async_copy(expert_in, expert_in_hbm, expert_sem.at[0]),
        pltpu.make_async_copy(expert_out, expert_out_hbm, expert_sem.at[1]),
    ]
    for store in stores:
        store.start()
    fill_turned(query_t_ref, rows_ref, True)
    fill_turned(grad_t_ref, grads_ref, False)
    fill_padded(query_ref, rows_ref, True)
    fill_padded(grad_ref, grads_ref, False)
    for head in range(GROUP):
        delta_ref[head] = jnp.sum(
            grad_t_ref[head][HEAD:].astype(jnp.float32) * turned_ref[head], axis=0, keepdims=True
        )
    grad_query_ref[...] = jnp.zeros_like(grad_query_ref)
    offsets_ref[...] = jnp.zeros_like(offsets_ref)

    def rest(chunk, head, held, scores, grads):
        probs = jnp.concatenate(
            [
                jnp.exp(
                    scores[tile * BLOCK : (tile + 1) * BLOCK]
                    - (lse_ref[head] - tile_consts(table_ref, head, place, chunk, tile, span))
                )
                for tile in range(tiles)
            ],
            axis=0,
        )
        slopes = probs * (grads - delta_ref[head])
        rounded = slopes.astype(jnp.bfloat16)
        part = contract(rounded, query_ref[head], 1, 0) + contract(
            probs.astype(jnp.bfloat16), grad_ref[head], 1, 0
        )
        grad_keys_ref[lax.rem(chunk, 2), :, head] = part.astype(grad_keys_ref.dtype).reshape(
            span, PAIR, 2 * HEAD
        )
        grad_query_ref[head] += contract(held, rounded, 0, 0)
        return slopes

    def put_even(chunk, head, tile, half, slopes):
        row = window_row(place, chunk, tile, half, span)
        offsets_ref[head, pl.ds(row, 1), :] += jnp.sum(slopes, axis=0, keepdims=True)

    def put_uneven(chunk, head, tile, half, slopes):
        row = window_row(place, chunk, tile, half, span)
        wide = jnp.concatenate([slopes, jnp.zeros_like(slopes)], axis=1)
        folded = jnp.zeros((8, PAIR), jnp.float32)
        for group in range(BLOCK // 8):
            folded = folded + pltpu.roll(
                wide[group * 8 : (group + 1) * 8], (BLOCK - 8 * group) % PAIR, 1
            )
        line = jnp.zeros((1, PAIR), jnp.float32)
        for step in range(8):
            line = line + pltpu.roll(folded, (PAIR - step) % PAIR, 1)[step : step + 1]
        offsets_ref[head, pl.ds(row, 1), :] += line[:, :BLOCK]
        offsets_ref[head, pl.ds(row + 1, 1), :] += line[:, BLOCK:]

    @pl.loop(0, chunks)
    def _(chunk):
        slot = lax.rem(chunk, 2)
        fetch(chunk).wait()

        @pl.when(chunk + 1 < chunks)
        def _():
            fetch(chunk + 1).start()

        def held_of(head):
            return held_ref[slot, :, head].reshape(length, 2 * HEAD)

        @pl.when(chunk >= 2)
        def _():
            give(chunk - 2).wait()

        mixed = chunk_mixed(uneven_ref, place, chunk, span)

        @pl.when(mixed == 0)
        def _():
            helds = [held_of(head) for head in range(GROUP)]
            scores = [contract(helds[head], query_t_ref[head], 1, 0) for head in range(GROUP)]
            grads = [contract(helds[head], grad_t_ref[head], 1, 0) for head in range(GROUP)]
            for head in range(GROUP):
                slopes = rest(chunk, head, helds[head], scores[head], grads[head])
                for tile in range(tiles):
                    for half in range(2):
                        part = slopes[
                            tile * BLOCK : (tile + 1) * BLOCK, half * BLOCK : (half + 1) * BLOCK
                        ]
                        put_even(chunk, head, tile, half, part)

        @pl.when(mixed > 0)
        def _():
            for head in range(GROUP):
                score_ref[head] = contract(held_of(head), query_t_ref[head], 1, 0)
            add_uneven(table_ref, uneven_ref, score_ref, place, chunk, span)
            for head in range(GROUP):
                held = held_of(head)
                grads = contract(held, grad_t_ref[head], 1, 0)
                score_ref[head] = rest(chunk, head, held, score_ref[head], grads)
            for tile in range(tiles):
                for half in range(2):
                    rows = slice(tile * BLOCK, (tile + 1) * BLOCK)
                    cols = slice(half * BLOCK, (half + 1) * BLOCK)
                    uneven = uneven_ref[0, window_row(place, chunk, tile, half, span)]

                    @pl.when(uneven == 0)
                    def _():
                        for head in range(GROUP):
                            put_even(chunk, head, tile, half, score_ref[head, rows, cols])

                    @pl.when(uneven > 0)
                    def _():
                        for head in range(GROUP):
                            put_uneven(chunk, head, tile, half, score_ref[head, rows, cols])

        give(chunk).start()

    for chunk in (chunks - 2, chunks - 1):
        give(chunk).wait()
    grad_rows_ref[...] = side_by_side([grad_query_ref[head][:HEAD] for head in range(GROUP)])
    lanes = lax.broadcasted_iota(jnp.int32, (1, BLOCK), 1)
    for bucket in range(slab_ref.shape[0]):
        hit = flipped_ref[...] == bucket
        line = jnp.zeros((1, BLOCK), jnp.float32)
        for head in range(GROUP):
            part = jnp.sum(jnp.where(hit, offsets_ref[head], 0.0), axis=0, keepdims=True)
            part = jnp.sum(part, axis=1, keepdims=True)
            line = jnp.where(lanes == place_ref[1] * GROUP + head, part, line)
        slab_ref[pl.ds(bucket, 1)] = line
    for store in stores:
        store.wait()


def attend(place, rel_table, buckets, keys, rows):
    shape = jax.ShapeDtypeStruct
    anywhere = pl.BlockSpec(memory_space=pl.ANY)
    return pl.pallas_call(
        forward_kernel,
        out_shape=(
            shape(rows.shape, jnp.bfloat16),
            shape((GROUP, HEAD, PAIR), jnp.float32),
            shape((GROUP, 1, PAIR), jnp.float32),
            shape((BLOCK, BLOCK), jnp.int32),
            shape((GROUP, BLOCK, BLOCK), jnp.float32),
            shape((1, BLOCK), jnp.int32),
        ),
        in_specs=[SMEM, SMEM, VMEM, anywhere, VMEM],
        out_specs=(VMEM,) * 6,
        scratch_shapes=[
            pltpu.VMEM((2, FORWARD_SPAN) + keys.shape[1:], keys.dtype),
            pltpu.SemaphoreType.DMA((2,)),
            pltpu.SMEM((1, BLOCK), jnp.int32),
            pltpu.SemaphoreType.DMA,
            pltpu.VMEM((GROUP, 2 * HEAD, PAIR), jnp.bfloat16),
            pltpu.VMEM((GROUP, 1, PAIR), jnp.float32),
            pltpu.VMEM((GROUP, 1, PAIR), jnp.float32),
            pltpu.VMEM((GROUP, 2 * HEAD, PAIR), jnp.float32),
            pltpu.VMEM((GROUP, FORWARD_SPAN * PAIR, PAIR), jnp.float32),
        ],
        compiler_params=LARGE,
        name="attend",
    )(place, rel_table, buckets, keys, rows)


def attend_back(
    place, uneven, table, keys, rows, grads, turned, lse, flipped, rows_in, rows_grad, activ,
    grad_pre, buckets,
):
    shape = jax.ShapeDtypeStruct
    wide_row, hidden = rows_in.shape[1], activ.shape[1]
    anywhere = pl.BlockSpec(memory_space=pl.ANY)
    return pl.pallas_call(
        backward_kernel,
        out_shape=(
            shape(keys.shape, jnp.bfloat16),
            shape(rows.shape, jnp.bfloat16),
            shape((buckets, BLOCK), jnp.float32),
            shape((wide_row, hidden), jnp.float32),
            shape((hidden, wide_row), jnp.float32),
        ),
        in_specs=[SMEM, SMEM, VMEM, anywhere] + [VMEM] * 9,
        out_specs=(anywhere, VMEM, VMEM, anywhere, anywhere),
        scratch_shapes=[
            pltpu.VMEM((2, BACKWARD_SPAN) + keys.shape[1:], keys.dtype),
            pltpu.SemaphoreType.DMA((2,)),
            pltpu.VMEM((2, BACKWARD_SPAN) + keys.shape[1:], keys.dtype),
            pltpu.SemaphoreType.DMA((2,)),
            pltpu.VMEM((wide_row, hidden), jnp.float32),
            pltpu.VMEM((hidden, wide_row), jnp.float32),
            pltpu.SemaphoreType.DMA((2,)),
            pltpu.VMEM((GROUP, BLOCK, BLOCK), jnp.float32),
            pltpu.VMEM((GROUP, 2 * HEAD, PAIR), jnp.bfloat16),
            pltpu.VMEM((GROUP, 2 * HEAD, PAIR), jnp.bfloat16),
            pltpu.VMEM((GROUP, PAIR, 2 * HEAD), jnp.bfloat16),
            pltpu.VMEM((GROUP, PAIR, 2 * HEAD), jnp.bfloat16),
            pltpu.VMEM((GROUP, 1, PAIR), jnp.float32),
            pltpu.VMEM((GROUP, 2 * HEAD, PAIR), jnp.float32),
            pltpu.VMEM((GROUP, BACKWARD_SPAN * PAIR, PAIR), jnp.float32),
        ],
        compiler_params=LARGE,
        name="attend_back",
    )(
        place, uneven, table, keys, rows, grads, turned, lse, flipped, rows_in, rows_grad, activ,
        grad_pre,
    )


EPSILON = 1e-06
PRECISE = lax.Precision.HIGHEST
ANYWHERE = pl.BlockSpec(memory_space=pl.ANY)
SIDE = 4


class Place:
    def __init__(self):
        self.me = lax.axis_index("ctx")
        self.core = lax.rem(self.me, 2)
        self.z = lax.rem(self.me // 2, SIDE)
        self.x = lax.rem(self.me // (2 * SIDE), SIDE)
        self.y = self.me // (2 * SIDE * SIDE)

    def at(self, dx=0, dz=0, dcore=0, dy=0):
        x = lax.rem(self.x + dx, SIDE)
        z = lax.rem(self.z + dz, SIDE)
        core = lax.rem(self.core + dcore, 2)
        y = lax.rem(self.y + dy, 2)
        return ((y * SIDE + x) * SIDE + z) * 2 + core

    def turned(self, axis, step):
        return self.at(dx=step) if axis == 0 else self.at(dz=step)

    def along(self, axis, step):
        return lax.rem((self.x if axis == 0 else self.z) + step, SIDE)


def greet(targets, across=False):
    barrier = pltpu.get_barrier_semaphore()
    if across:
        pl.semaphore_signal(
            barrier,
            inc=1,
            device_id={"mp": 1 - lax.axis_index("mp")},
            device_id_type=pl.DeviceIdType.MESH,
        )
    for target in targets:
        pl.semaphore_signal(
            barrier, inc=1, device_id={"ctx": target}, device_id_type=pl.DeviceIdType.MESH
        )
    return barrier, len(targets) + int(across)


def meet(targets, across=False):
    pl.semaphore_wait(*greet(targets, across))


def ring_targets(place):
    found = [place.at(dcore=1)]
    for step in range(1, SIDE):
        found += [place.at(dx=step), place.at(dz=step)]
    return found


def sender(target, src, dst, send_sem, recv_sem):
    return pltpu.make_async_remote_copy(
        src_ref=src,
        dst_ref=dst,
        send_sem=send_sem,
        recv_sem=recv_sem,
        device_id={"ctx": target},
        device_id_type=pl.DeviceIdType.MESH,
    )


def wide(value):
    return value.astype(jnp.float32)


class Sends:
    def __init__(self, place, sems):
        self.place, self.sems, self.started = place, sems, []

    def go(self, target, src, dst, recv_sem):
        copy = sender(target, src, dst, self.sems.at[len(self.started)], recv_sem)
        copy.start()
        self.started.append(copy)
        return copy

    def across(self, src, dst, recv_sem):
        copy = pltpu.make_async_remote_copy(
            src_ref=src,
            dst_ref=dst,
            send_sem=self.sems.at[len(self.started)],
            recv_sem=recv_sem,
            device_id={"mp": 1 - lax.axis_index("mp")},
            device_id_type=pl.DeviceIdType.MESH,
        )
        copy.start()
        self.started.append(copy)

    def landed(self, view, sem):
        sender(self.place.me, view, view, sem, sem).wait_recv()

    def finish(self):
        for copy in self.started:
            copy.wait_send()


def gather_kernel(
    tokens_ref, gain_ref, w_query_ref, w_key_ref, w_value_ref,
    normed_ref, rows_ref, out_ref,
    block_ref, given, other, local_sem, send_sem, ring_recv, twin_recv, swap_recv,
):
    place = Place()
    barrier = greet(ring_targets(place) + [place.at(dy=1)])
    sends = Sends(place, send_sem)
    half_rows = block_ref.shape[1] // 2
    sub_rows = half_rows // 2
    first = place.y == 0
    width = GROUP * HEAD
    floats_in = wide(tokens_ref[...])
    scale = lax.rsqrt(jnp.mean(floats_in * floats_in, axis=1, keepdims=True) + EPSILON)
    normed = (floats_in * scale * gain_ref[...][None]).astype(normed_ref.dtype)
    normed_ref[...] = normed
    kept = []
    for n, ref in enumerate((w_query_ref, w_key_ref, w_value_ref)):
        made = contract(normed, ref[...], 1, 0).astype(given.dtype)
        kept.append(jnp.where(first, made[:, :width], made[:, width:]))
        given[n] = jnp.where(first, made[:, width:], made[:, :width])

    def rows_at(half, start=0, count=half_rows):
        side = place.y if half == 0 else 1 - place.y
        return pl.ds(pl.multiple_of(side * half_rows + start, sub_rows), count)

    def put(half, query, key, value):
        rows_ref[rows_at(half)] = query
        for head in range(GROUP):
            lanes = slice(head * HEAD, (head + 1) * HEAD)
            block_ref[head, rows_at(half)] = jnp.concatenate(
                [key[:, lanes], value[:, lanes]], axis=1
            )

    put(0, *kept)
    pl.semaphore_wait(*barrier)
    sends.go(place.at(dy=1), given, other, swap_recv)

    def rows_of(half, piece):
        if piece is None:
            return rows_at(half)
        return rows_at(half, piece * sub_rows, sub_rows)

    def view(half, first, second, core, piece=None):
        x, z = (second, first) if half == 0 else (first, second)
        slot = (place.along(0, x) * SIDE + place.along(1, z)) * 2 + core
        return out_ref.at[slot, :, rows_of(half, piece)]

    def held(half, first, second, piece=None):
        if first == 0 and second == 0:
            return block_ref.at[:, rows_of(half, piece)]
        return view(half, first, second, place.core, piece)

    def shift(half, first, second, stage, step, piece=None):
        axis = 1 - half if stage == 0 else half
        if stage == 0:
            slot = ((first - step) % SIDE, second)
        else:
            slot = (first, (second - step) % SIDE)
        sends.go(
            place.turned(axis, step % SIDE),
            held(half, first, second, piece),
            view(half, first, second, place.core, piece),
            ring_recv.at[half, slot[0], slot[1], piece or 0],
        )

    def whole(dx, dz, core):
        return out_ref.at[(place.along(0, dx) * SIDE + place.along(1, dz)) * 2 + core]

    def to_twin(dx, dz):
        src = block_ref if dx == 0 and dz == 0 else whole(dx, dz, place.core)
        sends.go(place.at(dcore=1), src, whole(dx, dz, place.core), twin_recv.at[dx, dz])

    def wait(half, first, second):
        if second == 2:
            for piece in range(2):
                sends.landed(
                    view(half, first, second, place.core, piece),
                    ring_recv.at[half, first, second, piece],
                )
        else:
            sends.landed(
                view(half, first, second, place.core), ring_recv.at[half, first, second, 0]
            )

    def relay(half, first, second):
        if second == SIDE - 1:
            shift(half, first, second, 1, 1, 0)
        elif second == 1:
            shift(half, first, second, 1, -1, 1)

    for half in range(2):
        if half == 1:
            sends.landed(other, swap_recv)
            put(1, other[0], other[1], other[2])
        for stage in range(2):
            for step in (1, -1, 2)[: 3 - stage]:
                shift(half, 0, 0, stage, step)
    to_twin(0, 0)
    own = pltpu.make_async_copy(
        block_ref, out_ref.at[(place.x * SIDE + place.z) * 2 + place.core], local_sem
    )
    own.start()
    order = [(3, 0), (1, 0), (0, 3), (0, 1), (2, 0), (3, 3), (3, 1), (1, 3), (1, 1), (0, 2)]
    order += [(3, 2), (1, 2), (2, 3), (2, 1), (2, 2)]
    passed = set()
    for first, second in order:
        for half in range(2):
            wait(half, first, second)
            if second == 0:
                for step in (1, -1):
                    shift(half, first, second, 1, step)
            else:
                relay(half, first, second)
        passed.add((first, second))
        if (second, first) in passed:
            for dx, dz in sorted({(first, second), (second, first)}):
                to_twin(dx, dz)
    for dx, dz in [(0, 0)] + order:
        sends.landed(whole(dx, dz, 1 - place.core), twin_recv.at[dx, dz])
    own.wait()
    sends.finish()


def gather_plane(tokens, gain, w_query, w_key, w_value):
    kind = tokens.dtype
    tok_rows = tokens.shape[0]
    width = GROUP * HEAD
    block = (GROUP, 2 * tok_rows, 2 * HEAD)
    shape = jax.ShapeDtypeStruct
    sem = pltpu.SemaphoreType.DMA
    return pl.pallas_call(
        gather_kernel,
        out_shape=(
            shape(tokens.shape, kind),
            shape((2 * tok_rows, width), kind),
            shape((2 * SIDE * SIDE,) + block, kind),
        ),
        in_specs=[VMEM] * 5,
        out_specs=(VMEM, VMEM, ANYWHERE),
        scratch_shapes=[
            pltpu.VMEM(block, kind),
            pltpu.VMEM((3, tok_rows, width), kind),
            pltpu.VMEM((3, tok_rows, width), kind),
            sem, sem((73,)), sem((2, SIDE, SIDE, 2)), sem((SIDE, SIDE)), sem,
        ],
        compiler_params=pltpu.CompilerParams(
            collective_id=1, has_side_effects=True, vmem_limit_bytes=60 * 1024 * 1024
        ),
        name="gather_plane",
    )(tokens, gain, w_query, w_key, w_value)


def ring_sum(sends, axis_of, sums, via, landing, via_recv, land_recv, ready):
    place = sends.place
    rows = sums.shape[-2] // 2
    middle = (slice(None),) * (len(sums.shape) - 4)

    def cut(ref, index, piece):
        return ref.at[index + middle + (pl.ds(piece * rows, rows),)]

    for half in range(2):
        ready(half, 2)
        for piece, step in ((0, 1), (1, SIDE - 1)):
            sends.go(
                place.turned(axis_of(half), step),
                cut(sums, (half, 2), piece),
                via.at[half, piece],
                via_recv.at[half, piece],
            )
    for half in range(2):
        for piece, step in ((0, 1), (1, SIDE - 1)):
            ready(half, step)
            sends.go(
                place.turned(axis_of(half), step),
                cut(sums, (half, step), 1 - piece),
                cut(landing, (half, piece), 1 - piece),
                land_recv.at[half, piece, 1 - piece],
            )
    for half in range(2):
        ready(half, 0)
    for half in range(2):
        for piece, step in ((0, 1), (1, SIDE - 1)):
            sends.landed(via.at[half, piece], via_recv.at[half, piece])
            spot = (half, step) + middle + (slice(piece * rows, (piece + 1) * rows),)
            sums[spot] = (wide(sums[spot]) + wide(via[half, piece])).astype(sums.dtype)
            sends.go(
                place.turned(axis_of(half), step),
                cut(sums, (half, step), piece),
                cut(landing, (half, piece), piece),
                land_recv.at[half, piece, piece],
            )

    def finish(half):
        for piece in range(2):
            for part in (1 - piece, piece):
                sends.landed(cut(landing, (half, piece), part), land_recv.at[half, piece, part])

    return finish


def ring_sum_direct(sends, axis_of, sums, landing, land_recv, ready):
    for step in (2, 1, 3):
        for half in range(2):
            ready(half, step)
            sends.go(
                sends.place.turned(axis_of(half), step),
                sums.at[half, step],
                landing.at[half, step - 1],
                land_recv.at[half, step - 1],
            )
    for half in range(2):
        ready(half, 0)

    def finish(half):
        for step in range(1, SIDE):
            sends.landed(landing.at[half, step - 1], land_recv.at[half, step - 1])

    return finish


def scatter_kernel(
    parts_ref, rows_ref, out_ref, mine, twin, sums, via_one, land_one, halves, land_two,
    both, other, rows_other,
    local_sem, send_sem, twin_recv, via_one_recv, land_one_recv, land_two_recv,
    far_recv,
):
    place = Place()
    half_rows = parts_ref.shape[4] // 2

    def source(half, group, core):
        rows = pl.ds(half * half_rows, half_rows)
        if half == 0:
            return parts_ref.at[group, :, core, :, rows]
        return parts_ref.at[:, group, core, :, rows]

    barrier = greet(ring_targets(place) + [place.at(dy=1)])
    loads = {}
    order = (2, 1, 3, 0)
    for step in order:
        for half in range(2):
            loads[half, step] = pltpu.make_async_copy(
                source(half, place.along(half, step), place.core),
                mine.at[half, step],
                local_sem.at[half, step],
            )
            loads[half, step].start()
    pl.semaphore_wait(*barrier)
    sends = Sends(place, send_sem)
    their_rows = pl.ds(pl.multiple_of((1 - place.y) * half_rows, half_rows), half_rows)
    sends.go(place.at(dy=1), rows_ref.at[their_rows], rows_other, far_recv.at[1])
    for step in order:
        for half in range(2):
            sends.go(
                place.at(dcore=1),
                source(half, place.along(half, step), 1 - place.core),
                twin.at[half, step],
                twin_recv.at[half, step],
            )

    def ready_one(half, step):
        loads[half, step].wait()
        sends.landed(twin.at[half, step], twin_recv.at[half, step])
        sums[half, step] = (wide(mine[half, step]) + wide(twin[half, step])).astype(sums.dtype)

    done_one = ring_sum(
        sends, lambda half: half, sums, via_one, land_one, via_one_recv, land_one_recv, ready_one
    )
    arrived = set()

    def ready_two(half, step):
        if half not in arrived:
            arrived.add(half)
            done_one(half)
        spot = place.along(1 - half, step)
        total = wide(sums[half, 0, spot])
        for side in range(2):
            total = total + wide(land_one[half, side, spot])
        halves[half, step] = total.astype(halves.dtype)

    done_two = ring_sum_direct(
        sends, lambda half: 1 - half, halves, land_two, land_two_recv, ready_two
    )
    for half in range(2):
        done_two(half)
        total = wide(halves[half, 0])
        for side in range(SIDE - 1):
            total = total + wide(land_two[half, side])
        total = total.astype(both.dtype)
        parts = [total[head, :, :HEAD] for head in range(GROUP)]
        parts += [total[head, :, HEAD:] for head in range(GROUP)]
        both[half] = jnp.concatenate(parts, axis=1)
    sends.go(place.at(dy=1), both.at[1 - place.y], other, far_recv.at[0])
    width = GROUP * HEAD
    mine_rows = pl.ds(pl.multiple_of(place.y * half_rows, half_rows), half_rows)
    kept = jnp.concatenate([rows_ref[mine_rows], both[place.y]], axis=1)
    sends.landed(rows_other, far_recv.at[1])
    sends.landed(other, far_recv.at[0])
    received = jnp.concatenate([rows_other[...], other[...]], axis=1)
    low = jnp.where(place.y == 0, kept, received)
    high = jnp.where(place.y == 0, received, kept)
    parts = []
    for n in range(3):
        parts += [low[:, n * width : (n + 1) * width], high[:, n * width : (n + 1) * width]]
    out_ref[...] = jnp.concatenate(parts, axis=1)
    sends.finish()


def scatter_plane(parts, rows_grad):
    heads, rows, lanes = parts.shape[1:]
    piece = (heads, rows // 2, lanes)
    small = (heads, rows // 4, lanes)
    kind = parts.dtype
    sem = pltpu.SemaphoreType.DMA
    return pl.pallas_call(
        scatter_kernel,
        out_shape=jax.ShapeDtypeStruct((rows // 2, 6 * rows_grad.shape[1]), kind),
        in_specs=[ANYWHERE, VMEM],
        out_specs=pl.BlockSpec(memory_space=pltpu.VMEM),
        scratch_shapes=[
            pltpu.VMEM((2, SIDE, SIDE) + piece, kind),
            pltpu.VMEM((2, SIDE, SIDE) + piece, kind),
            pltpu.VMEM((2, SIDE, SIDE) + piece, kind),
            pltpu.VMEM((2, 2, SIDE) + small, kind),
            pltpu.VMEM((2, 2, SIDE) + piece, kind),
            pltpu.VMEM((2, SIDE) + piece, kind),
            pltpu.VMEM((2, SIDE - 1) + piece, kind),
            pltpu.VMEM((2, rows // 2, 2 * rows_grad.shape[1]), kind),
            pltpu.VMEM((rows // 2, 2 * rows_grad.shape[1]), kind),
            pltpu.VMEM((rows // 2, rows_grad.shape[1]), kind),
            sem((2, SIDE)), sem((34,)), sem((2, SIDE)),
            sem((2, 2)), sem((2, 2, 2)), sem((2, SIDE - 1)), sem((2,)),
        ],
        compiler_params=pltpu.CompilerParams(
            collective_id=2, has_side_effects=True, vmem_limit_bytes=60 * 1024 * 1024
        ),
        name="scatter_plane",
    )(parts.reshape((SIDE, SIDE, 2) + parts.shape[1:]), rows_grad)


LANES = 128
UNIT = 16
UNITS = 9
BLOCK_ROWS = UNIT * (UNITS + 1)


def runs(slab_rows):
    found, unit = [], 0
    for slab, rows in enumerate(slab_rows):
        row = 0
        while row < rows:
            block, inside = divmod(unit, UNITS)
            take = min(UNITS - inside, (rows - row) // UNIT)
            found.append((slab, row, block, inside * UNIT, take * UNIT))
            row += take * UNIT
            unit += take
    return found


def block_at(block):
    return block // 32, block // 16 % 2, block // 4 % 4, block % 4


def weights_kernel(
    normed_ref, grads_ref, context_ref, attended_ref, router_ref, slab_ref, ffn_ref, w_query_ref,
    w_key_ref, w_value_ref, tokens_ref, hidden_ref, gain_ref,
    full, input_ref,
    share, share_other, parts, twin, sums, via_one, land_one, halves, land_two, other,
    send_sem, twin_recv, via_one_recv, land_one_recv, land_two_recv,
    far_recv, far_back_recv, two_back_recv, one_back_recv, twin_back_recv, share_recv,
):
    place = Place()
    width = context_ref.shape[1]
    barrier = greet(ring_targets(place) + [place.at(dy=1)], True)
    sends = Sends(place, send_sem)
    partial = jnp.zeros(share.shape, jnp.float32)
    for n, ref in enumerate((w_query_ref, w_key_ref, w_value_ref)):
        partial = partial + contract(grads_ref[:, n * width : (n + 1) * width], ref[...], 1, 1)
    share[...] = partial.astype(share.dtype)
    pl.semaphore_wait(*barrier)
    sends.across(share, share_other, share_recv)
    slabs, table = slab_table(normed_ref.shape[1], width)
    operands = ((normed_ref, grads_ref), (context_ref, attended_ref))
    for index, (output, lane) in enumerate(slabs):
        left, right = operands[output // 3]
        lane = lane if output == 3 else output * width + lane
        grad = contract(left[...], right[:, lane : lane + LANES], 0, 0).astype(parts.dtype)
        for slab, row, block, inside, rows in table:
            if slab == index:
                parts[block_at(block) + (slice(inside, inside + rows),)] = grad[row : row + rows]
    sends.landed(share_other, share_recv)
    grad_normed = wide(share[...]) + wide(share_other[...])
    floats_in = wide(tokens_ref[...])
    scale = lax.rsqrt(jnp.mean(floats_in * floats_in, axis=1, keepdims=True) + EPSILON)
    scaled = gain_ref[...][None] * grad_normed
    input_ref[...] = (
        hidden_ref[...]
        + scale * scaled
        - floats_in * scale**3 * jnp.mean(scaled * floats_in, axis=1, keepdims=True)
    )
    gain_sum = jnp.sum(grad_normed * floats_in * scale, axis=0, keepdims=True)
    tall = router_ref.shape[0] // 2
    router = jnp.concatenate([router_ref[:tall], router_ref[tall:]], axis=1)
    lines = [
        line[:, n : n + LANES]
        for line in (gain_sum, ffn_ref[...])
        for n in range(0, gain_sum.shape[1], LANES)
    ]
    lines.append(jnp.zeros((UNIT - len(lines), LANES), jnp.float32))
    small = [router[n : n + UNIT] for n in range(0, tall, UNIT)]
    small += [slab_ref[n : n + UNIT] for n in range(0, slab_ref.shape[0], UNIT)]
    small.append(jnp.concatenate(lines, axis=0))
    for block in range(64):
        part = small[block] if block < len(small) else jnp.zeros((UNIT, LANES), jnp.float32)
        parts[block_at(block) + (slice(UNIT * UNITS, BLOCK_ROWS),)] = part.astype(parts.dtype)

    order = (2, 1, 3, 0)
    for step in order:
        for half in range(2):
            sends.go(
                place.at(dcore=1),
                parts.at[half, 1 - place.core, place.along(half, step)],
                twin.at[half, step],
                twin_recv.at[half, step],
            )

    def ready_one(half, step):
        sends.landed(twin.at[half, step], twin_recv.at[half, step])
        own = parts[half, place.core, place.along(half, step)]
        sums[half, step] = (wide(own) + wide(twin[half, step])).astype(sums.dtype)

    done_one = ring_sum(
        sends, lambda half: half, sums, via_one, land_one, via_one_recv, land_one_recv, ready_one
    )
    arrived = set()

    def ready_two(half, step):
        if half not in arrived:
            arrived.add(half)
            done_one(half)
        spot = place.along(1 - half, step)
        total = wide(sums[half, 0, spot])
        for side in range(2):
            total = total + wide(land_one[half, side, spot])
        halves[half, step] = total.astype(halves.dtype)

    done_two = ring_sum_direct(
        sends, lambda half: 1 - half, halves, land_two, land_two_recv, ready_two
    )
    low = BLOCK_ROWS // 2
    for half in range(2):
        done_two(half)
        total = wide(halves[half, 0])
        for side in range(SIDE - 1):
            total = total + wide(land_two[half, side])
        halves[half, 0] = total.astype(halves.dtype)
        sends.go(
            place.at(dy=1),
            halves.at[half, 0, pl.ds(pl.multiple_of((1 - place.y) * low, UNIT), low)],
            other.at[half],
            far_recv.at[half],
        )

    def spot(half, core, first, second, rows=None):
        place_of = (half, core, place.along(half, first), place.along(1 - half, second))
        return full.at[place_of] if rows is None else full.at[place_of + (rows,)]

    def y_rows(y):
        return pl.ds(pl.multiple_of(y * low, UNIT), low)

    for half in range(2):
        sends.landed(other.at[half], far_recv.at[half])
        total = wide(halves[half, 0, y_rows(place.y)]) + wide(other[half])
        full[
            half, place.core, place.along(half, 0), place.along(1 - half, 0), y_rows(place.y)
        ] = total.astype(full.dtype)
        view = spot(half, place.core, 0, 0, y_rows(place.y))
        sends.go(place.at(dy=1), view, view, far_back_recv.at[half])

    subs = [pl.ds(piece * low, low) for piece in range(2)]
    for half in range(2):
        sends.landed(
            spot(half, place.core, 0, 0, y_rows(1 - place.y)), far_back_recv.at[half]
        )
        view = spot(half, place.core, 0, 0)
        for step in range(1, SIDE):
            sends.go(
                place.turned(1 - half, step), view, view, two_back_recv.at[half, SIDE - step]
            )

    def group(half, core, first, rows=None):
        if rows is None:
            return full.at[half, core, place.along(half, first)]
        return full.at[half, core, place.along(half, first), :, rows]

    for half in range(2):
        for step in range(1, SIDE):
            sends.landed(spot(half, place.core, 0, step), two_back_recv.at[half, step])
        view = group(half, place.core, 0)
        for step in (1, SIDE - 1):
            sends.go(place.turned(half, step), view, view, one_back_recv.at[half, SIDE - step, 0])
        sends.go(place.at(dcore=1), view, view, twin_back_recv.at[half, 0])
    for half in range(2):
        for piece, step in ((0, 1), (1, SIDE - 1)):
            view = group(half, place.core, SIDE - step)
            sends.landed(view, one_back_recv.at[half, SIDE - step, 0])
            part = group(half, place.core, SIDE - step, subs[piece])
            sends.go(place.turned(half, step), part, part, one_back_recv.at[half, 2, piece])
            sends.go(place.at(dcore=1), view, view, twin_back_recv.at[half, SIDE - step])
    for half in range(2):
        for piece in range(2):
            sends.landed(group(half, place.core, 2, subs[piece]), one_back_recv.at[half, 2, piece])
        view = group(half, place.core, 2)
        sends.go(place.at(dcore=1), view, view, twin_back_recv.at[half, 2])
    for first in (0, 3, 1, 2):
        for half in range(2):
            sends.landed(group(half, 1 - place.core, first), twin_back_recv.at[half, first])

    sends.finish()


def slab_table(tall, width):
    slabs = [(output, lane) for output in range(3) for lane in range(0, width, LANES)]
    slabs += [(3, lane) for lane in range(0, tall, LANES)]
    return slabs, runs([tall if output < 3 else width for output, _ in slabs])


def unpack_kernel(
    full, input_ref, mixed_ref,
    query_ref, key_ref, value_ref, proj_ref, router_ref, slab_ref, gains_ref, grad_input_ref,
    mixed_out_ref,
):
    grad_input_ref[...] = input_ref[...]
    mixed_out_ref[...] = mixed_ref[...]
    slabs, table = slab_table(query_ref.shape[0], query_ref.shape[1])
    for slab, row, block, inside, rows in table:
        output, lane = slabs[slab]
        ref = (query_ref, key_ref, value_ref, proj_ref)[output]
        ref[row : row + rows, lane : lane + LANES] = wide(
            full[block_at(block) + (slice(inside, inside + rows),)]
        )
    experts = router_ref.shape[0]
    tall = router_ref.shape[1] // 2

    def small(block):
        return wide(full[block_at(block) + (slice(UNIT * UNITS, BLOCK_ROWS),)])

    base = tall // UNIT
    turned = jnp.concatenate([small(block) for block in range(base)], axis=0).T
    router_ref[:, :tall] = turned[:experts]
    router_ref[:, tall:] = turned[experts:]
    heads, buckets = slab_ref.shape
    slab = [small(base + block) for block in range(buckets // UNIT)]
    slab_ref[...] = jnp.concatenate(slab, axis=0).T[:heads]
    gains_ref[...] = small(base + buckets // UNIT)


def weight_totals(
    normed, grads, context, attended, grad_router, slab, grad_ffn, weights, tokens, grad_hidden,
    gain, mixed,
):
    kind = jnp.bfloat16
    tall = normed.shape[1]
    local = context.shape[1]
    piece = (BLOCK_ROWS, LANES)
    part = (BLOCK_ROWS // 2, LANES)
    sem = pltpu.SemaphoreType.DMA
    floats = functools.partial(jax.ShapeDtypeStruct, dtype=jnp.float32)
    full, grad_input = pl.pallas_call(
        weights_kernel,
        out_shape=(
            jax.ShapeDtypeStruct((2, 2, SIDE, SIDE) + piece, kind),
            floats(tokens.shape),
        ),
        in_specs=[VMEM] * 13,
        out_specs=(VMEM,) * 2,
        scratch_shapes=[
            pltpu.VMEM(tokens.shape, kind),
            pltpu.VMEM(tokens.shape, kind),
            pltpu.VMEM((2, 2, SIDE, SIDE) + piece, kind),
            pltpu.VMEM((2, SIDE, SIDE) + piece, kind),
            pltpu.VMEM((2, SIDE, SIDE) + piece, kind),
            pltpu.VMEM((2, 2, SIDE) + part, kind),
            pltpu.VMEM((2, 2, SIDE) + piece, kind),
            pltpu.VMEM((2, SIDE) + piece, kind),
            pltpu.VMEM((2, SIDE - 1) + piece, kind),
            pltpu.VMEM((2,) + part, kind),
            sem((64,)), sem((2, SIDE)),
            sem((2, 2)), sem((2, 2, 2)), sem((2, SIDE - 1)),
            sem((2,)), sem((2,)), sem((2, SIDE)), sem((2, SIDE, 2)), sem((2, SIDE)), sem,
        ],
        compiler_params=pltpu.CompilerParams(
            collective_id=3, has_side_effects=True, vmem_limit_bytes=60 * 1024 * 1024
        ),
        name="weight_totals",
    )(
        normed, grads, context, attended, grad_router, slab, grad_ffn, *weights, tokens,
        grad_hidden, gain,
    )
    return pl.pallas_call(
        unpack_kernel,
        out_shape=(
            floats((tall, local)),
            floats((tall, local)),
            floats((tall, local)),
            floats((local, tall)),
            floats(grad_router.shape[::-1]),
            floats((local // HEAD, slab.shape[0])),
            floats((UNIT, LANES)),
            floats(tokens.shape),
            jax.ShapeDtypeStruct(tokens.shape, kind),
        ),
        in_specs=[VMEM] * 3,
        out_specs=(VMEM,) * 9,
        compiler_params=pltpu.CompilerParams(vmem_limit_bytes=60 * 1024 * 1024),
        name="unpack",
    )(full, grad_input, mixed)


QUARTERS = 4
STRIDE = 11


def gelu_pair(values):
    root = 0.7978845608028654
    cubic = 0.044715
    square = values * values
    bend = jnp.tanh(root * values * (1.0 + cubic * square))
    active = 0.5 * values * (1.0 + bend)
    slope = 0.5 * (1.0 + bend) + 0.5 * values * (1.0 - bend * bend) * root * (
        1.0 + 3.0 * cubic * square
    )
    return active, slope


def middle_kernel(
    both_ref, tokens_ref, cotangent_ref, proj_ref, gain_ref, router_ref, route_ref, slot_ref,
    w_in_hbm, w_out_hbm,
    mixed_ref, hidden_ref, attended_ref, context_ref, grad_both_ref, grad_router_ref,
    grad_gain_ref, rows_in_ref, rows_grad_ref, activ_ref, grad_pre_ref,
    w_in, w_out, swapped, share, share_other, order, order_t, gather_t, send_one, recv_one,
    send_two, recv_two, sums, sums_other, given,
    load_sem, send_sem, one_send, one_recv, two_send, two_recv, swap_recv, share_recv,
    sums_recv, back_recv,
):
    place = Place()
    me = place.me
    count = 2 * 2 * SIDE * SIDE
    loads = [
        pltpu.make_async_copy(w_in_hbm, w_in, load_sem.at[0]),
        pltpu.make_async_copy(w_out_hbm, w_out, load_sem.at[1]),
    ]
    for load in loads:
        load.start()
    barrier = pltpu.get_barrier_semaphore()

    @pl.loop(1, count)
    def _(step):
        pl.semaphore_signal(
            barrier,
            inc=1,
            device_id={"ctx": lax.rem(me + step, count)},
            device_id_type=pl.DeviceIdType.MESH,
        )

    pl.semaphore_signal(
        barrier,
        inc=1,
        device_id={"mp": 1 - lax.axis_index("mp")},
        device_id_type=pl.DeviceIdType.MESH,
    )
    tok_rows = tokens_ref.shape[0]
    spots = tok_rows * QUARTERS
    cells = 16 * count
    route = route_ref[...].astype(jnp.float32)
    spot = route * 16.0 + slot_ref[...].astype(jnp.float32)
    square = (tok_rows, tok_rows)
    diagonal = lax.broadcasted_iota(jnp.int32, square, 0) == lax.broadcasted_iota(
        jnp.int32, square, 1
    )

    def column(line):
        return jnp.sum(jnp.where(diagonal, line, 0.0), axis=1, keepdims=True).astype(jnp.int32)

    spot_row = jnp.concatenate(
        [spot.astype(jnp.int32) + 4 * n for n in range(QUARTERS)], axis=1
    )
    spot_col = column(spot)
    gather = jnp.where(
        lax.broadcasted_iota(jnp.int32, (cells, spots), 0) == spot_row, 1.0, 0.0
    ).astype(jnp.bfloat16)
    pl.semaphore_wait(barrier, count)
    sends = Sends(place, send_sem)
    first = place.y == 0

    mine = pl.ds(pl.multiple_of(place.y * tok_rows, tok_rows), tok_rows)
    theirs = pl.ds(pl.multiple_of((1 - place.y) * tok_rows, tok_rows), tok_rows)
    sends.go(place.at(dy=1), both_ref.at[theirs], swapped, swap_recv)
    kept = both_ref[mine]
    sends.landed(swapped, swap_recv)
    received = swapped[...]
    context = jnp.concatenate(
        [jnp.where(first, kept, received), jnp.where(first, received, kept)], axis=1
    )
    context_ref[...] = context
    share[...] = contract(context, proj_ref[...], 1, 0).astype(share.dtype)
    sends.across(share, share_other, share_recv)
    sends.landed(share_other, share_recv)
    hidden = wide(tokens_ref[...]) + (wide(share[...]) + wide(share_other[...]))
    scale = lax.rsqrt(jnp.mean(hidden * hidden, axis=1, keepdims=True) + EPSILON)
    normed = hidden * scale * gain_ref[...][None]
    logits = lax.dot_general(
        normed, router_ref[...], (((1,), (1,)), ((), ())), precision=PRECISE,
        preferred_element_type=jnp.float32,
    )
    shifted = jnp.exp(logits - jnp.max(logits, axis=1, keepdims=True))
    probs = shifted / jnp.sum(shifted, axis=1, keepdims=True)
    chosen = jnp.where(
        column(route) == lax.broadcasted_iota(jnp.int32, probs.shape, 1), 1.0, 0.0
    )
    gate = jnp.sum(probs * chosen, axis=1, keepdims=True)
    grad_y = wide(cotangent_ref[...])
    width = 2 * tokens_ref.shape[1] // QUARTERS
    payload = [normed[:, :width], normed[:, width:]]
    payload += [gate * grad_y[:, :width], gate * grad_y[:, width:]]
    payload = jnp.concatenate(payload, axis=0).astype(jnp.bfloat16)
    send_one[...] = (
        contract(gather, payload, 1, 0).astype(send_one.dtype).reshape(send_one.shape)
    )

    def exchange(src, dst, send, recv):
        @pl.loop(1, count)
        def _(step):
            target = lax.rem(me + step * STRIDE, count)
            sender(target, src.at[target], dst.at[me], send, recv).start()

        dst[me] = src[me]

    def arrive(dst, recv):
        others = dst.at[pl.ds(0, count - 1)]
        sends.landed(others, recv)

    exchange(send_one, recv_one, one_send, one_recv)
    rows = cells // QUARTERS

    def cell_of(index):
        row = index & (rows - 1)
        return (row >> 2) * 16 + (index >> 8) * 4 + (row & 3)

    down = lax.broadcasted_iota(jnp.int32, (cells, cells), 0)
    right = lax.broadcasted_iota(jnp.int32, (cells, cells), 1)
    order[...] = jnp.where(cell_of(down) == right, 1.0, 0.0).astype(order.dtype)
    order_t[...] = jnp.where(down == cell_of(right), 1.0, 0.0).astype(order_t.dtype)
    cell = lax.broadcasted_iota(jnp.int32, (tok_rows, cells), 1)
    for n in range(QUARTERS):
        gather_t[n * tok_rows : (n + 1) * tok_rows] = jnp.where(
            spot_col + 4 * n == cell, 1.0, 0.0
        ).astype(gather_t.dtype)
    for load in loads:
        load.wait()
    arrive(recv_one, one_recv)

    got = contract(order[...], recv_one[...].reshape(cells, width), 1, 0).astype(jnp.bfloat16)
    rows_in_ref[...] = jnp.concatenate([got[:rows], got[rows : 2 * rows]], axis=1)
    rows_grad_ref[...] = jnp.concatenate([got[2 * rows : 3 * rows], got[3 * rows :]], axis=1)
    hidden_units = w_in.shape[1]
    chunk = hidden_units // 3
    out = jnp.zeros(rows_in_ref.shape, jnp.float32)
    back = jnp.zeros(rows_in_ref.shape, jnp.float32)
    for start in range(0, hidden_units, chunk):
        units = slice(start, start + chunk)
        active, slope = gelu_pair(contract(rows_in_ref[...], w_in[:, units], 1, 0))
        active = active.astype(jnp.bfloat16)
        activ_ref[:, units] = active
        out = out + contract(active, w_out[units], 1, 0)
        grad_pre = (contract(rows_grad_ref[...], w_out[units], 1, 1) * slope).astype(jnp.bfloat16)
        grad_pre_ref[:, units] = grad_pre
        back = back + contract(grad_pre, w_in[:, units], 1, 1)
    whole = [out[:, :width], out[:, width:], back[:, :width], back[:, width:]]
    whole = jnp.concatenate(whole, axis=0).astype(jnp.bfloat16)
    send_two[...] = (
        contract(order_t[...], whole, 1, 0).astype(send_two.dtype).reshape(send_two.shape)
    )
    exchange(send_two, recv_two, two_send, two_recv)
    arrive(recv_two, two_recv)
    sums[...] = contract(gather_t[...], recv_two[...].reshape(cells, width), 1, 0).astype(
        sums.dtype
    )
    pairs = [pl.ds(n * 2 * tok_rows, 2 * tok_rows) for n in range(2)]
    for n, pair in enumerate(pairs):
        sends.across(sums.at[pair], sums_other.at[pair], sums_recv.at[n])

    def summed(n):
        sends.landed(sums_other.at[pairs[n]], sums_recv.at[n])
        total = wide(sums[pairs[n]]) + wide(sums_other[pairs[n]])
        total = jnp.concatenate([total[:tok_rows], total[tok_rows:]], axis=1)
        return total.astype(jnp.bfloat16).astype(jnp.float32)

    expert_rows = summed(0)

    mixed_ref[...] = (hidden + gate * expert_rows).astype(mixed_ref.dtype)
    grad_gate = jnp.sum(grad_y * expert_rows, axis=1, keepdims=True)
    grad_logits = grad_gate * gate * (chosen - probs)
    grad_router_ref[...] = lax.dot_general(
        normed, grad_logits, (((0,), (0,)), ((), ())), precision=PRECISE,
        preferred_element_type=jnp.float32,
    )
    grad_normed = lax.dot_general(
        grad_logits, router_ref[...], (((1,), (0,)), ((), ())), precision=PRECISE,
        preferred_element_type=jnp.float32,
    )
    grad_normed = summed(1) + grad_normed
    scaled = gain_ref[...][None] * grad_normed
    grad_gain_ref[...] = jnp.sum(grad_normed * hidden * scale, axis=0, keepdims=True)
    grad_hidden = (
        grad_y
        + scale * scaled
        - hidden * scale**3 * jnp.mean(scaled * hidden, axis=1, keepdims=True)
    )
    hidden_ref[...] = grad_hidden
    attended = grad_hidden.astype(jnp.bfloat16)
    attended_ref[...] = attended
    grad_context = contract(attended, proj_ref[...], 1, 1).astype(jnp.bfloat16)
    half = grad_context.shape[1] // 2
    left, right_part = grad_context[:, :half], grad_context[:, half:]
    given[...] = jnp.where(first, right_part, left)
    grad_both_ref[mine] = jnp.where(first, left, right_part)
    sends.go(place.at(dy=1), given, grad_both_ref.at[mine], back_recv)
    sends.landed(grad_both_ref.at[theirs], back_recv)
    sends.finish()

    for src, send in ((send_one, one_send), (send_two, two_send)):
        others = src.at[pl.ds(0, count - 1)]
        sender(me, others, others, send, send).wait_send()


def middle(
    both, tokens, cotangent, w_proj, gain, router, w_in, w_out, route, slot
):
    kind = jnp.bfloat16
    tok_rows, wide_row = tokens.shape
    count = router.shape[0]
    rows = 4 * count
    hidden = w_in.shape[1]
    width = 2 * wide_row // QUARTERS
    spots = QUARTERS * tok_rows
    shape = jax.ShapeDtypeStruct
    sem = pltpu.SemaphoreType.DMA
    buffer = pltpu.VMEM((count, 16, width), kind)
    return pl.pallas_call(
        middle_kernel,
        out_shape=(
            shape(tokens.shape, kind),
            shape(tokens.shape, jnp.float32),
            shape(tokens.shape, kind),
            shape((tok_rows, 2 * both.shape[1]), kind),
            shape(both.shape, kind),
            shape(router.shape[::-1], jnp.float32),
            shape((1, wide_row), jnp.float32),
            shape((rows, wide_row), kind),
            shape((rows, wide_row), kind),
            shape((rows, hidden), kind),
            shape((rows, hidden), kind),
        ),
        in_specs=[VMEM] * 8 + [ANYWHERE] * 2,
        out_specs=(VMEM,) * 11,
        scratch_shapes=[
            pltpu.VMEM(w_in.shape, kind),
            pltpu.VMEM(w_out.shape, kind),
            pltpu.VMEM((tok_rows, both.shape[1]), kind),
            pltpu.VMEM(tokens.shape, kind),
            pltpu.VMEM(tokens.shape, kind),
            pltpu.VMEM((16 * count, 16 * count), kind),
            pltpu.VMEM((16 * count, 16 * count), kind),
            pltpu.VMEM((spots, 16 * count), kind),
            buffer, buffer, buffer, buffer,
            pltpu.VMEM((spots, width), kind),
            pltpu.VMEM((spots, width), kind),
            pltpu.VMEM((tok_rows, both.shape[1]), kind),
            sem((2,)), sem((5,)), sem, sem, sem, sem, sem, sem, sem((2,)), sem,
        ],
        compiler_params=pltpu.CompilerParams(
            collective_id=4, has_side_effects=True, vmem_limit_bytes=60 * 1024 * 1024
        ),
        name="middle",
    )(
        both, tokens, cotangent, w_proj, gain, router, route[None], slot[None], w_in, w_out,
    )


def shards(
    tokens,
    attn_gain,
    w_query,
    w_key,
    w_value,
    w_proj,
    rel_table,
    rel_bucket,
    ffn_gain,
    router,
    w_in,
    w_out,
    expert_route,
    expert_slot,
    cotangent,
):
    me = lax.axis_index("ctx")
    side = 2 * SIDE * SIDE
    place = jnp.stack([me % side, me // side]).astype(jnp.int32)
    normed, rows, held = gather_plane(tokens, attn_gain, w_query, w_key, w_value)

    buckets = jnp.pad(rel_bucket, (0, 1), constant_values=31).reshape(BLOCK, BLOCK)
    both, turned, lse, flipped, table, uneven = attend(place, rel_table.T, buckets, held, rows)
    (
        mixed, grad_hidden1, grad_attended, context, grad_both, grad_router, grad_ffn_gain,
        rows_in, rows_grad, activ, grad_pre,
    ) = middle(
        both, tokens, cotangent, w_proj, ffn_gain, router.T, w_in[0], w_out[0], expert_route,
        expert_slot,
    )
    grad_parts, grad_rows, slab, grad_expert_in, grad_expert_out = attend_back(
        place, uneven, table, held, rows, grad_both, turned, lse, flipped, rows_in, rows_grad,
        activ, grad_pre, rel_table.shape[0],
    )
    grads = scatter_plane(grad_parts, grad_rows)
    (
        grad_query, grad_key, grad_value, grad_proj, grad_router, grad_table, gains, grad_input,
        mixed,
    ) = weight_totals(
        normed, grads, context, grad_attended, grad_router, slab, grad_ffn_gain,
        (w_query, w_key, w_value), tokens, grad_hidden1, attn_gain, mixed,
    )
    lines = tokens.shape[1] // LANES
    return (
        mixed,
        grad_input,
        gains[:lines].reshape(-1),
        grad_query,
        grad_key,
        grad_value,
        grad_proj,
        grad_table.T,
        gains[lines : 2 * lines].reshape(-1),
        grad_router.T,
        grad_expert_in[None],
        grad_expert_out[None],
    )


def solution(mesh):
    return jax.shard_map(
        shards,
        mesh=mesh,
        in_specs=(
            P("ctx", None),
            P(),
            P(None, "mp"),
            P(None, "mp"),
            P(None, "mp"),
            P("mp", None),
            P(None, "mp"),
            P(),
            P(),
            P(),
            P("ctx", None, "mp"),
            P("ctx", "mp", None),
            P("ctx"),
            P("ctx"),
            P("ctx", None),
        ),
        out_specs=(
            P("ctx", None),
            P("ctx", None),
            P(),
            P(None, "mp"),
            P(None, "mp"),
            P(None, "mp"),
            P("mp", None),
            P(None, "mp"),
            P(),
            P(),
            P("ctx", None, "mp"),
            P("ctx", "mp", None),
        ),
        check_vma=False,
    )
```
